32 devices in a mesh: lat: 4 (over y, x), lon: 8 (over z, core).
Axes of the slice: x: 2, y: 2, z: 4, core: 2. Of those that a mesh axis runs over, the one named last changes fastest.
Arguments:
- coarse: bfloat16 [73, 16, 64], P(None, 'lat', 'lon'), may hold values from -6 to 6
- row_src: int32 [128], P('lat'), may hold values from 0 to 14, as said below
- row_frac: float32 [128], P('lat'), may hold values from 0 to 1
- col_src: int32 [1024], P('lon'), may hold values from 0 to 63, as said below
- col_frac: float32 [1024], P('lon'), may hold values from 0 to 1
- embed_weight: bfloat16 [73, 128], replicated, may hold values from -0.75 to 0.75
- conv1_weight: bfloat16 [3, 3, 128, 128], replicated, may hold values from -0.1875 to 0.1875
- conv2_weight: bfloat16 [3, 3, 128, 128], replicated, may hold values from -0.1875 to 0.1875
- cotangent: bfloat16 [128, 1024, 128], P('lat', 'lon'), may hold values from -6 to 6
Outputs:
- features: bfloat16 [128, 1024, 128], P('lat', 'lon')
- grad_embed: float32 [73, 128], replicated
- grad_conv1: float32 [3, 3, 128, 128], replicated
- grad_conv2: float32 [3, 3, 128, 128], replicated
The draws below stay inside these ranges and needn't reach their ends.
Inputs may be any that keep to these rules, and one draw needn't show every extreme that they name: row_src[r] differs from (r * 16) // 128 by at most 1; both bounds are reached. col_src[c] differs cyclically (mod 64) from (c * 64) // 1024 by at most 1; both bounds are reached.
All inputs are finite; a program needn't handle non-finite values.
Results may differ from the reference program's by a relative error of at most 0.0062.
Values may be sent and summed in bfloat16 or wider, within the bound.
No kernel may reach another device: no remote copies, remote signals or barrier semaphores. Data moves between devices by JAX's collectives and lax.ppermute only.
A program may use at most 128 MiB of HBM per device.

```python
import math
import jax
import jax.numpy as jnp
from jax import lax

CH_IN = 73
HID = 128
ROWS = 32
COLS = 128
CR_DEV = 4
CC_DEV = 8
FROWS = 128
FCOLS = 1024
CROWS = 16
CCOLS = 64


def draw_row_src(key, part):
    key = jax.random.fold_in(key, 11)
    line = jnp.arange(FROWS, dtype=jnp.int32)
    base = line * CROWS // FROWS
    offset = jax.random.randint(key, (FROWS,), -1, 2, dtype=jnp.int32)
    picked = jnp.clip(base + offset, 0, CROWS - 2)
    picked = picked.at[0].set(0)
    picked = picked.at[FROWS - 1].set(CROWS - 2)
    tiles = jnp.arange(1, FROWS // ROWS, dtype=jnp.int32)
    edge_value = tiles * CR_DEV - 1
    picked = picked.at[tiles * ROWS].set(edge_value)
    picked = picked.at[tiles * ROWS + 1].set(edge_value)
    return picked.astype(jnp.int32)


def draw_col_src(key, part):
    key = jax.random.fold_in(key, 23)
    line = jnp.arange(FCOLS, dtype=jnp.int32)
    base = line * CCOLS // FCOLS
    offset = jax.random.randint(key, (FCOLS,), -1, 2, dtype=jnp.int32)
    picked = jnp.mod(base + offset, CCOLS)
    picked = picked.at[2].set(0)
    picked = picked.at[FCOLS - 1].set(CCOLS - 1)
    tiles = jnp.arange(0, FCOLS // COLS, dtype=jnp.int32)
    edge_value = jnp.mod(tiles * CC_DEV - 1, CCOLS)
    picked = picked.at[tiles * COLS].set(edge_value)
    picked = picked.at[tiles * COLS + 1].set(edge_value)
    return picked.astype(jnp.int32)


def levels(rng, dims, split, low, largest):
    loudness = 1.0
    for position, blocks in split:
        heights = jax.random.uniform(jax.random.fold_in(jax.random.fold_in(rng, 6), position), (blocks,), jnp.float32, low / len(split), largest / len(split))
        loudness = loudness * jnp.repeat(jnp.exp(heights), dims[position] // blocks).reshape((-1,) + (1,) * (len(dims) - 1 - position))
    return loudness


def scatter_about(own_key, extent, spread, bound, shards=(), kind=jnp.bfloat16):
    drawn = spread * jax.random.normal(own_key, extent, jnp.float32)
    if shards:
        drawn = drawn * levels(own_key, extent, shards, -0.22, 0.18)
    return jnp.clip(drawn, -bound, bound).astype(kind)


def setup_inputs(seed: int = 0) -> dict:
    seeds = jax.random.split(jax.random.key(seed), 10)
    coarse = scatter_about(seeds[0], (CH_IN, CROWS, CCOLS), 1.0, 6.0, ((1, 4), (2, 8)))
    row_src = draw_row_src(jax.random.fold_in(seeds[9], 71), 0)
    row_frac = jnp.clip(1.0 * jax.random.uniform(seeds[2], (FROWS,), jnp.float32) ** levels(seeds[2], (FROWS,), ((0, 4),), -0.2, 0.2), 0.0, 1.0)
    col_src = draw_col_src(jax.random.fold_in(seeds[9], 71), 0)
    col_frac = jnp.clip(1.0 * jax.random.uniform(seeds[4], (FCOLS,), jnp.float32) ** levels(seeds[4], (FCOLS,), ((0, 8),), -0.2, 0.2), 0.0, 1.0)
    embed_weight = scatter_about(seeds[5], (CH_IN, HID), CH_IN ** -0.5, 0.75)
    conv1_weight = scatter_about(seeds[6], (3, 3, HID, HID), (9 * HID) ** -0.5, 0.1875)
    conv2_weight = scatter_about(seeds[7], (3, 3, HID, HID), (9 * HID) ** -0.5, 0.1875)
    cotangent = scatter_about(seeds[8], (FROWS, FCOLS, HID), 1.0, 6.0, ((0, 4), (1, 8)))
    return {"coarse": coarse, "row_src": row_src, "row_frac": row_frac, "col_src": col_src, "col_frac": col_frac, "embed_weight": embed_weight, "conv1_weight": conv1_weight, "conv2_weight": conv2_weight, "cotangent": cotangent}


def pad_grid(field):
    wrapped = jnp.concatenate([field[:, -1:], field, field[:, :1]], axis=1)
    return jnp.pad(wrapped, ((1, 1), (0, 0), (0, 0)))

def convolve(padded, weight, span_rows, span_cols):
    channels = weight.shape[2]
    total = jnp.zeros((span_rows * span_cols, weight.shape[3]), jnp.float32)
    for tap_row in range(3):
        for tap_col in range(3):
            window = padded[tap_row:tap_row + span_rows, tap_col:tap_col + span_cols].reshape(-1, channels)
            total = total + jnp.dot(window, weight[tap_row, tap_col], preferred_element_type=jnp.float32)
    return total.reshape(span_rows, span_cols, -1)

def convolve_back(padded, weight, span_rows, span_cols):
    channels = weight.shape[3]
    total = jnp.zeros((span_rows * span_cols, weight.shape[2]), jnp.float32)
    for tap_row in range(3):
        for tap_col in range(3):
            window = padded[2 - tap_row:2 - tap_row + span_rows, 2 - tap_col:2 - tap_col + span_cols].reshape(-1, channels)
            total = total + jnp.dot(window, weight[tap_row, tap_col].T, preferred_element_type=jnp.float32)
    return total.reshape(span_rows, span_cols, -1)

def weight_grads(padded, delta, span_rows, span_cols):
    channels = padded.shape[2]
    flat_delta = delta.reshape(-1, delta.shape[2])
    blocks = []
    for tap_row in range(3):
        line = []
        for tap_col in range(3):
            window = padded[tap_row:tap_row + span_rows, tap_col:tap_col + span_cols].reshape(-1, channels)
            line.append(lax.dot_general(window, flat_delta, (((0,), (0,)), ((), ())), preferred_element_type=jnp.float32))
        blocks.append(jnp.stack(line))
    return jnp.stack(blocks)

def reference(coarse, row_src, row_frac, col_src, col_frac, embed_weight, conv1_weight, conv2_weight, cotangent):
    span_rows = cotangent.shape[0]
    span_cols = cotangent.shape[1]
    coarse_f = coarse.astype(jnp.float32)
    row_mixed = (1.0 - row_frac)[None, :, None] * coarse_f[:, row_src, :] + row_frac[None, :, None] * coarse_f[:, row_src + 1, :]
    next_col = jnp.mod(col_src + 1, coarse.shape[2]).astype(jnp.int32)
    fine_input = ((1.0 - col_frac)[None, None, :] * row_mixed[:, :, col_src] + col_frac[None, None, :] * row_mixed[:, :, next_col]).astype(jnp.bfloat16)
    lifted = jnp.einsum('krc,kh->rch', fine_input.astype(jnp.float32), embed_weight.astype(jnp.float32)).astype(jnp.bfloat16)
    lifted_pad = pad_grid(lifted)
    pre_first = convolve(lifted_pad, conv1_weight, span_rows, span_cols)
    hidden = jax.nn.silu(pre_first).astype(jnp.bfloat16)
    hidden_pad = pad_grid(hidden)
    features = (lifted.astype(jnp.float32) + convolve(hidden_pad, conv2_weight, span_rows, span_cols)).astype(jnp.bfloat16)
    norm_scale = 1.0 / math.sqrt(span_rows * span_cols)
    grad_conv2 = weight_grads(hidden_pad, cotangent, span_rows, span_cols) * norm_scale
    cot_pad = pad_grid(cotangent)
    back_hidden = convolve_back(cot_pad, conv2_weight, span_rows, span_cols)
    sig = jax.nn.sigmoid(pre_first)
    delta = (back_hidden * sig * (1.0 + pre_first * (1.0 - sig))).astype(jnp.bfloat16)
    grad_conv1 = weight_grads(lifted_pad, delta, span_rows, span_cols) * norm_scale
    back_lifted = (cotangent.astype(jnp.float32) + convolve_back(pad_grid(delta), conv1_weight, span_rows, span_cols)).astype(jnp.bfloat16)
    grad_embed = jnp.einsum('krc,rch->kh', fine_input.astype(jnp.float32), back_lifted.astype(jnp.float32)) * norm_scale
    return (features, grad_embed, grad_conv1, grad_conv2)
```

```python
import math

import jax
import jax.numpy as jnp
from jax import lax
from jax.experimental import pallas as pl
from jax.experimental.pallas import tpu as pltpu
from jax.sharding import PartitionSpec as P

F32 = jnp.float32
BF16 = jnp.bfloat16
LANES = 128
ROW_HALO = 3
COL_HALO = 4
SPAN = 16
GRAD_ROWS = 80
VMEM_BYTES = 36 * 1024 * 1024


def split_two(value):
    high = value.astype(BF16)
    return high, (value - high.astype(F32)).astype(BF16)


def prepare_kernel(
    cot_hbm, w2_hbm, w1_hbm, embed_hbm,
    shift_ref, back_ref, fore_ref, turned_ref, first_ref, cot_ref, w1_ref, padded_ref,
    w2_ref, embed_ref, line_ref, sems
):
    rows, cols, _ = cot_ref.shape
    wide = cols + 16
    pairs = rows // 2 + 1
    chunks = sems.shape[0] - 3
    share = rows // chunks
    weight_copy = pltpu.make_async_copy(w2_hbm, w2_ref, sems.at[chunks])
    weight_copy.start()
    copies = []
    for n in range(chunks):
        part = pl.ds(n * share, share)
        copies.append(pltpu.make_async_copy(cot_hbm.at[part], cot_ref.at[part], sems.at[n]))
        copies[-1].start()
    other_copy = pltpu.make_async_copy(w1_hbm, w1_ref, sems.at[chunks + 1])
    other_copy.start()
    embed_copy = pltpu.make_async_copy(embed_hbm, embed_ref, sems.at[chunks + 2])
    embed_copy.start()
    line_ref[...] = jnp.zeros_like(line_ref)
    back_ref[...] = jnp.zeros_like(back_ref)
    fore_ref[...] = jnp.zeros_like(fore_ref)
    blank = jnp.zeros((wide, LANES), BF16)
    for b in range(3):
        for parity in range(2):
            shift_ref[b, parity, 0:wide] = blank
            shift_ref[b, parity, pairs * wide : (pairs + 1) * wide] = blank
    weight_copy.wait()
    for a in range(3):
        for b in range(3):
            straight = w2_ref[a * 3 + b]
            turned = straight.astype(F32).T.astype(BF16)
            for q in range(2):
                column = slice(q * LANES, (q + 1) * LANES)
                at = (b * 4 + 2 + q - a) * LANES
                back_ref[at : at + LANES, column] = turned
                at = (b * 4 + a + q) * LANES
                fore_ref[at : at + LANES, column] = straight
    for r in range(rows):
        slot = r % 4
        if r % share == 0:
            copies[r // share].wait()
        line = cot_ref[r].astype(F32)
        line_ref[slot, 8 : 8 + cols] = line
        start = (r // 2 + 1) * wide
        for b in range(3):
            shift_ref[b, r % 2, start : start + wide] = line_ref[slot, 8 - b : 8 - b + wide].astype(BF16)
        turned_ref[(r % 2) * LANES : (r % 2 + 1) * LANES, (r // 2) * cols : (r // 2 + 1) * cols] = line.T.astype(BF16)
    embed_copy.wait()
    padded_ref[...] = padded_embed(embed_ref, line_ref)
    other_copy.wait()
    for tap in range(9):
        first_ref[tap * LANES : (tap + 1) * LANES] = w1_ref[tap].astype(F32).T.astype(BF16)


def edge_line(block, at):
    index = block[at : at + 1]
    return index, block[at + 1 : at + 2] + block[at + 2 : at + 3] + block[at + 3 : at + 4]


def row_spots(place_ref, rsrc_ref, rfrac_ref, before_ref, after_ref, rows, band_rows, lat_count):
    lat = place_ref[0]
    line_of = lax.broadcasted_iota(jnp.int32, (1, LANES), 1)

    def one_of(value, at):
        return jnp.sum(jnp.where(line_of == at, value, 0.0))

    before_line = edge_line(before_ref[ROW_HALO].astype(F32), 0)
    after_line = edge_line(after_ref[ROW_HALO].astype(F32), 0)
    spots = []
    for q in range(rows + 4):
        line_at = lat * rows + q - 2
        inside = jnp.logical_and(line_at >= 0, line_at < lat_count * rows)
        if q < 2:
            index, f = (one_of(v, rows - 2 + q) for v in before_line)
            index = index.astype(jnp.int32)
        elif q < rows + 2:
            index, f = rsrc_ref[0, q - 2], rfrac_ref[0, q - 2]
        else:
            index, f = (one_of(v, q - rows - 2) for v in after_line)
            index = index.astype(jnp.int32)
        j0 = jnp.clip(index - lat * band_rows + ROW_HALO, 0, band_rows + 2 * ROW_HALO - 2)
        spots.append((j0, jnp.where(inside, 1.0 - f, 0.0), jnp.where(inside, f, 0.0)))
    return spots


def blend_rows(cells_ref, spots):
    return jnp.concatenate(
        [w0 * cells_ref[j0] + w1 * cells_ref[j0 + 1] for j0, w0, w1 in spots], axis=0
    )


def lift_rows(mixed, embed):
    pair = jnp.concatenate(list(split_two(mixed)), axis=1)
    return jnp.dot(pair, jnp.concatenate([embed, embed], axis=0), preferred_element_type=F32)


def turned_rows(mixed, width):
    fill = jnp.zeros((width - mixed.shape[0], LANES), F32)
    turned = jnp.concatenate([mixed, fill], axis=0).T[:GRAD_ROWS]
    step = 2 * COL_HALO
    lines = [turned] + [pltpu.roll(turned, width - a * step, 1) for a in (1, 2)]
    return split_two(jnp.concatenate(lines, axis=0))


def tap_rows(lifted, w1_ref, cells):
    count = lifted.shape[0] - 2 * cells
    pairs = [split_two(lifted[a * cells : a * cells + count]) for a in range(3)]
    left = jnp.concatenate([p[0] for p in pairs] + [p[1] for p in pairs], axis=1)
    lines = [jnp.concatenate([w1_ref[a * 3 + b] for b in range(3)], axis=1) for a in range(3)]
    return jnp.dot(left, jnp.concatenate(lines + lines, axis=0), preferred_element_type=F32)


def blend_cols(src, frac, lon, band_cols, coarse_cols):
    shape = (SPAN, src.shape[1])
    local = jnp.broadcast_to(src, shape) - lon * band_cols
    frac = jnp.broadcast_to(frac, shape)
    local = jnp.where(local < -COL_HALO, local + coarse_cols, local)
    local = jnp.where(local >= band_cols + COL_HALO, local - coarse_cols, local)
    line = lax.broadcasted_iota(jnp.int32, shape, 0)

    def spot(at):
        east = jnp.where(at >= band_cols, at + COL_HALO, at)
        return jnp.where(at < 0, at + band_cols + COL_HALO, east)

    return jnp.where(line == spot(local), 1.0 - frac, 0.0) + jnp.where(
        line == spot(local + 1), frac, 0.0
    )


def back_kernel(
    place_ref,
    rsrc_ref,
    rfrac_ref,
    shift_ref,
    weight_ref,
    before_ref,
    own_ref,
    after_ref,
    csrc_ref,
    cfrac_ref,
    embed_ref,
    w1_ref,
    cot_ref,
    bh_ref,
    rows_ref,
    lifted_ref,
    tap_ref,
    cot_col_ref,
    cells_ref,
    *,
    lat_count,
    coarse_cols,
):
    rows, cols, _ = cot_ref.shape
    wide = bh_ref.shape[1]
    pairs = bh_ref.shape[0] // 2
    band_rows, band_cols = own_ref.shape[0] - 1, own_ref.shape[1]
    step = 6
    for first in range(0, pairs, step):
        count = min(step, pairs - first)
        blocks = []
        for b in range(3):
            for i in range(4):
                start = (first + i // 2) * wide
                blocks.append(shift_ref[b, i % 2, start : start + count * wide])
        out = jnp.dot(jnp.concatenate(blocks, axis=1), weight_ref[...], preferred_element_type=F32)
        for m in range(count):
            for q in range(2):
                bh_ref[2 * (first + m) + q] = out[m * wide : (m + 1) * wide, q * LANES : (q + 1) * LANES]

    for j in range(cells_ref.shape[0]):
        if j < ROW_HALO:
            middle = before_ref[j]
        elif j < ROW_HALO + band_rows:
            middle = own_ref[j - ROW_HALO]
        else:
            middle = after_ref[j - ROW_HALO - band_rows]
        cells_ref[j] = middle.astype(F32)
    spots = row_spots(place_ref, rsrc_ref, rfrac_ref, before_ref, after_ref, rows, band_rows, lat_count)
    mixed = blend_rows(cells_ref, spots)
    rows_ref[0], rows_ref[1] = turned_rows(mixed, rows_ref.shape[2])
    lifted = lift_rows(mixed, embed_ref[...])
    lifted_ref[...] = lifted
    tap_ref[...] = tap_rows(lifted, w1_ref, band_cols)

    blend = blend_cols(csrc_ref[...], cfrac_ref[...], place_ref[1], band_cols, coarse_cols)
    own_t = jnp.concatenate(list(split_two(blend)), axis=0)
    every = jnp.concatenate([cot_ref[r] for r in range(rows)], axis=1)
    back = jnp.dot(own_t, every, preferred_element_type=F32)
    back = back[:SPAN] + back[SPAN:]
    for r in range(rows):
        cot_col_ref[r] = back[:, r * LANES : (r + 1) * LANES]


def pack_kernel(cells_hbm, rsrc_hbm, rfrac_hbm, csrc_hbm, cfrac_hbm, out_ref, *space):
    sources = (cells_hbm, rsrc_hbm, rfrac_hbm, csrc_hbm, cfrac_hbm)
    *lines, cells_ref, sems = space
    targets = (cells_ref, *lines)
    copies = [
        pltpu.make_async_copy(source, target, sems.at[n])
        for n, (source, target) in enumerate(zip(sources, targets))
    ]
    for copy in copies:
        copy.start()
    cells_ref, rsrc_ref, rfrac_ref, csrc_ref, cfrac_ref = targets
    depth, span, fields = cells_ref.shape
    out_ref[...] = jnp.zeros_like(out_ref)
    for copy in copies:
        copy.wait()
    for j in range(depth):
        out_ref[j, :, :fields] = cells_ref[j].astype(F32)
    at = 0
    for index_ref, fraction_ref in ((rsrc_ref, rfrac_ref), (csrc_ref, cfrac_ref)):
        width = index_ref.shape[1]
        fraction = fraction_ref[...]
        one = fraction.astype(BF16).astype(F32)
        two = (fraction - one).astype(BF16).astype(F32)
        for value in (index_ref[...].astype(F32), one, two, fraction - one - two):
            out_ref[depth, at : at + 1, :width] = value
            at += 1


def main_kernel(
    place_ref,
    rsrc_ref,
    rfrac_ref,
    before_ref,
    after_ref,
    west_ref,
    east_ref,
    csrc_ref,
    cfrac_ref,
    embed_ref,
    w1_ref,
    turned_ref,
    bh_ref,
    rows_ref,
    lifted_ref,
    tap_ref,
    cot_col_ref,
    hid_ref,
    lift_ref,
    msg_ref,
    cells_ref,
    side_tap_ref,
    line_ref,
    right_ref,
    lift_right_ref,
    delta_ref,
    back_ref,
    *,
    lat_count,
    coarse_cols,
    band_rows,
    band_cols,
):
    rows, cols, _ = lift_ref.shape
    wide = bh_ref.shape[1]
    pairs = bh_ref.shape[0] // 2
    depth = cells_ref.shape[0]
    half_rows = msg_ref.shape[1]
    lat = place_ref[0]
    lon = place_ref[1]
    core = place_ref[2]
    taps = 3 * SPAN

    def send(at, value):
        side = lax.rem(at // half_rows + core, 2)
        at = at % half_rows
        msg_ref[side, at : at + value.shape[0]] = value.astype(BF16)

    for j in range(depth):
        cells_ref[j, :COL_HALO] = west_ref[j].astype(F32)
        cells_ref[j, COL_HALO:] = east_ref[j].astype(F32)
    spots = row_spots(place_ref, rsrc_ref, rfrac_ref, before_ref, after_ref, rows, band_rows, lat_count)
    side_mixed = blend_rows(cells_ref, spots)
    side_lifted = lift_rows(side_mixed, embed_ref[...])
    side_tap_ref[...] = tap_rows(side_lifted, w1_ref, band_cols)

    lane_count = 2 * LANES
    lane = lax.broadcasted_iota(jnp.int32, (1, lane_count), 1)
    west_line = edge_line(jnp.concatenate([west_ref[j] for j in (depth, depth + 1)], axis=0).astype(F32), 4)
    east_line = edge_line(jnp.concatenate([east_ref[j] for j in (depth, depth + 1)], axis=0).astype(F32), 4)
    own_line = (csrc_ref[...].astype(F32), cfrac_ref[...])
    blank = jnp.zeros((1, lane_count - cols), F32)
    lines = []
    for parts in zip(west_line, own_line, east_line):
        out = []
        for part, shift in zip(parts, (lane_count - cols + 2, 2, cols + 2)):
            part = jnp.concatenate([part, blank], axis=1)
            out.append(pltpu.roll(jnp.broadcast_to(part, (8, lane_count)), shift, 1)[:1])
        lines.append(jnp.where(lane < 2, out[0], jnp.where(lane < cols + 2, out[1], out[2])))
    known = lane < cols + 4
    src = jnp.where(known, lines[0], -1e6).astype(jnp.int32)
    blend = blend_cols(src, jnp.where(known, lines[1], 0.0), lon, band_cols, coarse_cols)
    rolled = [blend] + [pltpu.roll(blend, lane_count - b, 1) for b in (1, 2)]
    stack = jnp.concatenate(rolled, axis=0)[:, :wide]
    high, low = split_two(stack)
    high_f, low_f = high.astype(F32), low.astype(F32)
    col_t = jnp.concatenate([high_f, low_f], axis=0).astype(BF16)
    col_lhs = jnp.concatenate([high_f.T, low_f.T, high_f.T], axis=1).astype(BF16)
    own_hi, own_lo = split_two(rolled[2][:, :cols])
    own_hi, own_lo = own_hi.astype(F32).T, own_lo.astype(F32).T
    own_lhs = jnp.concatenate([own_hi, own_lo, own_hi], axis=1).astype(BF16)

    def stacked(value):
        one, two = split_two(value)
        return jnp.concatenate([one, one, two], axis=0)

    for t in range(2 * pairs):
        part = slice(t * band_cols, (t + 1) * band_cols)
        blocks = []
        for b in range(3):
            column = slice(b * LANES, (b + 1) * LANES)
            blocks += [tap_ref[part, column], side_tap_ref[part, column]]
        right_ref[:, t * LANES : (t + 1) * LANES] = stacked(jnp.concatenate(blocks, axis=0))
    for r in range(rows):
        part = slice((r + 2) * band_cols, (r + 3) * band_cols)
        lift_right_ref[:, r * LANES : (r + 1) * LANES] = stacked(
            jnp.concatenate([lifted_ref[part], side_lifted[part]], axis=0)
        )
    pre = jnp.dot(col_lhs, right_ref[...], preferred_element_type=F32)
    for t in range(2 * pairs):
        v = pre[:, t * LANES : (t + 1) * LANES]
        s = 0.5 + 0.5 * jnp.tanh(0.5 * v)
        if t == 0:
            s = s * jnp.where(lat > 0, 1.0, 0.0)
        elif t == 2 * pairs - 1:
            s = s * jnp.where(lat < lat_count - 1, 1.0, 0.0)
        h = v * s
        slope = s + h * (1.0 - s)
        line_ref[t] = h
        delta_ref[:, t * LANES : (t + 1) * LANES] = (bh_ref[t] * slope).astype(BF16)
    for t in range(2 * pairs):
        for b in range(3):
            at = (t // 2) * cols
            hid_ref[b, t % 2, at : at + cols] = line_ref[t, b : b + cols].astype(BF16)
    own = jnp.dot(own_lhs, lift_right_ref[...], preferred_element_type=F32)
    for r in range(rows):
        lift_ref[r] = own[:, r * LANES : (r + 1) * LANES]

    back = jnp.dot(col_t, delta_ref[...], preferred_element_type=F32)
    back = back[:taps] + back[taps:]
    width = rows_ref.shape[2]
    used = 2 * pairs * band_cols
    blank = jnp.zeros((2, width - used, back_ref.shape[2]), BF16)
    back_ref[:, used:width] = blank
    back_ref[:, width + used :] = blank
    nothing = jnp.zeros((SPAN, LANES), F32)
    for p in range(pairs):
        for b in range(4):
            lines = []
            for t in (2 * p, 2 * p + 1):
                if b < 3:
                    lines.append(back[b * SPAN : (b + 1) * SPAN, t * LANES : (t + 1) * LANES])
                else:
                    lines.append(cot_col_ref[t - 1] if 1 <= t <= rows else nothing)
            column = slice(b * LANES, (b + 1) * LANES)
            for side in range(2):
                cells = slice(side * band_cols, (side + 1) * band_cols)
                one, two = split_two(jnp.concatenate([v[cells] for v in lines], axis=0))
                at = side * width + p * SPAN
                back_ref[0, at : at + SPAN, column] = one
                back_ref[1, at : at + SPAN, column] = two
    side_hi, side_lo = turned_rows(side_mixed, width)
    upper = jnp.concatenate([rows_ref[0], side_hi], axis=1)
    lower = jnp.concatenate([rows_ref[1], side_lo], axis=1)
    g = jnp.dot(jnp.concatenate([upper, lower], axis=0), back_ref[0], preferred_element_type=F32)
    g = g[: 3 * GRAD_ROWS] + g[3 * GRAD_ROWS :]
    g = g + jnp.dot(upper, back_ref[1], preferred_element_type=F32)
    for a in range(3):
        line = g[a * GRAD_ROWS : (a + 1) * GRAD_ROWS]
        for b in range(3):
            send(9 * LANES + (a * 3 + b) * GRAD_ROWS, line[:, b * LANES : (b + 1) * LANES])
    send(9 * LANES + 9 * GRAD_ROWS, g[GRAD_ROWS : 2 * GRAD_ROWS, 3 * LANES:])
    tail = 9 * LANES + 10 * GRAD_ROWS
    if 2 * half_rows > tail:
        send(tail, jnp.zeros((2 * half_rows - tail, LANES), F32))

    half = (rows // 2) * cols
    left_t = turned_ref[...]
    for b in range(3):
        right = jnp.concatenate(
            [hid_ref[b, i % 2, (i // 2) * cols : (i // 2) * cols + half] for i in range(4)], axis=1
        )
        out = jnp.dot(left_t, right, preferred_element_type=F32)
        for a in range(3):
            upper = out[:LANES, a * LANES : (a + 1) * LANES]
            lower = out[LANES:, (a + 1) * LANES : (a + 2) * LANES]
            tap = a * 3 + b
            send(tap * LANES, (upper + lower).T)


def features_kernel(weight_ref, hid_ref, lift_ref, *refs, first, last):
    out_hbm, feat_ref, sems = refs[-3:]
    cols = feat_ref.shape[1]
    step = (last - first) // sems.shape[0]
    copies = []
    for n in range(sems.shape[0]):
        top = first + n * step
        blocks = []
        for b in range(3):
            for i in range(4):
                start = (top + i // 2) * cols
                blocks.append(hid_ref[b, i % 2, start : start + step * cols])
        out = jnp.dot(jnp.concatenate(blocks, axis=1), weight_ref[...], preferred_element_type=F32)
        for m in range(step):
            for q in range(2):
                piece = out[m * cols : (m + 1) * cols, q * LANES : (q + 1) * LANES]
                r = 2 * (top + m) + q
                feat_ref[r - 2 * first] = (lift_ref[r] + piece).astype(BF16)
        part = feat_ref.at[pl.ds(2 * n * step, 2 * step)]
        copies.append(pltpu.make_async_copy(part, out_hbm.at[pl.ds(2 * top, 2 * step)], sems.at[n]))
        copies[-1].start()
    for copy in copies:
        copy.wait()


def reduce_kernel(in_ref, out_ref):
    total = in_ref[0].astype(F32)
    for d in range(1, in_ref.shape[0]):
        total = total + in_ref[d].astype(F32)
    total = total.astype(BF16)
    for d in range(out_ref.shape[0]):
        out_ref[d] = total


def padded_embed(embed_ref, space_ref):
    fields = embed_ref.shape[0]
    space_ref[0, :LANES] = jnp.zeros((LANES, LANES), F32)
    space_ref[0, :fields] = embed_ref[...].astype(F32)
    return space_ref[0, :LANES].astype(BF16)


def last_kernel(
    place_ref, mine_ref, other_ref, embed_ref, first_ref, ge_hbm, g1_hbm, g2_hbm,
    sum_ref, ge_ref, g1_ref, g2_ref, sems, *, scale
):
    core = place_ref[2]
    half_rows = mine_ref.shape[0]
    sum_ref[core] = mine_ref[...]
    sum_ref[1 - core] = other_ref[...]

    def read(at, count):
        return sum_ref[at // half_rows, at % half_rows : at % half_rows + count]

    copies = []

    def leave(source, target):
        copies.append(pltpu.make_async_copy(source, target, sems.at[len(copies)]))
        copies[-1].start()

    for a in range(3):
        for tap in range(3 * a, 3 * a + 3):
            g2_ref[tap] = read(tap * LANES, LANES).astype(F32) * scale
        leave(g2_ref.at[pl.ds(3 * a, 3)], g2_hbm.at[pl.ds(3 * a, 3)])
    embed_t = embed_ref[...].astype(F32).T.astype(BF16)[:, :GRAD_ROWS]
    base = 9 * LANES
    g = jnp.concatenate([read(base + tap * GRAD_ROWS, GRAD_ROWS) for tap in range(9)], axis=1)
    for a in range(3):
        part = g[:, 3 * a * LANES : (3 * a + 3) * LANES]
        out = jnp.dot(embed_t, part, preferred_element_type=F32) * scale
        for b in range(3):
            g1_ref[3 * a + b] = out[:, b * LANES : (b + 1) * LANES]
        leave(g1_ref.at[pl.ds(3 * a, 3)], g1_hbm.at[pl.ds(3 * a, 3)])
    lift = read(base + 9 * GRAD_ROWS, GRAD_ROWS).astype(F32)
    lift = lift + jnp.dot(g, first_ref[...], preferred_element_type=F32)
    ge_ref[...] = lift[: ge_ref.shape[0]] * scale
    leave(ge_ref, ge_hbm)
    for copy in copies:
        copy.wait()


def from_hbm(value):
    return pltpu.with_memory_space_constraint(value, pltpu.HBM)


def on_device(
    coarse,
    row_src,
    row_frac,
    col_src,
    col_frac,
    embed_weight,
    conv1_weight,
    conv2_weight,
    cotangent,
):
    lat_count = lax.axis_size("lat")
    ring_count = lax.axis_size("ring")
    core_count = lax.axis_size("core")
    lon_count = ring_count * core_count
    lat_place = lax.axis_index("lat")
    core_place = lax.axis_index("core")
    lon_place = lax.axis_index("ring") * core_count + core_place
    fields, band_rows, band_cols = coarse.shape
    rows, cols, hidden = cotangent.shape
    group = lat_count * ring_count
    wide = cols + 16
    pairs = rows // 2 + 1
    depth = band_rows + 2 * ROW_HALO
    params = pltpu.CompilerParams(vmem_limit_bytes=VMEM_BYTES)
    vmem = pl.BlockSpec(memory_space=pltpu.VMEM)
    smem = pl.BlockSpec(memory_space=pltpu.SMEM)
    far = pl.BlockSpec(memory_space=pltpu.HBM)

    w1 = conv1_weight.reshape(9, hidden, hidden)
    w2 = conv2_weight.reshape(9, hidden, hidden)
    place = jnp.stack([lat_place, lon_place, core_place]).astype(jnp.int32)
    row_line = (row_src.reshape(1, rows), row_frac.reshape(1, rows))
    col_line = (col_src.reshape(1, cols), col_frac.reshape(1, cols))

    pack_inputs = (
        jnp.transpose(coarse, (1, 2, 0)),
        *row_line,
        *col_line,
    )
    own, *lines = pl.pallas_call(
        pack_kernel,
        in_specs=[far] * 5,
        out_shape=[jax.ShapeDtypeStruct((band_rows + 1, band_cols, LANES), F32)]
        + [jax.ShapeDtypeStruct(x.shape, x.dtype) for x in pack_inputs[1:]],
        scratch_shapes=[
            pltpu.VMEM(pack_inputs[0].shape, BF16),
            pltpu.SemaphoreType.DMA((5,)),
        ],
        compiler_params=params,
        name="pack",
    )(*(from_hbm(x) for x in pack_inputs))
    own = own.astype(BF16)
    row_line, col_line = lines[:2], lines[2:]
    edge = own[band_rows:]
    to_next = own[band_rows - ROW_HALO :]
    to_last = jnp.concatenate([own[:ROW_HALO], edge])
    even = lat_place % 2 == 0
    inner = [(i, i ^ 1) for i in range(lat_count)]
    outer = [(i, i + 1) for i in range(1, lat_count - 1, 2)]
    outer = outer + [(j, i) for i, j in outer]
    got_outer = lax.ppermute(jnp.where(even, to_last, to_next), "lat", outer)
    got_inner = lax.ppermute(jnp.where(even, to_next, to_last), "lat", inner)
    before, after = got_outer, got_inner

    shift, back_weight, fore_weight, turned, first_weight, cot, near_w1, embed = pl.pallas_call(
        prepare_kernel,
        out_shape=[
            jax.ShapeDtypeStruct((3, 2, (pairs + 1) * wide, hidden), BF16),
            jax.ShapeDtypeStruct((12 * hidden, 2 * hidden), BF16),
            jax.ShapeDtypeStruct((12 * hidden, 2 * hidden), BF16),
            jax.ShapeDtypeStruct((2 * hidden, rows // 2 * cols), BF16),
            jax.ShapeDtypeStruct((9 * hidden, hidden), BF16),
            jax.ShapeDtypeStruct((rows, cols, hidden), BF16),
            jax.ShapeDtypeStruct((9, hidden, hidden), BF16),
            jax.ShapeDtypeStruct((LANES, hidden), BF16),
        ],
        in_specs=[far] * 4,
        scratch_shapes=[
            pltpu.VMEM((9, hidden, hidden), BF16),
            pltpu.VMEM((fields, hidden), BF16),
            pltpu.VMEM((4, wide + 16, hidden), F32),
            pltpu.SemaphoreType.DMA((11,)),
        ],
        compiler_params=params,
        name="prepare",
    )(from_hbm(cotangent), from_hbm(w2), from_hbm(w1), from_hbm(embed_weight))
    before, after, shift, back_weight = lax.optimization_barrier((before, after, shift, back_weight))
    before, after = jnp.where(even, before, after), jnp.where(even, after, before)

    def back_body(*refs):
        back_kernel(*refs, lat_count=lat_count, coarse_cols=band_cols * lon_count)

    reach = rows + 4
    width = -(-reach * band_cols // LANES) * LANES
    bh, mixed, lifted, tap, cot_col = pl.pallas_call(
        back_body,
        in_specs=[smem] * 3 + [vmem] * 10,
        out_shape=[
            jax.ShapeDtypeStruct((2 * pairs, wide, hidden), F32),
            jax.ShapeDtypeStruct((2, 3 * GRAD_ROWS, width), BF16),
            jax.ShapeDtypeStruct((reach * band_cols, hidden), F32),
            jax.ShapeDtypeStruct(((reach - 2) * band_cols, 3 * hidden), F32),
            jax.ShapeDtypeStruct((rows, SPAN, hidden), F32),
        ],
        scratch_shapes=[
            pltpu.VMEM((depth, band_cols, LANES), F32),
        ],
        compiler_params=params,
        name="back_hidden",
    )(
        place, *row_line, shift, back_weight, before, own, after, *col_line,
        embed, near_w1, cot,
    )

    tall = jnp.concatenate([before[:ROW_HALO], own[:band_rows], after[:ROW_HALO]])
    lines = edge.reshape(band_cols // COL_HALO, COL_HALO, LANES)
    lon = ("ring", "core")
    to_next = jnp.concatenate([tall[:, band_cols - COL_HALO :], lines])
    to_last = jnp.concatenate([tall[:, :COL_HALO], lines])
    first = core_place == 0
    inner = [(i, i ^ 1) for i in range(lon_count)]
    outer = [(i, (i + (1 if i % 2 else -1)) % lon_count) for i in range(lon_count)]
    got_outer = lax.ppermute(jnp.where(first, to_last, to_next), lon, outer)
    got_inner = lax.ppermute(jnp.where(first, to_next, to_last), lon, inner)
    west = jnp.where(first, got_outer, got_inner)
    east = jnp.where(first, got_inner, got_outer)

    blocks = 9 * LANES + 10 * GRAD_ROWS
    chunk = -(-blocks // (core_count * group * 16)) * 16
    half_rows = max(group * chunk, -(-blocks // (2 * LANES)) * LANES)

    def body(*refs):
        main_kernel(
            *refs,
            lat_count=lat_count,
            coarse_cols=band_cols * lon_count,
            band_rows=band_rows,
            band_cols=band_cols,
        )

    hid, lift, message = pl.pallas_call(
        body,
        in_specs=[smem] * 3 + [vmem] * 14,
        out_specs=[vmem] * 3,
        out_shape=[
            jax.ShapeDtypeStruct((3, 2, pairs * cols, hidden), BF16),
            jax.ShapeDtypeStruct((rows, cols, hidden), F32),
            jax.ShapeDtypeStruct((2, half_rows, LANES), BF16),
        ],
        scratch_shapes=[
            pltpu.VMEM((depth, 2 * COL_HALO, LANES), F32),
            pltpu.VMEM(((reach - 2) * band_cols, 3 * hidden), F32),
            pltpu.VMEM((2 * pairs, wide, hidden), F32),
            pltpu.VMEM((9 * SPAN, 2 * pairs * hidden), BF16),
            pltpu.VMEM((3 * SPAN, rows * hidden), BF16),
            pltpu.VMEM((wide, 2 * pairs * hidden), BF16),
            pltpu.VMEM((2, 2 * width, 4 * hidden), BF16),
        ],
        compiler_params=params,
        name="tile",
    )(
        place, *row_line, before, after, west, east, *col_line,
        embed, near_w1, turned, bh, mixed, lifted, tap, cot_col,
    )

    def half_features(first, last, *arrays):
        def body(*refs):
            features_kernel(*refs, first=first, last=last)

        return pl.pallas_call(
            body,
            in_specs=[vmem] * 3 + [far] * (len(arrays) - 3),
            out_specs=far,
            out_shape=jax.ShapeDtypeStruct((rows, cols, hidden), BF16),
            input_output_aliases={n: 0 for n in range(3, len(arrays))},
            scratch_shapes=[
                pltpu.VMEM((2 * (last - first), cols, hidden), BF16),
                pltpu.SemaphoreType.DMA((2,)),
            ],
            compiler_params=params,
            name=f"features_{first}",
        )(*arrays)

    swap = [(0, 1), (1, 0)]
    received = lax.ppermute(message[1], "core", swap)
    middle = rows // 4
    part = half_features(0, middle, fore_weight, hid, lift)
    received, part = lax.optimization_barrier((received, part))
    pair = (message[0].astype(F32) + received.astype(F32)).astype(BF16)
    axes = ("lat", "ring")
    chunk = half_rows // group
    parts = lax.all_to_all(pair, axes, 0, 0, tiled=True)
    copies = pl.pallas_call(
        reduce_kernel,
        out_shape=jax.ShapeDtypeStruct((group, chunk, LANES), BF16),
        compiler_params=params,
        name="sum_chunks",
    )(parts.reshape(group, chunk, LANES))
    mine = lax.all_to_all(copies.reshape(half_rows, LANES), axes, 0, 0, tiled=True)
    other = lax.ppermute(mine, "core", swap)
    _, part = lax.optimization_barrier((mine, part))
    features = half_features(middle, rows // 2, fore_weight, hid, lift, part)
    scale = 1.0 / math.sqrt(rows * lat_count * cols * lon_count)

    def finish(*refs):
        last_kernel(*refs, scale=scale)

    grad_embed, grad_first, grad_second = pl.pallas_call(
        finish,
        in_specs=[smem] + [vmem] * 4,
        out_specs=[far] * 3,
        out_shape=[
            jax.ShapeDtypeStruct((fields, hidden), F32),
            jax.ShapeDtypeStruct((9, hidden, hidden), F32),
            jax.ShapeDtypeStruct((9, hidden, hidden), F32),
        ],
        scratch_shapes=[
            pltpu.VMEM((2, half_rows, LANES), BF16),
            pltpu.VMEM((fields, hidden), F32),
            pltpu.VMEM((9, hidden, hidden), F32),
            pltpu.VMEM((9, hidden, hidden), F32),
            pltpu.SemaphoreType.DMA((7,)),
        ],
        compiler_params=params,
        name="finish",
    )(place, mine, other, embed, first_weight)
    shape = (3, 3, hidden, hidden)
    return (features, grad_embed, grad_first.reshape(shape), grad_second.reshape(shape))


def solution(mesh):
    lat_count, lon_count = mesh.devices.shape
    inner = jax.sharding.Mesh(
        mesh.devices.reshape(lat_count, lon_count // 2, 2), ("lat", "ring", "core")
    )
    lon = ("ring", "core")
    in_specs = (
        P(None, "lat", lon),
        P("lat"),
        P("lat"),
        P(lon),
        P(lon),
        P(),
        P(),
        P(),
        P("lat", lon, None),
    )
    out_specs = (P("lat", lon, None), P(), P(), P())
    return jax.shard_map(
        on_device, mesh=inner, in_specs=in_specs, out_specs=out_specs, check_vma=False
    )
```

```python
import math

import jax
import jax.numpy as jnp
from jax import lax
from jax.experimental import pallas as pl
from jax.experimental.pallas import tpu as pltpu
from jax.sharding import PartitionSpec as P

F32 = jnp.float32
BF16 = jnp.bfloat16
LANES = 128
ROW_HALO = 3
COL_HALO = 4
SPAN = 16
GRAD_ROWS = 80
VMEM_BYTES = 24 * 1024 * 1024


def split_two(value):
    high = value.astype(BF16)
    return high, (value - high.astype(F32)).astype(BF16)


def prepare_kernel(
    cot_hbm, w2_hbm, w1_hbm, embed_hbm,
    shift_ref, back_ref, fore_ref, turned_ref, first_ref, cot_ref, w1_ref, padded_ref,
    w2_ref, embed_ref, line_ref, sems
):
    rows, cols, _ = cot_ref.shape
    wide = cols + 16
    pairs = rows // 2 + 1
    chunks = sems.shape[0] - 3
    share = rows // chunks
    weight_copy = pltpu.make_async_copy(w2_hbm, w2_ref, sems.at[chunks])
    weight_copy.start()
    copies = []
    for n in range(chunks):
        part = pl.ds(n * share, share)
        copies.append(pltpu.make_async_copy(cot_hbm.at[part], cot_ref.at[part], sems.at[n]))
        copies[-1].start()
    other_copy = pltpu.make_async_copy(w1_hbm, w1_ref, sems.at[chunks + 1])
    other_copy.start()
    embed_copy = pltpu.make_async_copy(embed_hbm, embed_ref, sems.at[chunks + 2])
    embed_copy.start()
    line_ref[...] = jnp.zeros_like(line_ref)
    back_ref[...] = jnp.zeros_like(back_ref)
    fore_ref[...] = jnp.zeros_like(fore_ref)
    blank = jnp.zeros((wide, LANES), BF16)
    for b in range(3):
        for parity in range(2):
            shift_ref[b, parity, 0:wide] = blank
            shift_ref[b, parity, pairs * wide : (pairs + 1) * wide] = blank
    weight_copy.wait()
    for a in range(3):
        for b in range(3):
            straight = w2_ref[a * 3 + b]
            turned = straight.astype(F32).T.astype(BF16)
            for q in range(2):
                column = slice(q * LANES, (q + 1) * LANES)
                at = (b * 4 + 2 + q - a) * LANES
                back_ref[at : at + LANES, column] = turned
                at = (b * 4 + a + q) * LANES
                fore_ref[at : at + LANES, column] = straight
    for r in range(rows):
        slot = r % 4
        if r % share == 0:
            copies[r // share].wait()
        line = cot_ref[r].astype(F32)
        line_ref[slot, 8 : 8 + cols] = line
        start = (r // 2 + 1) * wide
        for b in range(3):
            shift_ref[b, r % 2, start : start + wide] = line_ref[slot, 8 - b : 8 - b + wide].astype(BF16)
        turned_ref[(r % 2) * LANES : (r % 2 + 1) * LANES, (r // 2) * cols : (r // 2 + 1) * cols] = line.T.astype(BF16)
    embed_copy.wait()
    padded_ref[...] = padded_embed(embed_ref, line_ref)
    other_copy.wait()
    for tap in range(9):
        first_ref[tap * LANES : (tap + 1) * LANES] = w1_ref[tap].astype(F32).T.astype(BF16)


def edge_line(block, at):
    index = block[at : at + 1]
    return index, block[at + 1 : at + 2] + block[at + 2 : at + 3] + block[at + 3 : at + 4]


def joined_line(first, own, last, width):
    lane_count = 2 * LANES
    lane = lax.broadcasted_iota(jnp.int32, (1, lane_count), 1)
    out = []
    for part, shift in zip((first, own, last), (lane_count - width + 2, 2, width + 2)):
        part = jnp.concatenate([part[:, :width], jnp.zeros((1, lane_count - width), F32)], axis=1)
        out.append(pltpu.roll(jnp.broadcast_to(part, (8, lane_count)), shift, 1)[:1])
    return jnp.where(lane < 2, out[0], jnp.where(lane < width + 2, out[1], out[2]))


def row_blend(rsrc_ref, rfrac_ref, before_ref, after_ref, lat, lat_count, band_rows):
    rows = rsrc_ref.shape[1]
    cells = 2 * COL_HALO
    before_line = edge_line(before_ref[ROW_HALO].astype(F32), 0)
    after_line = edge_line(after_ref[ROW_HALO].astype(F32), 0)
    own_line = (rsrc_ref[...].astype(F32), rfrac_ref[...])
    src, frac = (
        joined_line(*lines, rows) for lines in zip(before_line, own_line, after_line)
    )
    spot = (src - (lat * band_rows - ROW_HALO).astype(F32)) * cells
    shape = (cells, LANES)
    at = lax.broadcasted_iota(jnp.int32, shape, 1) - lax.broadcasted_iota(jnp.int32, shape, 0)
    at = at.astype(F32)
    parts = []
    for q in range(rows + 4):
        here = jnp.broadcast_to(spot[:, q : q + 1], shape)
        f = jnp.broadcast_to(frac[:, q : q + 1], shape)
        part = jnp.where(at == here, 1.0 - f, 0.0) + jnp.where(at == here + cells, f, 0.0)
        if q < 2:
            part = part * jnp.where(lat > 0, 1.0, 0.0)
        elif q >= rows + 2:
            part = part * jnp.where(lat < lat_count - 1, 1.0, 0.0)
        parts.append(part)
    return jnp.concatenate(list(split_two(jnp.concatenate(parts, axis=0))), axis=1)


def blend_rows(matrix, cells):
    fill = jnp.zeros((LANES - sum(c.shape[0] for c in cells), LANES), F32)
    column = jnp.concatenate(list(cells) + [fill], axis=0).astype(BF16)
    return jnp.dot(matrix, jnp.concatenate([column, column], axis=0), preferred_element_type=F32)


def lift_rows(mixed, embed):
    pair = jnp.concatenate(list(split_two(mixed)), axis=1)
    return jnp.dot(pair, jnp.concatenate([embed, embed], axis=0), preferred_element_type=F32)


def turned_rows(mixed, width):
    fill = jnp.zeros((width - mixed.shape[0], LANES), F32)
    turned = jnp.concatenate([mixed, fill], axis=0).T[:GRAD_ROWS]
    step = 2 * COL_HALO
    lines = [turned] + [pltpu.roll(turned, width - a * step, 1) for a in (1, 2)]
    return split_two(jnp.concatenate(lines, axis=0))


def tap_rows(lifted, w1_ref, cells):
    count = lifted.shape[0] - 2 * cells
    pairs = [split_two(lifted[a * cells : a * cells + count]) for a in range(3)]
    left = jnp.concatenate([p[0] for p in pairs] + [p[1] for p in pairs], axis=1)
    lines = [jnp.concatenate([w1_ref[a * 3 + b] for b in range(3)], axis=1) for a in range(3)]
    return jnp.dot(left, jnp.concatenate(lines + lines, axis=0), preferred_element_type=F32)


def blend_cols(src, frac, lon, band_cols, coarse_cols):
    shape = (SPAN, src.shape[1])
    local = jnp.broadcast_to(src, shape) - lon * band_cols
    frac = jnp.broadcast_to(frac, shape)
    local = jnp.where(local < -COL_HALO, local + coarse_cols, local)
    local = jnp.where(local >= band_cols + COL_HALO, local - coarse_cols, local)
    line = lax.broadcasted_iota(jnp.int32, shape, 0)

    def spot(at):
        east = jnp.where(at >= band_cols, at + COL_HALO, at)
        return jnp.where(at < 0, at + band_cols + COL_HALO, east)

    return jnp.where(line == spot(local), 1.0 - frac, 0.0) + jnp.where(
        line == spot(local + 1), frac, 0.0
    )


def back_kernel(
    rsrc_ref,
    rfrac_ref,
    shift_ref,
    weight_ref,
    before_ref,
    own_ref,
    after_ref,
    csrc_ref,
    cfrac_ref,
    embed_ref,
    w1_ref,
    cot_ref,
    bh_ref,
    rows_ref,
    lifted_ref,
    tap_ref,
    cot_col_ref,
    blend_ref,
    *,
    lat_count,
    coarse_cols,
):
    rows, cols, _ = cot_ref.shape
    wide = bh_ref.shape[1]
    pairs = bh_ref.shape[0] // 2
    band_rows, band_cols = own_ref.shape[0] - 1, own_ref.shape[1]
    step = 6
    for first in range(0, pairs, step):
        count = min(step, pairs - first)
        blocks = []
        for b in range(3):
            for i in range(4):
                start = (first + i // 2) * wide
                blocks.append(shift_ref[b, i % 2, start : start + count * wide])
        out = jnp.dot(jnp.concatenate(blocks, axis=1), weight_ref[...], preferred_element_type=F32)
        for m in range(count):
            for q in range(2):
                bh_ref[2 * (first + m) + q] = out[m * wide : (m + 1) * wide, q * LANES : (q + 1) * LANES]

    lat = lax.axis_index("lat")
    lon = lax.axis_index("ring") * 2 + lax.axis_index("core")
    matrix = row_blend(rsrc_ref, rfrac_ref, before_ref, after_ref, lat, lat_count, band_rows)
    blend_ref[...] = matrix
    cells = [before_ref[j] for j in range(ROW_HALO)] + [own_ref[j] for j in range(band_rows)]
    cells += [after_ref[j] for j in range(ROW_HALO)]
    mixed = blend_rows(matrix, [c.astype(F32) for c in cells])
    rows_ref[0], rows_ref[1] = turned_rows(mixed, rows_ref.shape[2])
    lifted = lift_rows(mixed, embed_ref[...])
    lifted_ref[...] = lifted
    tap_ref[...] = tap_rows(lifted, w1_ref, band_cols)

    blend = blend_cols(csrc_ref[...], cfrac_ref[...], lon, band_cols, coarse_cols)
    own_t = jnp.concatenate(list(split_two(blend)), axis=0)
    every = jnp.concatenate([cot_ref[r] for r in range(rows)], axis=1)
    back = jnp.dot(own_t, every, preferred_element_type=F32)
    back = back[:SPAN] + back[SPAN:]
    for r in range(rows):
        cot_col_ref[r] = back[:, r * LANES : (r + 1) * LANES]


def pack_kernel(cells_hbm, rsrc_hbm, rfrac_hbm, csrc_hbm, cfrac_hbm, out_ref, *space):
    sources = (cells_hbm, rsrc_hbm, rfrac_hbm, csrc_hbm, cfrac_hbm)
    *lines, cells_ref, sems = space
    targets = (cells_ref, *lines)
    copies = [
        pltpu.make_async_copy(source, target, sems.at[n])
        for n, (source, target) in enumerate(zip(sources, targets))
    ]
    for copy in copies:
        copy.start()
    cells_ref, rsrc_ref, rfrac_ref, csrc_ref, cfrac_ref = targets
    depth, span, fields = cells_ref.shape
    out_ref[...] = jnp.zeros_like(out_ref)
    for copy in copies:
        copy.wait()
    for j in range(depth):
        out_ref[j, :, :fields] = cells_ref[j].astype(F32)
    at = 0
    for index_ref, fraction_ref in ((rsrc_ref, rfrac_ref), (csrc_ref, cfrac_ref)):
        width = index_ref.shape[1]
        fraction = fraction_ref[...]
        one = fraction.astype(BF16).astype(F32)
        two = (fraction - one).astype(BF16).astype(F32)
        for value in (index_ref[...].astype(F32), one, two, fraction - one - two):
            out_ref[depth, at : at + 1, :width] = value
            at += 1


def main_kernel(
    far_ref,
    near_ref,
    csrc_ref,
    cfrac_ref,
    embed_ref,
    w1_ref,
    turned_ref,
    bh_ref,
    rows_ref,
    lifted_ref,
    tap_ref,
    cot_col_ref,
    blend_ref,
    hid_ref,
    own_ref,
    lift_right_ref,
    msg_ref,
    side_tap_ref,
    line_ref,
    right_ref,
    delta_ref,
    back_ref,
    *,
    lat_count,
    coarse_cols,
    band_cols,
):
    rows, cols = cot_col_ref.shape[0], own_ref.shape[0]
    wide = bh_ref.shape[1]
    pairs = bh_ref.shape[0] // 2
    depth = 2 * (far_ref.shape[0] - 1)
    half_rows = msg_ref.shape[1]
    lat = lax.axis_index("lat")
    core = lax.axis_index("core")
    lon = lax.axis_index("ring") * 2 + core
    taps = 3 * SPAN

    def send(at, value):
        side = lax.rem(at // half_rows + core, 2)
        at = at % half_rows
        msg_ref[side, at : at + value.shape[0]] = value.astype(BF16)

    sides = []
    for j in range(depth // 2 + 1):
        far, near = far_ref[j].astype(F32), near_ref[j].astype(F32)
        sides.append((jnp.where(core == 1, near, far), jnp.where(core == 1, far, near)))
    cells = []
    for j in range(depth):
        part = slice(j % 2 * COL_HALO, (j % 2 + 1) * COL_HALO)
        cells += [v[part] for v in sides[j // 2]]
    side_mixed = blend_rows(blend_ref[...], cells)
    side_lifted = lift_rows(side_mixed, embed_ref[...])
    side_tap_ref[...] = tap_rows(side_lifted, w1_ref, band_cols)

    lane_count = 2 * LANES
    lane = lax.broadcasted_iota(jnp.int32, (1, lane_count), 1)
    west_line, east_line = (edge_line(v, 4) for v in sides[depth // 2])
    own_line = (csrc_ref[...].astype(F32), cfrac_ref[...])
    lines = [joined_line(*v, cols) for v in zip(west_line, own_line, east_line)]
    known = lane < cols + 4
    src = jnp.where(known, lines[0], -1e6).astype(jnp.int32)
    blend = blend_cols(src, jnp.where(known, lines[1], 0.0), lon, band_cols, coarse_cols)
    rolled = [blend] + [pltpu.roll(blend, lane_count - b, 1) for b in (1, 2)]
    stack = jnp.concatenate(rolled, axis=0)[:, :wide]
    high, low = split_two(stack)
    high_f, low_f = high.astype(F32), low.astype(F32)
    col_t = jnp.concatenate([high_f, low_f], axis=0).astype(BF16)
    col_lhs = jnp.concatenate([high_f.T, low_f.T, high_f.T], axis=1).astype(BF16)
    own_hi, own_lo = split_two(rolled[2][:, :cols])
    own_hi, own_lo = own_hi.astype(F32).T, own_lo.astype(F32).T
    own_ref[...] = jnp.concatenate([own_hi, own_lo, own_hi], axis=1).astype(BF16)

    def stacked(value):
        one, two = split_two(value)
        return jnp.concatenate([one, one, two], axis=0)

    for t in range(2 * pairs):
        part = slice(t * band_cols, (t + 1) * band_cols)
        blocks = []
        for b in range(3):
            column = slice(b * LANES, (b + 1) * LANES)
            blocks += [tap_ref[part, column], side_tap_ref[part, column]]
        right_ref[:, t * LANES : (t + 1) * LANES] = stacked(jnp.concatenate(blocks, axis=0))
    for r in range(rows):
        part = slice((r + 2) * band_cols, (r + 3) * band_cols)
        lift_right_ref[:, r * LANES : (r + 1) * LANES] = stacked(
            jnp.concatenate([lifted_ref[part], side_lifted[part]], axis=0)
        )
    half = rows // 2 + 2
    spans = ((0, half), (half, 2 * pairs))
    cells_half = rows // 4 * cols

    def first_product(n):
        span = slice(spans[n][0] * LANES, spans[n][1] * LANES)
        return jnp.dot(col_lhs, right_ref[:, span], preferred_element_type=F32)

    def activate(pre, first, t):
        v = pre[:, (t - first) * LANES : (t - first + 1) * LANES]
        s = 0.5 + 0.5 * jnp.tanh(0.5 * v)
        if t == 0:
            s = s * jnp.where(lat > 0, 1.0, 0.0)
        elif t == 2 * pairs - 1:
            s = s * jnp.where(lat < lat_count - 1, 1.0, 0.0)
        h = v * s
        slope = s + h * (1.0 - s)
        line_ref[t] = h
        delta_ref[:, t * LANES : (t + 1) * LANES] = (bh_ref[t] * slope).astype(BF16)

    def place_hidden(t):
        at = (t // 2) * cols
        for b in range(3):
            hid_ref[b, t % 2, at : at + cols] = line_ref[t, b : b + cols].astype(BF16)

    def second_gradient(n, b):
        right = []
        for i in range(4):
            start = (i // 2) * cols + n * cells_half
            right.append(hid_ref[b, i % 2, start : start + cells_half])
        left = turned_ref[:, n * cells_half : (n + 1) * cells_half]
        return jnp.dot(left, jnp.concatenate(right, axis=1), preferred_element_type=F32)

    pre = first_product(0)
    for t in range(*spans[0]):
        activate(pre, 0, t)
    pre = first_product(1)
    for t in range(*spans[0]):
        place_hidden(t)
    grads = []
    rest = list(range(*spans[1]))
    share = -(-len(rest) // 3)
    for b in range(3):
        grads.append(second_gradient(0, b))
        for t in rest[b * share : (b + 1) * share]:
            activate(pre, spans[1][0], t)
            place_hidden(t)
    back = jnp.dot(col_t, delta_ref[...], preferred_element_type=F32)
    back = back[:taps] + back[taps:]
    for b in range(3):
        grads[b] = grads[b] + second_gradient(1, b)

    width = rows_ref.shape[2]
    used = 2 * pairs * band_cols
    blank = jnp.zeros((2, width - used, back_ref.shape[2]), BF16)
    back_ref[:, used:width] = blank
    back_ref[:, width + used :] = blank
    nothing = jnp.zeros((SPAN, LANES), F32)
    for p in range(pairs):
        for b in range(4):
            lines = []
            for t in (2 * p, 2 * p + 1):
                if b < 3:
                    lines.append(back[b * SPAN : (b + 1) * SPAN, t * LANES : (t + 1) * LANES])
                else:
                    lines.append(cot_col_ref[t - 1] if 1 <= t <= rows else nothing)
            column = slice(b * LANES, (b + 1) * LANES)
            for side in range(2):
                cells = slice(side * band_cols, (side + 1) * band_cols)
                one, two = split_two(jnp.concatenate([v[cells] for v in lines], axis=0))
                at = side * width + p * SPAN
                back_ref[0, at : at + SPAN, column] = one
                back_ref[1, at : at + SPAN, column] = two
    side_hi, side_lo = turned_rows(side_mixed, width)
    upper = jnp.concatenate([rows_ref[0], side_hi], axis=1)
    lower = jnp.concatenate([rows_ref[1], side_lo], axis=1)
    g = jnp.dot(jnp.concatenate([upper, lower], axis=0), back_ref[0], preferred_element_type=F32)
    g = g[: 3 * GRAD_ROWS] + g[3 * GRAD_ROWS :]
    g = g + jnp.dot(upper, back_ref[1], preferred_element_type=F32)
    for a in range(3):
        line = g[a * GRAD_ROWS : (a + 1) * GRAD_ROWS]
        for b in range(3):
            send(9 * LANES + (a * 3 + b) * GRAD_ROWS, line[:, b * LANES : (b + 1) * LANES])
    send(9 * LANES + 9 * GRAD_ROWS, g[GRAD_ROWS : 2 * GRAD_ROWS, 3 * LANES:])
    tail = 9 * LANES + 10 * GRAD_ROWS
    if 2 * half_rows > tail:
        send(tail, jnp.zeros((2 * half_rows - tail, LANES), F32))

    for b in range(3):
        for a in range(3):
            upper = grads[b][:LANES, a * LANES : (a + 1) * LANES]
            lower = grads[b][LANES:, (a + 1) * LANES : (a + 2) * LANES]
            send((a * 3 + b) * LANES, (upper + lower).T)


def join_kernel(own_ref, inner_ref, outer_ref, ready_ref, before_ref, after_ref, far_ref, near_ref):
    band_rows, band_cols = own_ref.shape[0] - 1, own_ref.shape[1]
    even = lax.rem(lax.axis_index("lat"), 2) == 0
    first = lax.axis_index("core") == 0
    outer = [outer_ref[j].astype(F32) for j in range(ROW_HALO + 1)]
    inner = [inner_ref[j].astype(F32) for j in range(ROW_HALO + 1)]
    before = [jnp.where(even, v, w) for v, w in zip(outer, inner)]
    after = [jnp.where(even, w, v) for v, w in zip(outer, inner)]
    own = [own_ref[j].astype(F32) for j in range(band_rows + 1)]
    for j in range(ROW_HALO + 1):
        before_ref[j] = before[j].astype(BF16)
        after_ref[j] = after[j].astype(BF16)
    tall = before[:ROW_HALO] + own[:band_rows] + after[:ROW_HALO]
    for j in range(0, len(tall), 2):
        to_last = jnp.concatenate([v[:COL_HALO] for v in tall[j : j + 2]], axis=0)
        to_next = jnp.concatenate([v[band_cols - COL_HALO :] for v in tall[j : j + 2]], axis=0)
        far_ref[j // 2] = jnp.where(first, to_last, to_next).astype(BF16)
        near_ref[j // 2] = jnp.where(first, to_next, to_last).astype(BF16)
    far_ref[len(tall) // 2] = own[band_rows].astype(BF16)
    near_ref[len(tall) // 2] = own[band_rows].astype(BF16)


def features_kernel(weight_ref, hid_ref, own_ref, lift_right_ref, *refs, first):
    feat_ref = refs[-1]
    rows, cols, _ = feat_ref.shape
    step = 4
    for n in range(0, rows // 2, step):
        top = first + n
        blocks = []
        for b in range(3):
            for i in range(4):
                start = (top + i // 2) * cols
                blocks.append(hid_ref[b, i % 2, start : start + step * cols])
        out = jnp.dot(jnp.concatenate(blocks, axis=1), weight_ref[...], preferred_element_type=F32)
        span = slice(2 * top * LANES, 2 * (top + step) * LANES)
        lift = jnp.dot(own_ref[...], lift_right_ref[:, span], preferred_element_type=F32)
        for m in range(step):
            for q in range(2):
                piece = out[m * cols : (m + 1) * cols, q * LANES : (q + 1) * LANES]
                own = lift[:, (2 * m + q) * LANES : (2 * m + q + 1) * LANES]
                feat_ref[2 * (n + m) + q] = (own + piece).astype(BF16)


def reduce_kernel(in_ref, out_ref):
    total = in_ref[0].astype(F32)
    for d in range(1, in_ref.shape[0]):
        total = total + in_ref[d].astype(F32)
    total = total.astype(BF16)
    for d in range(out_ref.shape[0]):
        out_ref[d] = total


def padded_embed(embed_ref, space_ref):
    fields = embed_ref.shape[0]
    space_ref[0, :LANES] = jnp.zeros((LANES, LANES), F32)
    space_ref[0, :fields] = embed_ref[...].astype(F32)
    return space_ref[0, :LANES].astype(BF16)


def last_kernel(
    mine_ref, other_ref, embed_ref, first_ref, upper_ref, lower_ref, feat_hbm, ge_hbm, g1_hbm, g2_hbm,
    sum_ref, ge_ref, g1_ref, g2_ref, sems, *, scale
):
    core = lax.axis_index("core")
    half_rows = mine_ref.shape[0]
    copies = []

    def leave(source, target):
        copies.append(pltpu.make_async_copy(source, target, sems.at[len(copies)]))
        copies[-1].start()

    count = upper_ref.shape[0]
    leave(upper_ref, feat_hbm.at[pl.ds(0, count)])
    leave(lower_ref, feat_hbm.at[pl.ds(count, count)])
    sum_ref[core] = mine_ref[...]
    sum_ref[1 - core] = other_ref[...]

    def read(at, count):
        return sum_ref[at // half_rows, at % half_rows : at % half_rows + count]

    for a in range(3):
        for tap in range(3 * a, 3 * a + 3):
            g2_ref[tap] = read(tap * LANES, LANES).astype(F32) * scale
        leave(g2_ref.at[pl.ds(3 * a, 3)], g2_hbm.at[pl.ds(3 * a, 3)])
    embed_t = embed_ref[...].astype(F32).T.astype(BF16)[:, :GRAD_ROWS]
    base = 9 * LANES
    g = jnp.concatenate([read(base + tap * GRAD_ROWS, GRAD_ROWS) for tap in range(9)], axis=1)
    for a in range(3):
        part = g[:, 3 * a * LANES : (3 * a + 3) * LANES]
        out = jnp.dot(embed_t, part, preferred_element_type=F32) * scale
        for b in range(3):
            g1_ref[3 * a + b] = out[:, b * LANES : (b + 1) * LANES]
        leave(g1_ref.at[pl.ds(3 * a, 3)], g1_hbm.at[pl.ds(3 * a, 3)])
    lift = read(base + 9 * GRAD_ROWS, GRAD_ROWS).astype(F32)
    lift = lift + jnp.dot(g, first_ref[...], preferred_element_type=F32)
    ge_ref[...] = lift[: ge_ref.shape[0]] * scale
    leave(ge_ref, ge_hbm)
    for copy in copies:
        copy.wait()


def from_hbm(value):
    return pltpu.with_memory_space_constraint(value, pltpu.HBM)


def on_device(
    coarse,
    row_src,
    row_frac,
    col_src,
    col_frac,
    embed_weight,
    conv1_weight,
    conv2_weight,
    cotangent,
):
    lat_count = lax.axis_size("lat")
    ring_count = lax.axis_size("ring")
    core_count = lax.axis_size("core")
    lon_count = ring_count * core_count
    lat_place = lax.axis_index("lat")
    core_place = lax.axis_index("core")
    lon_place = lax.axis_index("ring") * core_count + core_place
    fields, band_rows, band_cols = coarse.shape
    rows, cols, hidden = cotangent.shape
    group = lat_count * ring_count
    wide = cols + 16
    pairs = rows // 2 + 1
    depth = band_rows + 2 * ROW_HALO
    params = pltpu.CompilerParams(vmem_limit_bytes=VMEM_BYTES)
    vmem = pl.BlockSpec(memory_space=pltpu.VMEM)
    far = pl.BlockSpec(memory_space=pltpu.HBM)

    w1 = conv1_weight.reshape(9, hidden, hidden)
    w2 = conv2_weight.reshape(9, hidden, hidden)
    row_line = (row_src.reshape(1, rows), row_frac.reshape(1, rows))
    col_line = (col_src.reshape(1, cols), col_frac.reshape(1, cols))

    pack_inputs = (
        jnp.transpose(coarse, (1, 2, 0)),
        *row_line,
        *col_line,
    )
    own, *lines = pl.pallas_call(
        pack_kernel,
        in_specs=[far] * 5,
        out_shape=[jax.ShapeDtypeStruct((band_rows + 1, band_cols, LANES), F32)]
        + [jax.ShapeDtypeStruct(x.shape, x.dtype) for x in pack_inputs[1:]],
        scratch_shapes=[
            pltpu.VMEM(pack_inputs[0].shape, BF16),
            pltpu.SemaphoreType.DMA((5,)),
        ],
        compiler_params=params,
        name="pack",
    )(*(from_hbm(x) for x in pack_inputs))
    own = own.astype(BF16)
    row_line, col_line = lines[:2], lines[2:]
    edge = own[band_rows:]
    to_next = own[band_rows - ROW_HALO :]
    to_last = jnp.concatenate([own[:ROW_HALO], edge])
    even = lat_place % 2 == 0
    inner = [(i, i ^ 1) for i in range(lat_count)]
    outer = [(i, i + 1) for i in range(1, lat_count - 1, 2)]
    outer = outer + [(j, i) for i, j in outer]
    got_outer = lax.ppermute(jnp.where(even, to_last, to_next), "lat", outer)
    got_inner = lax.ppermute(jnp.where(even, to_next, to_last), "lat", inner)

    shift, back_weight, fore_weight, turned, first_weight, cot, near_w1, embed = pl.pallas_call(
        prepare_kernel,
        out_shape=[
            jax.ShapeDtypeStruct((3, 2, (pairs + 1) * wide, hidden), BF16),
            jax.ShapeDtypeStruct((12 * hidden, 2 * hidden), BF16),
            jax.ShapeDtypeStruct((12 * hidden, 2 * hidden), BF16),
            jax.ShapeDtypeStruct((2 * hidden, rows // 2 * cols), BF16),
            jax.ShapeDtypeStruct((9 * hidden, hidden), BF16),
            jax.ShapeDtypeStruct((rows, cols, hidden), BF16),
            jax.ShapeDtypeStruct((9, hidden, hidden), BF16),
            jax.ShapeDtypeStruct((LANES, hidden), BF16),
        ],
        in_specs=[far] * 4,
        scratch_shapes=[
            pltpu.VMEM((9, hidden, hidden), BF16),
            pltpu.VMEM((fields, hidden), BF16),
            pltpu.VMEM((4, wide + 16, hidden), F32),
            pltpu.SemaphoreType.DMA((11,)),
        ],
        compiler_params=params,
        name="prepare",
    )(from_hbm(cotangent), from_hbm(w2), from_hbm(w1), from_hbm(embed_weight))
    before, after, far_message, near_message = pl.pallas_call(
        join_kernel,
        out_shape=[jax.ShapeDtypeStruct((ROW_HALO + 1, band_cols, LANES), BF16)] * 2
        + [jax.ShapeDtypeStruct((depth // 2 + 1, band_cols, LANES), BF16)] * 2,
        compiler_params=params,
        name="join",
    )(own, got_inner, got_outer, embed)
    lon = ("ring", "core")
    inner = [(i, i ^ 1) for i in range(lon_count)]
    outer = [(i, (i + (1 if i % 2 else -1)) % lon_count) for i in range(lon_count)]
    got_far = lax.ppermute(far_message, lon, outer)
    got_near = lax.ppermute(near_message, lon, inner)

    def back_body(*refs):
        back_kernel(*refs, lat_count=lat_count, coarse_cols=band_cols * lon_count)

    reach = rows + 4
    width = -(-reach * band_cols // LANES) * LANES
    bh, mixed, lifted, tap, cot_col, blend = pl.pallas_call(
        back_body,
        out_shape=[
            jax.ShapeDtypeStruct((2 * pairs, wide, hidden), F32),
            jax.ShapeDtypeStruct((2, 3 * GRAD_ROWS, width), BF16),
            jax.ShapeDtypeStruct((reach * band_cols, hidden), F32),
            jax.ShapeDtypeStruct(((reach - 2) * band_cols, 3 * hidden), F32),
            jax.ShapeDtypeStruct((rows, SPAN, hidden), F32),
            jax.ShapeDtypeStruct((reach * band_cols, 2 * LANES), BF16),
        ],
        compiler_params=params,
        name="back_hidden",
    )(
        *row_line, shift, back_weight, before, own, after, *col_line,
        embed, near_w1, cot,
    )

    blocks = 9 * LANES + 10 * GRAD_ROWS
    chunk = -(-blocks // (core_count * group * 16)) * 16
    half_rows = max(group * chunk, -(-blocks // (2 * LANES)) * LANES)

    def body(*refs):
        main_kernel(
            *refs,
            lat_count=lat_count,
            coarse_cols=band_cols * lon_count,
            band_cols=band_cols,
        )

    hid, own_blend, lift_right, message = pl.pallas_call(
        body,
        out_specs=[vmem] * 4,
        out_shape=[
            jax.ShapeDtypeStruct((3, 2, pairs * cols, hidden), BF16),
            jax.ShapeDtypeStruct((cols, 3 * SPAN), BF16),
            jax.ShapeDtypeStruct((3 * SPAN, rows * hidden), BF16),
            jax.ShapeDtypeStruct((2, half_rows, LANES), BF16),
        ],
        scratch_shapes=[
            pltpu.VMEM(((reach - 2) * band_cols, 3 * hidden), F32),
            pltpu.VMEM((2 * pairs, wide, hidden), F32),
            pltpu.VMEM((9 * SPAN, 2 * pairs * hidden), BF16),
            pltpu.VMEM((wide, 2 * pairs * hidden), BF16),
            pltpu.VMEM((2, 2 * width, 4 * hidden), BF16),
        ],
        compiler_params=params,
        name="tile",
    )(
        got_far, got_near, *col_line,
        embed, near_w1, turned, bh, mixed, lifted, tap, cot_col, blend,
    )

    def half_features(first, *arrays):
        def body(*refs):
            features_kernel(*refs, first=first)

        return pl.pallas_call(
            body,
            out_shape=jax.ShapeDtypeStruct((rows // 2, cols, hidden), BF16),
            compiler_params=params,
            name=f"features_{first}",
        )(*arrays)

    swap = [(0, 1), (1, 0)]
    received = lax.ppermute(message[1], "core", swap)
    middle = rows // 4
    part = half_features(0, fore_weight, hid, own_blend, lift_right)
    received, part = lax.optimization_barrier((received, part))
    pair = (message[0].astype(F32) + received.astype(F32)).astype(BF16)
    axes = ("lat", "ring")
    chunk = half_rows // group
    parts = lax.all_to_all(pair, axes, 0, 0, tiled=True)
    copies = pl.pallas_call(
        reduce_kernel,
        out_shape=jax.ShapeDtypeStruct((group, chunk, LANES), BF16),
        compiler_params=params,
        name="sum_chunks",
    )(parts.reshape(group, chunk, LANES))
    mine = lax.all_to_all(copies.reshape(half_rows, LANES), axes, 0, 0, tiled=True)
    other = lax.ppermute(mine, "core", swap)
    last_part = half_features(middle, fore_weight, hid, own_blend, lift_right, mine)
    scale = 1.0 / math.sqrt(rows * lat_count * cols * lon_count)

    def finish(*refs):
        last_kernel(*refs, scale=scale)

    features, grad_embed, grad_first, grad_second = pl.pallas_call(
        finish,
        out_specs=[far] * 4,
        out_shape=[
            jax.ShapeDtypeStruct((rows, cols, hidden), BF16),
            jax.ShapeDtypeStruct((fields, hidden), F32),
            jax.ShapeDtypeStruct((9, hidden, hidden), F32),
            jax.ShapeDtypeStruct((9, hidden, hidden), F32),
        ],
        scratch_shapes=[
            pltpu.VMEM((2, half_rows, LANES), BF16),
            pltpu.VMEM((fields, hidden), F32),
            pltpu.VMEM((9, hidden, hidden), F32),
            pltpu.VMEM((9, hidden, hidden), F32),
            pltpu.SemaphoreType.DMA((9,)),
        ],
        compiler_params=params,
        name="finish",
    )(mine, other, embed, first_weight, part, last_part)
    shape = (3, 3, hidden, hidden)
    return (features, grad_embed, grad_first.reshape(shape), grad_second.reshape(shape))


def solution(mesh):
    lat_count, lon_count = mesh.devices.shape
    inner = jax.sharding.Mesh(
        mesh.devices.reshape(lat_count, lon_count // 2, 2), ("lat", "ring", "core")
    )
    lon = ("ring", "core")
    in_specs = (
        P(None, "lat", lon),
        P("lat"),
        P("lat"),
        P(lon),
        P(lon),
        P(),
        P(),
        P(),
        P("lat", lon, None),
    )
    out_specs = (P("lat", lon, None), P(), P(), P())
    return jax.shard_map(
        on_device, mesh=inner, in_specs=in_specs, out_specs=out_specs, check_vma=False
    )
```

```python
import math

import jax
import jax.numpy as jnp
from jax import lax
from jax.experimental import pallas as pl
from jax.experimental.pallas import tpu as pltpu
from jax.sharding import PartitionSpec as P

F32 = jnp.float32
BF16 = jnp.bfloat16
LANES = 128
ROW_HALO = 3
COL_HALO = 4
SPAN = 16
GRAD_ROWS = 80
VMEM_BYTES = 24 * 1024 * 1024


def split_two(value):
    high = value.astype(BF16)
    return high, (value - high.astype(F32)).astype(BF16)


def prepare_kernel(
    cot_hbm, w2_hbm, w1_hbm, embed_hbm,
    shift_ref, back_ref, fore_ref, turned_ref, first_ref, cot_ref, w1_ref, padded_ref,
    w2_ref, embed_ref, line_ref, sems
):
    rows, cols, _ = cot_ref.shape
    wide = cols + 16
    pairs = rows // 2 + 1
    chunks = sems.shape[0] - 3
    share = rows // chunks
    weight_copy = pltpu.make_async_copy(w2_hbm, w2_ref, sems.at[chunks])
    weight_copy.start()
    copies = []
    for n in range(chunks):
        part = pl.ds(n * share, share)
        copies.append(pltpu.make_async_copy(cot_hbm.at[part], cot_ref.at[part], sems.at[n]))
        copies[-1].start()
    other_copy = pltpu.make_async_copy(w1_hbm, w1_ref, sems.at[chunks + 1])
    other_copy.start()
    embed_copy = pltpu.make_async_copy(embed_hbm, embed_ref, sems.at[chunks + 2])
    embed_copy.start()
    line_ref[...] = jnp.zeros_like(line_ref)
    back_ref[...] = jnp.zeros_like(back_ref)
    fore_ref[...] = jnp.zeros_like(fore_ref)
    blank = jnp.zeros((wide, LANES), BF16)
    for b in range(3):
        for parity in range(2):
            shift_ref[b, parity, 0:wide] = blank
            shift_ref[b, parity, pairs * wide : (pairs + 1) * wide] = blank
    weight_copy.wait()
    for a in range(3):
        for b in range(3):
            straight = w2_ref[a * 3 + b]
            turned = straight.astype(F32).T.astype(BF16)
            for q in range(2):
                column = slice(q * LANES, (q + 1) * LANES)
                at = (b * 4 + 2 + q - a) * LANES
                back_ref[at : at + LANES, column] = turned
                at = (b * 4 + a + q) * LANES
                fore_ref[at : at + LANES, column] = straight
    for r in range(rows):
        slot = r % 4
        if r % share == 0:
            copies[r // share].wait()
        line = cot_ref[r].astype(F32)
        line_ref[slot, 8 : 8 + cols] = line
        start = (r // 2 + 1) * wide
        for b in range(3):
            shift_ref[b, r % 2, start : start + wide] = line_ref[slot, 8 - b : 8 - b + wide].astype(BF16)
        turned_ref[(r % 2) * LANES : (r % 2 + 1) * LANES, (r // 2) * cols : (r // 2 + 1) * cols] = line.T.astype(BF16)
    embed_copy.wait()
    padded_ref[...] = padded_embed(embed_ref, line_ref)
    other_copy.wait()
    for tap in range(9):
        first_ref[tap * LANES : (tap + 1) * LANES] = w1_ref[tap].astype(F32).T.astype(BF16)


def edge_line(block, at):
    index = block[at : at + 1]
    return index, block[at + 1 : at + 2] + block[at + 2 : at + 3] + block[at + 3 : at + 4]


def joined_line(first, own, last, width):
    lane_count = 2 * LANES
    lane = lax.broadcasted_iota(jnp.int32, (1, lane_count), 1)
    out = []
    for part, shift in zip((first, own, last), (lane_count - width + 2, 2, width + 2)):
        part = jnp.concatenate([part[:, :width], jnp.zeros((1, lane_count - width), F32)], axis=1)
        out.append(pltpu.roll(jnp.broadcast_to(part, (8, lane_count)), shift, 1)[:1])
    return jnp.where(lane < 2, out[0], jnp.where(lane < width + 2, out[1], out[2]))


def row_blend(rsrc_ref, rfrac_ref, before_ref, after_ref, lat, lat_count, band_rows):
    rows = rsrc_ref.shape[1]
    cells = 2 * COL_HALO
    before_line = edge_line(before_ref[ROW_HALO].astype(F32), 0)
    after_line = edge_line(after_ref[ROW_HALO].astype(F32), 0)
    own_line = (rsrc_ref[...].astype(F32), rfrac_ref[...])
    src, frac = (
        joined_line(*lines, rows) for lines in zip(before_line, own_line, after_line)
    )
    spot = (src - (lat * band_rows - ROW_HALO).astype(F32)) * cells
    shape = (cells, LANES)
    at = lax.broadcasted_iota(jnp.int32, shape, 1) - lax.broadcasted_iota(jnp.int32, shape, 0)
    at = at.astype(F32)
    parts = []
    for q in range(rows + 4):
        here = jnp.broadcast_to(spot[:, q : q + 1], shape)
        f = jnp.broadcast_to(frac[:, q : q + 1], shape)
        part = jnp.where(at == here, 1.0 - f, 0.0) + jnp.where(at == here + cells, f, 0.0)
        if q < 2:
            part = part * jnp.where(lat > 0, 1.0, 0.0)
        elif q >= rows + 2:
            part = part * jnp.where(lat < lat_count - 1, 1.0, 0.0)
        parts.append(part)
    return jnp.concatenate(list(split_two(jnp.concatenate(parts, axis=0))), axis=1)


def blend_rows(matrix, cells):
    fill = jnp.zeros((LANES - sum(c.shape[0] for c in cells), LANES), F32)
    column = jnp.concatenate(list(cells) + [fill], axis=0).astype(BF16)
    return jnp.dot(matrix, jnp.concatenate([column, column], axis=0), preferred_element_type=F32)


def stacked(value):
    one, two = split_two(value)
    return jnp.concatenate([one, one, two], axis=0)


def lift_rows(mixed, embed):
    pair = jnp.concatenate(list(split_two(mixed)), axis=1)
    return jnp.dot(pair, jnp.concatenate([embed, embed], axis=0), preferred_element_type=F32)


def turned_rows(mixed, width):
    fill = jnp.zeros((width - mixed.shape[0], LANES), F32)
    turned = jnp.concatenate([mixed, fill], axis=0).T[:GRAD_ROWS]
    step = 2 * COL_HALO
    lines = [turned] + [pltpu.roll(turned, width - a * step, 1) for a in (1, 2)]
    return split_two(jnp.concatenate(lines, axis=0))


def tap_rows(lifted, w1_ref, cells):
    count = lifted.shape[0] - 2 * cells
    pairs = [split_two(lifted[a * cells : a * cells + count]) for a in range(3)]
    left = jnp.concatenate([p[0] for p in pairs] + [p[1] for p in pairs], axis=1)
    lines = [jnp.concatenate([w1_ref[a * 3 + b] for b in range(3)], axis=1) for a in range(3)]
    return jnp.dot(left, jnp.concatenate(lines + lines, axis=0), preferred_element_type=F32)


def blend_cols(src, frac, lon, band_cols, coarse_cols):
    shape = (SPAN, src.shape[1])
    local = jnp.broadcast_to(src, shape) - lon * band_cols
    frac = jnp.broadcast_to(frac, shape)
    local = jnp.where(local < -COL_HALO, local + coarse_cols, local)
    local = jnp.where(local >= band_cols + COL_HALO, local - coarse_cols, local)
    line = lax.broadcasted_iota(jnp.int32, shape, 0)

    def spot(at):
        east = jnp.where(at >= band_cols, at + COL_HALO, at)
        return jnp.where(at < 0, at + band_cols + COL_HALO, east)

    return jnp.where(line == spot(local), 1.0 - frac, 0.0) + jnp.where(
        line == spot(local + 1), frac, 0.0
    )


def back_kernel(
    rsrc_ref,
    rfrac_ref,
    shift_ref,
    weight_ref,
    before_ref,
    own_ref,
    after_ref,
    csrc_ref,
    cfrac_ref,
    embed_ref,
    w1_ref,
    cot_ref,
    bh_ref,
    rows_ref,
    lifted_ref,
    tap_ref,
    cot_col_ref,
    blend_ref,
    *,
    lat_count,
    coarse_cols,
):
    rows, cols, _ = cot_ref.shape
    wide = bh_ref.shape[1]
    pairs = bh_ref.shape[0] // 2
    band_rows, band_cols = own_ref.shape[0] - 1, own_ref.shape[1]
    step = 6
    for first in range(0, pairs, step):
        count = min(step, pairs - first)
        blocks = []
        for b in range(3):
            for i in range(4):
                start = (first + i // 2) * wide
                blocks.append(shift_ref[b, i % 2, start : start + count * wide])
        out = jnp.dot(jnp.concatenate(blocks, axis=1), weight_ref[...], preferred_element_type=F32)
        for m in range(count):
            for q in range(2):
                bh_ref[2 * (first + m) + q] = out[m * wide : (m + 1) * wide, q * LANES : (q + 1) * LANES]

    lat = lax.axis_index("lat")
    lon = lax.axis_index("ring") * 2 + lax.axis_index("core")
    matrix = row_blend(rsrc_ref, rfrac_ref, before_ref, after_ref, lat, lat_count, band_rows)
    blend_ref[...] = matrix
    cells = [before_ref[j] for j in range(ROW_HALO)] + [own_ref[j] for j in range(band_rows)]
    cells += [after_ref[j] for j in range(ROW_HALO)]
    mixed = blend_rows(matrix, [c.astype(F32) for c in cells])
    rows_ref[0], rows_ref[1] = turned_rows(mixed, rows_ref.shape[2])
    lifted = lift_rows(mixed, embed_ref[...])
    lifted_ref[...] = lifted
    tap_ref[...] = tap_rows(lifted, w1_ref, band_cols)

    blend = blend_cols(csrc_ref[...], cfrac_ref[...], lon, band_cols, coarse_cols)
    own_t = jnp.concatenate(list(split_two(blend)), axis=0)
    every = jnp.concatenate([cot_ref[r] for r in range(rows)], axis=1)
    back = jnp.dot(own_t, every, preferred_element_type=F32)
    back = back[:SPAN] + back[SPAN:]
    for r in range(rows):
        cot_col_ref[r] = back[:, r * LANES : (r + 1) * LANES]


def pack_kernel(cells_hbm, rsrc_hbm, rfrac_hbm, csrc_hbm, cfrac_hbm, *space):
    sources = (cells_hbm, rsrc_hbm, rfrac_hbm, csrc_hbm, cfrac_hbm)
    own_ref, early_ref, outer_ref, late_ref, *lines, cells_ref, out_ref, sems = space
    targets = (cells_ref, *lines)
    copies = [
        pltpu.make_async_copy(source, target, sems.at[n])
        for n, (source, target) in enumerate(zip(sources, targets))
    ]
    for copy in copies:
        copy.start()
    cells_ref, rsrc_ref, rfrac_ref, csrc_ref, cfrac_ref = targets
    depth, span, fields = cells_ref.shape
    out_ref[...] = jnp.zeros_like(out_ref)
    for copy in copies:
        copy.wait()
    for j in range(depth):
        out_ref[j, :, :fields] = cells_ref[j].astype(F32)
    at = 0
    for index_ref, fraction_ref in ((rsrc_ref, rfrac_ref), (csrc_ref, cfrac_ref)):
        width = index_ref.shape[1]
        fraction = fraction_ref[...]
        one = fraction.astype(BF16).astype(F32)
        two = (fraction - one).astype(BF16).astype(F32)
        for value in (index_ref[...].astype(F32), one, two, fraction - one - two):
            out_ref[depth, at : at + 1, :width] = value
            at += 1
    lat = lax.axis_index("lat")
    even = lax.rem(lat, 2) == 0
    own = [out_ref[j] for j in range(depth + 1)]
    to_next = own[depth - ROW_HALO :]
    to_last = own[:ROW_HALO] + own[depth:]
    for j in range(depth + 1):
        own_ref[j] = own[j].astype(BF16)
    for j in range(ROW_HALO + 1):
        inner = jnp.where(even, to_next[j], to_last[j]).astype(BF16)
        early_ref[j] = inner
        outer_ref[j] = jnp.where(even, to_last[j], to_next[j]).astype(BF16)
        late_ref[j] = inner


def main_kernel(
    far_ref,
    near_ref,
    csrc_ref,
    cfrac_ref,
    embed_ref,
    w1_ref,
    turned_ref,
    bh_ref,
    rows_ref,
    tap_ref,
    cot_col_ref,
    blend_ref,
    hid_ref,
    own_ref,
    side_lifted_ref,
    msg_ref,
    side_tap_ref,
    line_ref,
    right_ref,
    delta_ref,
    back_ref,
    *,
    lat_count,
    coarse_cols,
    band_cols,
):
    rows, cols = cot_col_ref.shape[0], own_ref.shape[0]
    wide = bh_ref.shape[1]
    pairs = bh_ref.shape[0] // 2
    depth = 2 * (far_ref.shape[0] - 1)
    half_rows = msg_ref.shape[1]
    lat = lax.axis_index("lat")
    core = lax.axis_index("core")
    lon = lax.axis_index("ring") * 2 + core
    taps = 3 * SPAN

    def send(at, value):
        side = lax.rem(at // half_rows + core, 2)
        at = at % half_rows
        msg_ref[side, at : at + value.shape[0]] = value.astype(BF16)

    sides = []
    for j in range(depth // 2 + 1):
        far, near = far_ref[j].astype(F32), near_ref[j].astype(F32)
        sides.append((jnp.where(core == 1, near, far), jnp.where(core == 1, far, near)))
    cells = []
    for j in range(depth):
        part = slice(j % 2 * COL_HALO, (j % 2 + 1) * COL_HALO)
        cells += [v[part] for v in sides[j // 2]]
    side_mixed = blend_rows(blend_ref[...], cells)
    side_lifted = lift_rows(side_mixed, embed_ref[...])
    side_lifted_ref[...] = side_lifted
    side_tap_ref[...] = tap_rows(side_lifted, w1_ref, band_cols)

    lane_count = 2 * LANES
    lane = lax.broadcasted_iota(jnp.int32, (1, lane_count), 1)
    west_line, east_line = (edge_line(v, 4) for v in sides[depth // 2])
    own_line = (csrc_ref[...].astype(F32), cfrac_ref[...])
    lines = [joined_line(*v, cols) for v in zip(west_line, own_line, east_line)]
    known = lane < cols + 4
    src = jnp.where(known, lines[0], -1e6).astype(jnp.int32)
    blend = blend_cols(src, jnp.where(known, lines[1], 0.0), lon, band_cols, coarse_cols)
    rolled = [blend] + [pltpu.roll(blend, lane_count - b, 1) for b in (1, 2)]
    stack = jnp.concatenate(rolled, axis=0)[:, :wide]
    high, low = split_two(stack)
    high_f, low_f = high.astype(F32), low.astype(F32)
    col_t = jnp.concatenate([high_f, low_f], axis=0).astype(BF16)
    col_lhs = jnp.concatenate([high_f.T, low_f.T, high_f.T], axis=1).astype(BF16)
    own_hi, own_lo = split_two(rolled[2][:, :cols])
    own_hi, own_lo = own_hi.astype(F32).T, own_lo.astype(F32).T
    own_ref[...] = jnp.concatenate([own_hi, own_lo, own_hi], axis=1).astype(BF16)

    for t in range(2 * pairs):
        part = slice(t * band_cols, (t + 1) * band_cols)
        blocks = []
        for b in range(3):
            column = slice(b * LANES, (b + 1) * LANES)
            blocks += [tap_ref[part, column], side_tap_ref[part, column]]
        right_ref[:, t * LANES : (t + 1) * LANES] = stacked(jnp.concatenate(blocks, axis=0))
    half = rows // 2 + 2
    spans = ((0, half), (half, 2 * pairs))
    cells_half = rows // 4 * cols

    def first_product(n):
        span = slice(spans[n][0] * LANES, spans[n][1] * LANES)
        return jnp.dot(col_lhs, right_ref[:, span], preferred_element_type=F32)

    def activate(pre, first, t):
        v = pre[:, (t - first) * LANES : (t - first + 1) * LANES]
        s = 0.5 + 0.5 * jnp.tanh(0.5 * v)
        if t == 0:
            s = s * jnp.where(lat > 0, 1.0, 0.0)
        elif t == 2 * pairs - 1:
            s = s * jnp.where(lat < lat_count - 1, 1.0, 0.0)
        h = v * s
        slope = s + h * (1.0 - s)
        line_ref[t] = h
        delta_ref[:, t * LANES : (t + 1) * LANES] = (bh_ref[t] * slope).astype(BF16)

    def place_hidden(t):
        at = (t // 2) * cols
        for b in range(3):
            hid_ref[b, t % 2, at : at + cols] = line_ref[t, b : b + cols].astype(BF16)

    def second_gradient(n, b):
        right = []
        for i in range(4):
            start = (i // 2) * cols + n * cells_half
            right.append(hid_ref[b, i % 2, start : start + cells_half])
        left = turned_ref[:, n * cells_half : (n + 1) * cells_half]
        return jnp.dot(left, jnp.concatenate(right, axis=1), preferred_element_type=F32)

    pre = first_product(0)
    for t in range(*spans[0]):
        activate(pre, 0, t)
    pre = first_product(1)
    for t in range(*spans[0]):
        place_hidden(t)
    grads = []
    rest = list(range(*spans[1]))
    share = -(-len(rest) // 3)
    for b in range(3):
        grads.append(second_gradient(0, b))
        for t in rest[b * share : (b + 1) * share]:
            activate(pre, spans[1][0], t)
            place_hidden(t)
    back = jnp.dot(col_t, delta_ref[...], preferred_element_type=F32)
    back = back[:taps] + back[taps:]
    for b in range(3):
        grads[b] = grads[b] + second_gradient(1, b)

    width = rows_ref.shape[2]
    used = 2 * pairs * band_cols
    blank = jnp.zeros((2, width - used, back_ref.shape[2]), BF16)
    back_ref[:, used:width] = blank
    back_ref[:, width + used :] = blank
    nothing = jnp.zeros((SPAN, LANES), F32)
    for p in range(pairs):
        for b in range(4):
            lines = []
            for t in (2 * p, 2 * p + 1):
                if b < 3:
                    lines.append(back[b * SPAN : (b + 1) * SPAN, t * LANES : (t + 1) * LANES])
                else:
                    lines.append(cot_col_ref[t - 1] if 1 <= t <= rows else nothing)
            column = slice(b * LANES, (b + 1) * LANES)
            for side in range(2):
                cells = slice(side * band_cols, (side + 1) * band_cols)
                one, two = split_two(jnp.concatenate([v[cells] for v in lines], axis=0))
                at = side * width + p * SPAN
                back_ref[0, at : at + SPAN, column] = one
                back_ref[1, at : at + SPAN, column] = two
    side_hi, side_lo = turned_rows(side_mixed, width)
    upper = jnp.concatenate([rows_ref[0], side_hi], axis=1)
    lower = jnp.concatenate([rows_ref[1], side_lo], axis=1)
    g = jnp.dot(jnp.concatenate([upper, lower], axis=0), back_ref[0], preferred_element_type=F32)
    g = g[: 3 * GRAD_ROWS] + g[3 * GRAD_ROWS :]
    g = g + jnp.dot(upper, back_ref[1], preferred_element_type=F32)
    for a in range(3):
        line = g[a * GRAD_ROWS : (a + 1) * GRAD_ROWS]
        for b in range(3):
            send(9 * LANES + (a * 3 + b) * GRAD_ROWS, line[:, b * LANES : (b + 1) * LANES])
    send(9 * LANES + 9 * GRAD_ROWS, g[GRAD_ROWS : 2 * GRAD_ROWS, 3 * LANES:])
    tail = 9 * LANES + 10 * GRAD_ROWS
    if 2 * half_rows > tail:
        send(tail, jnp.zeros((2 * half_rows - tail, LANES), F32))

    for b in range(3):
        for a in range(3):
            upper = grads[b][:LANES, a * LANES : (a + 1) * LANES]
            lower = grads[b][LANES:, (a + 1) * LANES : (a + 2) * LANES]
            send((a * 3 + b) * LANES, (upper + lower).T)


def join_kernel(own_ref, early_ref, outer_ref, late_ref, ready_ref, before_ref, after_ref, far_ref, near_ref):
    band_rows, band_cols = own_ref.shape[0] - 1, own_ref.shape[1]
    lat = lax.axis_index("lat")
    even = lax.rem(lat, 2) == 0
    sent_late = lax.rem(lat + lat // 2, 2) == 0
    first = lax.axis_index("core") == 0
    outer = [outer_ref[j].astype(F32) for j in range(ROW_HALO + 1)]
    inner = [
        jnp.where(sent_late, late_ref[j].astype(F32), early_ref[j].astype(F32))
        for j in range(ROW_HALO + 1)
    ]
    before = [jnp.where(even, v, w) for v, w in zip(outer, inner)]
    after = [jnp.where(even, w, v) for v, w in zip(outer, inner)]
    own = [own_ref[j].astype(F32) for j in range(band_rows + 1)]
    for j in range(ROW_HALO + 1):
        before_ref[j] = before[j].astype(BF16)
        after_ref[j] = after[j].astype(BF16)
    tall = before[:ROW_HALO] + own[:band_rows] + after[:ROW_HALO]
    for j in range(0, len(tall), 2):
        to_last = jnp.concatenate([v[:COL_HALO] for v in tall[j : j + 2]], axis=0)
        to_next = jnp.concatenate([v[band_cols - COL_HALO :] for v in tall[j : j + 2]], axis=0)
        far_ref[j // 2] = jnp.where(first, to_last, to_next).astype(BF16)
        near_ref[j // 2] = jnp.where(first, to_next, to_last).astype(BF16)
    far_ref[len(tall) // 2] = own[band_rows].astype(BF16)
    near_ref[len(tall) // 2] = own[band_rows].astype(BF16)


def features_kernel(weight_ref, hid_ref, own_ref, lifted_ref, side_lifted_ref, *refs, first):
    feat_ref = refs[-1]
    rows, cols, _ = feat_ref.shape
    cells = own_ref.shape[1] // 6
    step = 4
    for n in range(0, rows // 2, step):
        top = first + n
        blocks = []
        for b in range(3):
            for i in range(4):
                start = (top + i // 2) * cols
                blocks.append(hid_ref[b, i % 2, start : start + step * cols])
        out = jnp.dot(jnp.concatenate(blocks, axis=1), weight_ref[...], preferred_element_type=F32)
        right = []
        for r in range(2 * top, 2 * (top + step)):
            part = slice((r + 2) * cells, (r + 3) * cells)
            right.append(stacked(jnp.concatenate([lifted_ref[part], side_lifted_ref[part]], axis=0)))
        lift = jnp.dot(own_ref[...], jnp.concatenate(right, axis=1), preferred_element_type=F32)
        for m in range(step):
            for q in range(2):
                piece = out[m * cols : (m + 1) * cols, q * LANES : (q + 1) * LANES]
                own = lift[:, (2 * m + q) * LANES : (2 * m + q + 1) * LANES]
                feat_ref[2 * (n + m) + q] = (own + piece).astype(BF16)


def reduce_kernel(in_ref, out_ref):
    total = in_ref[0].astype(F32)
    for d in range(1, in_ref.shape[0]):
        total = total + in_ref[d].astype(F32)
    total = total.astype(BF16)
    for d in range(out_ref.shape[0]):
        out_ref[d] = total


def padded_embed(embed_ref, space_ref):
    fields = embed_ref.shape[0]
    space_ref[0, :LANES] = jnp.zeros((LANES, LANES), F32)
    space_ref[0, :fields] = embed_ref[...].astype(F32)
    return space_ref[0, :LANES].astype(BF16)


def last_kernel(
    mine_ref, other_ref, embed_ref, first_ref, upper_ref, lower_ref, feat_hbm, ge_hbm, g1_hbm, g2_hbm,
    sum_ref, ge_ref, g1_ref, g2_ref, sems, *, scale
):
    core = lax.axis_index("core")
    half_rows = mine_ref.shape[0]
    copies = []

    def leave(source, target):
        copies.append(pltpu.make_async_copy(source, target, sems.at[len(copies)]))
        copies[-1].start()

    count = upper_ref.shape[0]
    leave(upper_ref, feat_hbm.at[pl.ds(0, count)])
    leave(lower_ref, feat_hbm.at[pl.ds(count, count)])
    sum_ref[core] = mine_ref[...]
    sum_ref[1 - core] = other_ref[...]

    def read(at, count):
        return sum_ref[at // half_rows, at % half_rows : at % half_rows + count]

    for a in range(3):
        for tap in range(3 * a, 3 * a + 3):
            g2_ref[tap] = read(tap * LANES, LANES).astype(F32) * scale
        leave(g2_ref.at[pl.ds(3 * a, 3)], g2_hbm.at[pl.ds(3 * a, 3)])
    embed_t = embed_ref[...].astype(F32).T.astype(BF16)[:, :GRAD_ROWS]
    base = 9 * LANES
    g = jnp.concatenate([read(base + tap * GRAD_ROWS, GRAD_ROWS) for tap in range(9)], axis=1)
    for a in range(3):
        part = g[:, 3 * a * LANES : (3 * a + 3) * LANES]
        out = jnp.dot(embed_t, part, preferred_element_type=F32) * scale
        for b in range(3):
            g1_ref[3 * a + b] = out[:, b * LANES : (b + 1) * LANES]
        leave(g1_ref.at[pl.ds(3 * a, 3)], g1_hbm.at[pl.ds(3 * a, 3)])
    lift = read(base + 9 * GRAD_ROWS, GRAD_ROWS).astype(F32)
    lift = lift + jnp.dot(g, first_ref[...], preferred_element_type=F32)
    ge_ref[...] = lift[: ge_ref.shape[0]] * scale
    leave(ge_ref, ge_hbm)
    for copy in copies:
        copy.wait()


def from_hbm(value):
    return pltpu.with_memory_space_constraint(value, pltpu.HBM)


def on_device(
    coarse,
    row_src,
    row_frac,
    col_src,
    col_frac,
    embed_weight,
    conv1_weight,
    conv2_weight,
    cotangent,
):
    lat_count = lax.axis_size("lat")
    ring_count = lax.axis_size("ring")
    core_count = lax.axis_size("core")
    lon_count = ring_count * core_count
    fields, band_rows, band_cols = coarse.shape
    rows, cols, hidden = cotangent.shape
    group = lat_count * ring_count
    wide = cols + 16
    pairs = rows // 2 + 1
    depth = band_rows + 2 * ROW_HALO
    params = pltpu.CompilerParams(vmem_limit_bytes=VMEM_BYTES)
    vmem = pl.BlockSpec(memory_space=pltpu.VMEM)
    far = pl.BlockSpec(memory_space=pltpu.HBM)

    w1 = conv1_weight.reshape(9, hidden, hidden)
    w2 = conv2_weight.reshape(9, hidden, hidden)
    row_line = (row_src.reshape(1, rows), row_frac.reshape(1, rows))
    col_line = (col_src.reshape(1, cols), col_frac.reshape(1, cols))

    pack_inputs = (
        jnp.transpose(coarse, (1, 2, 0)),
        *row_line,
        *col_line,
    )
    own, to_early, to_outer, to_late, *lines = pl.pallas_call(
        pack_kernel,
        in_specs=[far] * 5,
        out_shape=[jax.ShapeDtypeStruct((band_rows + 1, band_cols, LANES), BF16)]
        + [jax.ShapeDtypeStruct((ROW_HALO + 1, band_cols, LANES), BF16)] * 3
        + [jax.ShapeDtypeStruct(x.shape, x.dtype) for x in pack_inputs[1:]],
        scratch_shapes=[
            pltpu.VMEM(pack_inputs[0].shape, BF16),
            pltpu.VMEM((band_rows + 1, band_cols, LANES), F32),
            pltpu.SemaphoreType.DMA((5,)),
        ],
        compiler_params=params,
        name="pack",
    )(*(from_hbm(x) for x in pack_inputs))
    row_line, col_line = lines[:2], lines[2:]
    early = [(i, i ^ 1) for i in range(lat_count) if (i + i // 2) % 2 == 0]
    late = [(j, i) for i, j in early]
    outer = [(i, i + 1) for i in range(1, lat_count - 1, 2)]
    outer = outer + [(j, i) for i, j in outer]
    got_early = lax.ppermute(to_early, "lat", early)
    got_outer = lax.ppermute(to_outer, "lat", outer)
    got_late = lax.ppermute(to_late, "lat", late)

    shift, back_weight, fore_weight, turned, first_weight, cot, near_w1, embed = pl.pallas_call(
        prepare_kernel,
        out_shape=[
            jax.ShapeDtypeStruct((3, 2, (pairs + 1) * wide, hidden), BF16),
            jax.ShapeDtypeStruct((12 * hidden, 2 * hidden), BF16),
            jax.ShapeDtypeStruct((12 * hidden, 2 * hidden), BF16),
            jax.ShapeDtypeStruct((2 * hidden, rows // 2 * cols), BF16),
            jax.ShapeDtypeStruct((9 * hidden, hidden), BF16),
            jax.ShapeDtypeStruct((rows, cols, hidden), BF16),
            jax.ShapeDtypeStruct((9, hidden, hidden), BF16),
            jax.ShapeDtypeStruct((LANES, hidden), BF16),
        ],
        in_specs=[far] * 4,
        scratch_shapes=[
            pltpu.VMEM((9, hidden, hidden), BF16),
            pltpu.VMEM((fields, hidden), BF16),
            pltpu.VMEM((4, wide + 16, hidden), F32),
            pltpu.SemaphoreType.DMA((11,)),
        ],
        compiler_params=params,
        name="prepare",
    )(from_hbm(cotangent), from_hbm(w2), from_hbm(w1), from_hbm(embed_weight))
    before, after, far_message, near_message = pl.pallas_call(
        join_kernel,
        out_shape=[jax.ShapeDtypeStruct((ROW_HALO + 1, band_cols, LANES), BF16)] * 2
        + [jax.ShapeDtypeStruct((depth // 2 + 1, band_cols, LANES), BF16)] * 2,
        compiler_params=params,
        name="join",
    )(own, got_early, got_outer, got_late, embed)
    lon = ("ring", "core")
    inner = [(i, i ^ 1) for i in range(lon_count)]
    outer = [(i, (i + (1 if i % 2 else -1)) % lon_count) for i in range(lon_count)]
    got_far = lax.ppermute(far_message, lon, outer)
    got_near = lax.ppermute(near_message, lon, inner)

    def back_body(*refs):
        back_kernel(*refs, lat_count=lat_count, coarse_cols=band_cols * lon_count)

    reach = rows + 4
    width = -(-reach * band_cols // LANES) * LANES
    bh, mixed, lifted, tap, cot_col, blend = pl.pallas_call(
        back_body,
        out_shape=[
            jax.ShapeDtypeStruct((2 * pairs, wide, hidden), F32),
            jax.ShapeDtypeStruct((2, 3 * GRAD_ROWS, width), BF16),
            jax.ShapeDtypeStruct((reach * band_cols, hidden), F32),
            jax.ShapeDtypeStruct(((reach - 2) * band_cols, 3 * hidden), F32),
            jax.ShapeDtypeStruct((rows, SPAN, hidden), F32),
            jax.ShapeDtypeStruct((reach * band_cols, 2 * LANES), BF16),
        ],
        compiler_params=params,
        name="back_hidden",
    )(
        *row_line, shift, back_weight, before, own, after, *col_line,
        embed, near_w1, cot,
    )

    blocks = 9 * LANES + 10 * GRAD_ROWS
    chunk = -(-blocks // (core_count * group * 16)) * 16
    half_rows = max(group * chunk, -(-blocks // (2 * LANES)) * LANES)

    def body(*refs):
        main_kernel(
            *refs,
            lat_count=lat_count,
            coarse_cols=band_cols * lon_count,
            band_cols=band_cols,
        )

    hid, own_blend, side_lifted, message = pl.pallas_call(
        body,
        out_specs=[vmem] * 4,
        out_shape=[
            jax.ShapeDtypeStruct((3, 2, pairs * cols, hidden), BF16),
            jax.ShapeDtypeStruct((cols, 3 * SPAN), BF16),
            jax.ShapeDtypeStruct((reach * band_cols, hidden), F32),
            jax.ShapeDtypeStruct((2, half_rows, LANES), BF16),
        ],
        scratch_shapes=[
            pltpu.VMEM(((reach - 2) * band_cols, 3 * hidden), F32),
            pltpu.VMEM((2 * pairs, wide, hidden), F32),
            pltpu.VMEM((9 * SPAN, 2 * pairs * hidden), BF16),
            pltpu.VMEM((wide, 2 * pairs * hidden), BF16),
            pltpu.VMEM((2, 2 * width, 4 * hidden), BF16),
        ],
        compiler_params=params,
        name="tile",
    )(
        got_far, got_near, *col_line,
        embed, near_w1, turned, bh, mixed, tap, cot_col, blend,
    )

    def half_features(first, *arrays):
        def body(*refs):
            features_kernel(*refs, first=first)

        return pl.pallas_call(
            body,
            out_shape=jax.ShapeDtypeStruct((rows // 2, cols, hidden), BF16),
            compiler_params=params,
            name=f"features_{first}",
        )(*arrays)

    swap = [(0, 1), (1, 0)]
    received = lax.ppermute(message[1], "core", swap)
    middle = rows // 4
    part = half_features(0, fore_weight, hid, own_blend, lifted, side_lifted)
    received, part = lax.optimization_barrier((received, part))
    pair = (message[0].astype(F32) + received.astype(F32)).astype(BF16)
    axes = ("lat", "ring")
    chunk = half_rows // group
    parts = lax.all_to_all(pair, axes, 0, 0, tiled=True)
    copies = pl.pallas_call(
        reduce_kernel,
        out_shape=jax.ShapeDtypeStruct((group, chunk, LANES), BF16),
        compiler_params=params,
        name="sum_chunks",
    )(parts.reshape(group, chunk, LANES))
    mine = lax.all_to_all(copies.reshape(half_rows, LANES), axes, 0, 0, tiled=True)
    other = lax.ppermute(mine, "core", swap)
    last_part = half_features(middle, fore_weight, hid, own_blend, lifted, side_lifted, mine)
    scale = 1.0 / math.sqrt(rows * lat_count * cols * lon_count)

    def finish(*refs):
        last_kernel(*refs, scale=scale)

    features, grad_embed, grad_first, grad_second = pl.pallas_call(
        finish,
        out_specs=[far] * 4,
        out_shape=[
            jax.ShapeDtypeStruct((rows, cols, hidden), BF16),
            jax.ShapeDtypeStruct((fields, hidden), F32),
            jax.ShapeDtypeStruct((9, hidden, hidden), F32),
            jax.ShapeDtypeStruct((9, hidden, hidden), F32),
        ],
        scratch_shapes=[
            pltpu.VMEM((2, half_rows, LANES), BF16),
            pltpu.VMEM((fields, hidden), F32),
            pltpu.VMEM((9, hidden, hidden), F32),
            pltpu.VMEM((9, hidden, hidden), F32),
            pltpu.SemaphoreType.DMA((9,)),
        ],
        compiler_params=params,
        name="finish",
    )(mine, other, embed, first_weight, part, last_part)
    shape = (3, 3, hidden, hidden)
    return (features, grad_embed, grad_first.reshape(shape), grad_second.reshape(shape))


def solution(mesh):
    lat_count, lon_count = mesh.devices.shape
    inner = jax.sharding.Mesh(
        mesh.devices.reshape(lat_count, lon_count // 2, 2), ("lat", "ring", "core")
    )
    lon = ("ring", "core")
    in_specs = (
        P(None, "lat", lon),
        P("lat"),
        P("lat"),
        P(lon),
        P(lon),
        P(),
        P(),
        P(),
        P("lat", lon, None),
    )
    out_specs = (P("lat", lon, None), P(), P(), P())
    return jax.shard_map(
        on_device, mesh=inner, in_specs=in_specs, out_specs=out_specs, check_vma=False
    )
```

```python
import math

import jax
import jax.numpy as jnp
from jax import lax
from jax.experimental import pallas as pl
from jax.experimental.pallas import tpu as pltpu
from jax.sharding import PartitionSpec as P

F32 = jnp.float32
BF16 = jnp.bfloat16
LANES = 128
ROW_HALO = 3
COL_HALO = 4
SPAN = 16
GRAD_ROWS = 80
VMEM_BYTES = 24 * 1024 * 1024


def split_two(value):
    high = value.astype(BF16)
    return high, (value - high.astype(F32)).astype(BF16)


def prepare_kernel(
    cot_hbm, w2_hbm, w1_hbm, embed_hbm,
    shift_ref, back_ref, fore_ref, turned_ref, first_ref, cot_ref, w1_ref, padded_ref,
    w2_ref, embed_ref, line_ref, sems
):
    rows, cols, _ = cot_ref.shape
    wide = cols + 16
    pairs = rows // 2 + 1
    chunks = sems.shape[0] - 3
    share = rows // chunks
    weight_copy = pltpu.make_async_copy(w2_hbm, w2_ref, sems.at[chunks])
    weight_copy.start()
    copies = []
    for n in range(chunks):
        part = pl.ds(n * share, share)
        copies.append(pltpu.make_async_copy(cot_hbm.at[part], cot_ref.at[part], sems.at[n]))
        copies[-1].start()
    other_copy = pltpu.make_async_copy(w1_hbm, w1_ref, sems.at[chunks + 1])
    other_copy.start()
    embed_copy = pltpu.make_async_copy(embed_hbm, embed_ref, sems.at[chunks + 2])
    embed_copy.start()
    line_ref[...] = jnp.zeros_like(line_ref)
    back_ref[...] = jnp.zeros_like(back_ref)
    fore_ref[...] = jnp.zeros_like(fore_ref)
    blank = jnp.zeros((wide, LANES), BF16)
    for b in range(3):
        for parity in range(2):
            shift_ref[b, parity, 0:wide] = blank
            shift_ref[b, parity, pairs * wide : (pairs + 1) * wide] = blank
    weight_copy.wait()
    for a in range(3):
        for b in range(3):
            straight = w2_ref[a * 3 + b]
            turned = straight.astype(F32).T.astype(BF16)
            for q in range(2):
                column = slice(q * LANES, (q + 1) * LANES)
                at = (b * 4 + 2 + q - a) * LANES
                back_ref[at : at + LANES, column] = turned
                at = (b * 4 + a + q) * LANES
                fore_ref[at : at + LANES, column] = straight
    for r in range(rows):
        slot = r % 4
        if r % share == 0:
            copies[r // share].wait()
        line = cot_ref[r].astype(F32)
        line_ref[slot, 8 : 8 + cols] = line
        start = (r // 2 + 1) * wide
        for b in range(3):
            shift_ref[b, r % 2, start : start + wide] = line_ref[slot, 8 - b : 8 - b + wide].astype(BF16)
        turned_ref[(r % 2) * LANES : (r % 2 + 1) * LANES, (r // 2) * cols : (r // 2 + 1) * cols] = line.T.astype(BF16)
    embed_copy.wait()
    padded_ref[...] = padded_embed(embed_ref, line_ref)
    other_copy.wait()
    for tap in range(9):
        first_ref[tap * LANES : (tap + 1) * LANES] = w1_ref[tap].astype(F32).T.astype(BF16)


def edge_line(block, at):
    index = block[at : at + 1]
    return index, block[at + 1 : at + 2] + block[at + 2 : at + 3] + block[at + 3 : at + 4]


def joined_line(first, own, last, width):
    lane_count = 2 * LANES
    lane = lax.broadcasted_iota(jnp.int32, (1, lane_count), 1)
    out = []
    for part, shift in zip((first, own, last), (lane_count - width + 2, 2, width + 2)):
        part = jnp.concatenate([part[:, :width], jnp.zeros((1, lane_count - width), F32)], axis=1)
        out.append(pltpu.roll(jnp.broadcast_to(part, (8, lane_count)), shift, 1)[:1])
    return jnp.where(lane < 2, out[0], jnp.where(lane < width + 2, out[1], out[2]))


def row_blend(rsrc_ref, rfrac_ref, before_ref, after_ref, lat, lat_count, band_rows):
    rows = rsrc_ref.shape[1]
    cells = 2 * COL_HALO
    before_line = edge_line(before_ref[ROW_HALO].astype(F32), 0)
    after_line = edge_line(after_ref[ROW_HALO].astype(F32), 0)
    own_line = (rsrc_ref[...].astype(F32), rfrac_ref[...])
    src, frac = (
        joined_line(*lines, rows) for lines in zip(before_line, own_line, after_line)
    )
    spot = (src - (lat * band_rows - ROW_HALO).astype(F32)) * cells
    shape = (cells, LANES)
    at = lax.broadcasted_iota(jnp.int32, shape, 1) - lax.broadcasted_iota(jnp.int32, shape, 0)
    at = at.astype(F32)
    parts = []
    for q in range(rows + 4):
        here = jnp.broadcast_to(spot[:, q : q + 1], shape)
        f = jnp.broadcast_to(frac[:, q : q + 1], shape)
        part = jnp.where(at == here, 1.0 - f, 0.0) + jnp.where(at == here + cells, f, 0.0)
        if q < 2:
            part = part * jnp.where(lat > 0, 1.0, 0.0)
        elif q >= rows + 2:
            part = part * jnp.where(lat < lat_count - 1, 1.0, 0.0)
        parts.append(part)
    return jnp.concatenate(list(split_two(jnp.concatenate(parts, axis=0))), axis=1)


def blend_rows(matrix, cells):
    fill = jnp.zeros((LANES - sum(c.shape[0] for c in cells), LANES), F32)
    column = jnp.concatenate(list(cells) + [fill], axis=0).astype(BF16)
    return jnp.dot(matrix, jnp.concatenate([column, column], axis=0), preferred_element_type=F32)


def stacked(value):
    one, two = split_two(value)
    return jnp.concatenate([one, one, two], axis=0)


def lift_rows(mixed, embed):
    pair = jnp.concatenate(list(split_two(mixed)), axis=1)
    return jnp.dot(pair, jnp.concatenate([embed, embed], axis=0), preferred_element_type=F32)


def turned_rows(mixed, width):
    fill = jnp.zeros((width - mixed.shape[0], LANES), F32)
    turned = jnp.concatenate([mixed, fill], axis=0).T[:GRAD_ROWS]
    step = 2 * COL_HALO
    lines = [turned] + [pltpu.roll(turned, width - a * step, 1) for a in (1, 2)]
    return split_two(jnp.concatenate(lines, axis=0))


def tap_rows(lifted, w1_ref, cells):
    count = lifted.shape[0] - 2 * cells
    pairs = [split_two(lifted[a * cells : a * cells + count]) for a in range(3)]
    left = jnp.concatenate([p[0] for p in pairs] + [p[1] for p in pairs], axis=1)
    lines = [jnp.concatenate([w1_ref[a * 3 + b] for b in range(3)], axis=1) for a in range(3)]
    return jnp.dot(left, jnp.concatenate(lines + lines, axis=0), preferred_element_type=F32)


def blend_cols(src, frac, lon, band_cols, coarse_cols):
    shape = (SPAN, src.shape[1])
    local = jnp.broadcast_to(src, shape) - lon * band_cols
    frac = jnp.broadcast_to(frac, shape)
    local = jnp.where(local < -COL_HALO, local + coarse_cols, local)
    local = jnp.where(local >= band_cols + COL_HALO, local - coarse_cols, local)
    line = lax.broadcasted_iota(jnp.int32, shape, 0)

    def spot(at):
        east = jnp.where(at >= band_cols, at + COL_HALO, at)
        return jnp.where(at < 0, at + band_cols + COL_HALO, east)

    return jnp.where(line == spot(local), 1.0 - frac, 0.0) + jnp.where(
        line == spot(local + 1), frac, 0.0
    )


def back_kernel(
    rsrc_ref,
    rfrac_ref,
    shift_ref,
    weight_ref,
    before_ref,
    own_ref,
    after_ref,
    csrc_ref,
    cfrac_ref,
    embed_ref,
    w1_ref,
    cot_ref,
    bh_ref,
    rows_ref,
    lifted_ref,
    tap_ref,
    cot_col_ref,
    blend_ref,
    *,
    lat_count,
    coarse_cols,
):
    rows, cols, _ = cot_ref.shape
    wide = bh_ref.shape[1]
    pairs = bh_ref.shape[0] // 2
    band_rows, band_cols = own_ref.shape[0] - 1, own_ref.shape[1]
    step = 6
    for first in range(0, pairs, step):
        count = min(step, pairs - first)
        blocks = []
        for b in range(3):
            for i in range(4):
                start = (first + i // 2) * wide
                blocks.append(shift_ref[b, i % 2, start : start + count * wide])
        out = jnp.dot(jnp.concatenate(blocks, axis=1), weight_ref[...], preferred_element_type=F32)
        for m in range(count):
            for q in range(2):
                bh_ref[2 * (first + m) + q] = out[m * wide : (m + 1) * wide, q * LANES : (q + 1) * LANES]

    lat = lax.axis_index("lat")
    lon = lax.axis_index("ring") * 2 + lax.axis_index("core")
    matrix = row_blend(rsrc_ref, rfrac_ref, before_ref, after_ref, lat, lat_count, band_rows)
    blend_ref[...] = matrix
    cells = [before_ref[j] for j in range(ROW_HALO)] + [own_ref[j] for j in range(band_rows)]
    cells += [after_ref[j] for j in range(ROW_HALO)]
    mixed = blend_rows(matrix, [c.astype(F32) for c in cells])
    rows_ref[0], rows_ref[1] = turned_rows(mixed, rows_ref.shape[2])
    lifted = lift_rows(mixed, embed_ref[...])
    lifted_ref[...] = lifted
    tap_ref[...] = tap_rows(lifted, w1_ref, band_cols)

    blend = blend_cols(csrc_ref[...], cfrac_ref[...], lon, band_cols, coarse_cols)
    own_t = jnp.concatenate(list(split_two(blend)), axis=0)
    every = jnp.concatenate([cot_ref[r] for r in range(rows)], axis=1)
    back = jnp.dot(own_t, every, preferred_element_type=F32)
    back = back[:SPAN] + back[SPAN:]
    for r in range(rows):
        cot_col_ref[r] = back[:, r * LANES : (r + 1) * LANES]


def pack_kernel(cells_hbm, rsrc_hbm, rfrac_hbm, csrc_hbm, cfrac_hbm, *space):
    sources = (cells_hbm, rsrc_hbm, rfrac_hbm, csrc_hbm, cfrac_hbm)
    own_ref, outer_ref, inner_ref, *lines, cells_ref, out_ref, sems = space
    targets = (cells_ref, *lines)
    copies = [
        pltpu.make_async_copy(source, target, sems.at[n])
        for n, (source, target) in enumerate(zip(sources, targets))
    ]
    for copy in copies:
        copy.start()
    cells_ref, rsrc_ref, rfrac_ref, csrc_ref, cfrac_ref = targets
    depth, span, fields = cells_ref.shape
    out_ref[...] = jnp.zeros_like(out_ref)
    for copy in copies:
        copy.wait()
    for j in range(depth):
        out_ref[j, :, :fields] = cells_ref[j].astype(F32)
    at = 0
    for index_ref, fraction_ref in ((rsrc_ref, rfrac_ref), (csrc_ref, cfrac_ref)):
        width = index_ref.shape[1]
        fraction = fraction_ref[...]
        one = fraction.astype(BF16).astype(F32)
        two = (fraction - one).astype(BF16).astype(F32)
        for value in (index_ref[...].astype(F32), one, two, fraction - one - two):
            out_ref[depth, at : at + 1, :width] = value
            at += 1
    lat = lax.axis_index("lat")
    even = lax.rem(lat, 2) == 0
    own = [out_ref[j] for j in range(depth + 1)]
    to_next = own[depth - ROW_HALO :]
    to_last = own[:ROW_HALO] + own[depth:]
    for j in range(depth + 1):
        own_ref[j] = own[j].astype(BF16)
    for j in range(ROW_HALO + 1):
        outer_ref[j] = jnp.where(even, to_last[j], to_next[j]).astype(BF16)
        inner_ref[j] = jnp.where(even, to_next[j], to_last[j]).astype(BF16)


def main_kernel(
    far_ref,
    near_ref,
    csrc_ref,
    cfrac_ref,
    embed_ref,
    w1_ref,
    turned_ref,
    bh_ref,
    rows_ref,
    tap_ref,
    cot_col_ref,
    blend_ref,
    hid_ref,
    own_ref,
    side_lifted_ref,
    msg_ref,
    side_tap_ref,
    line_ref,
    right_ref,
    delta_ref,
    back_ref,
    *,
    lat_count,
    coarse_cols,
    band_cols,
):
    rows, cols = cot_col_ref.shape[0], own_ref.shape[0]
    wide = bh_ref.shape[1]
    pairs = bh_ref.shape[0] // 2
    depth = 2 * (far_ref.shape[0] - 1)
    half_rows = msg_ref.shape[1]
    lat = lax.axis_index("lat")
    core = lax.axis_index("core")
    lon = lax.axis_index("ring") * 2 + core
    taps = 3 * SPAN

    def send(at, value):
        side = lax.rem(at // half_rows + core, 2)
        at = at % half_rows
        msg_ref[side, at : at + value.shape[0]] = value.astype(BF16)

    sides = []
    for j in range(depth // 2 + 1):
        far, near = far_ref[j].astype(F32), near_ref[j].astype(F32)
        sides.append((jnp.where(core == 1, near, far), jnp.where(core == 1, far, near)))
    cells = []
    for j in range(depth):
        part = slice(j % 2 * COL_HALO, (j % 2 + 1) * COL_HALO)
        cells += [v[part] for v in sides[j // 2]]
    side_mixed = blend_rows(blend_ref[...], cells)
    side_lifted = lift_rows(side_mixed, embed_ref[...])
    side_lifted_ref[...] = side_lifted
    side_tap_ref[...] = tap_rows(side_lifted, w1_ref, band_cols)

    lane_count = 2 * LANES
    lane = lax.broadcasted_iota(jnp.int32, (1, lane_count), 1)
    west_line, east_line = (edge_line(v, 4) for v in sides[depth // 2])
    own_line = (csrc_ref[...].astype(F32), cfrac_ref[...])
    lines = [joined_line(*v, cols) for v in zip(west_line, own_line, east_line)]
    known = lane < cols + 4
    src = jnp.where(known, lines[0], -1e6).astype(jnp.int32)
    blend = blend_cols(src, jnp.where(known, lines[1], 0.0), lon, band_cols, coarse_cols)
    rolled = [blend] + [pltpu.roll(blend, lane_count - b, 1) for b in (1, 2)]
    stack = jnp.concatenate(rolled, axis=0)[:, :wide]
    high, low = split_two(stack)
    high_f, low_f = high.astype(F32), low.astype(F32)
    col_t = jnp.concatenate([high_f, low_f], axis=0).astype(BF16)
    col_lhs = jnp.concatenate([high_f.T, low_f.T, high_f.T], axis=1).astype(BF16)
    own_hi, own_lo = split_two(rolled[2][:, :cols])
    own_hi, own_lo = own_hi.astype(F32).T, own_lo.astype(F32).T
    own_ref[...] = jnp.concatenate([own_hi, own_lo, own_hi], axis=1).astype(BF16)

    for t in range(2 * pairs):
        part = slice(t * band_cols, (t + 1) * band_cols)
        blocks = []
        for b in range(3):
            column = slice(b * LANES, (b + 1) * LANES)
            blocks += [tap_ref[part, column], side_tap_ref[part, column]]
        right_ref[:, t * LANES : (t + 1) * LANES] = stacked(jnp.concatenate(blocks, axis=0))
    half = rows // 2 + 2
    spans = ((0, half), (half, 2 * pairs))
    cells_half = rows // 4 * cols

    def first_product(n):
        span = slice(spans[n][0] * LANES, spans[n][1] * LANES)
        return jnp.dot(col_lhs, right_ref[:, span], preferred_element_type=F32)

    def activate(pre, first, t):
        v = pre[:, (t - first) * LANES : (t - first + 1) * LANES]
        s = 0.5 + 0.5 * jnp.tanh(0.5 * v)
        if t == 0:
            s = s * jnp.where(lat > 0, 1.0, 0.0)
        elif t == 2 * pairs - 1:
            s = s * jnp.where(lat < lat_count - 1, 1.0, 0.0)
        h = v * s
        slope = s + h * (1.0 - s)
        line_ref[t] = h
        delta_ref[:, t * LANES : (t + 1) * LANES] = (bh_ref[t] * slope).astype(BF16)

    def place_hidden(t):
        at = (t // 2) * cols
        for b in range(3):
            hid_ref[b, t % 2, at : at + cols] = line_ref[t, b : b + cols].astype(BF16)

    def second_gradient(n, b):
        right = []
        for i in range(4):
            start = (i // 2) * cols + n * cells_half
            right.append(hid_ref[b, i % 2, start : start + cells_half])
        left = turned_ref[:, n * cells_half : (n + 1) * cells_half]
        return jnp.dot(left, jnp.concatenate(right, axis=1), preferred_element_type=F32)

    pre = first_product(0)
    for t in range(*spans[0]):
        activate(pre, 0, t)
    pre = first_product(1)
    for t in range(*spans[0]):
        place_hidden(t)
    grads = []
    rest = list(range(*spans[1]))
    share = -(-len(rest) // 3)
    for b in range(3):
        grads.append(second_gradient(0, b))
        for t in rest[b * share : (b + 1) * share]:
            activate(pre, spans[1][0], t)
            place_hidden(t)
    back = jnp.dot(col_t, delta_ref[...], preferred_element_type=F32)
    back = back[:taps] + back[taps:]
    width = rows_ref.shape[2]
    used = 2 * pairs * band_cols
    blank = jnp.zeros((2, width - used, back_ref.shape[2]), BF16)
    back_ref[:, used:width] = blank
    back_ref[:, width + used :] = blank
    nothing = jnp.zeros((SPAN, LANES), F32)

    def place_back(p):
        for b in range(4):
            lines = []
            for t in (2 * p, 2 * p + 1):
                if b < 3:
                    lines.append(back[b * SPAN : (b + 1) * SPAN, t * LANES : (t + 1) * LANES])
                else:
                    lines.append(cot_col_ref[t - 1] if 1 <= t <= rows else nothing)
            column = slice(b * LANES, (b + 1) * LANES)
            for side in range(2):
                cells = slice(side * band_cols, (side + 1) * band_cols)
                one, two = split_two(jnp.concatenate([v[cells] for v in lines], axis=0))
                at = side * width + p * SPAN
                back_ref[0, at : at + SPAN, column] = one
                back_ref[1, at : at + SPAN, column] = two

    def send_second(b):
        for a in range(3):
            upper = grads[b][:LANES, a * LANES : (a + 1) * LANES]
            lower = grads[b][LANES:, (a + 1) * LANES : (a + 2) * LANES]
            send((a * 3 + b) * LANES, (upper + lower).T)

    share = -(-pairs // 3)
    side_hi, side_lo = turned_rows(side_mixed, width)
    for b in range(3):
        grads[b] = grads[b] + second_gradient(1, b)
        for p in range(b * share, min((b + 1) * share, pairs)):
            place_back(p)
    upper = jnp.concatenate([rows_ref[0], side_hi], axis=1)
    lower = jnp.concatenate([rows_ref[1], side_lo], axis=1)
    g = jnp.dot(jnp.concatenate([upper, lower], axis=0), back_ref[0], preferred_element_type=F32)
    send_second(0)
    send_second(1)
    g = g[: 3 * GRAD_ROWS] + g[3 * GRAD_ROWS :]
    g = g + jnp.dot(upper, back_ref[1], preferred_element_type=F32)
    send_second(2)
    for a in range(3):
        line = g[a * GRAD_ROWS : (a + 1) * GRAD_ROWS]
        for b in range(3):
            send(9 * LANES + (a * 3 + b) * GRAD_ROWS, line[:, b * LANES : (b + 1) * LANES])
    send(9 * LANES + 9 * GRAD_ROWS, g[GRAD_ROWS : 2 * GRAD_ROWS, 3 * LANES:])
    tail = 9 * LANES + 10 * GRAD_ROWS
    if 2 * half_rows > tail:
        send(tail, jnp.zeros((2 * half_rows - tail, LANES), F32))


def join_kernel(own_ref, outer_ref, inner_ref, ready_ref, before_ref, after_ref, far_ref, near_ref):
    band_rows, band_cols = own_ref.shape[0] - 1, own_ref.shape[1]
    lat = lax.axis_index("lat")
    even = lax.rem(lat, 2) == 0
    first = lax.axis_index("core") == 0
    outer = [outer_ref[j].astype(F32) for j in range(ROW_HALO + 1)]
    inner = [inner_ref[j].astype(F32) for j in range(ROW_HALO + 1)]
    before = [jnp.where(even, v, w) for v, w in zip(outer, inner)]
    after = [jnp.where(even, w, v) for v, w in zip(outer, inner)]
    own = [own_ref[j].astype(F32) for j in range(band_rows + 1)]
    for j in range(ROW_HALO + 1):
        before_ref[j] = before[j].astype(BF16)
        after_ref[j] = after[j].astype(BF16)
    tall = before[:ROW_HALO] + own[:band_rows] + after[:ROW_HALO]
    for j in range(0, len(tall), 2):
        to_last = jnp.concatenate([v[:COL_HALO] for v in tall[j : j + 2]], axis=0)
        to_next = jnp.concatenate([v[band_cols - COL_HALO :] for v in tall[j : j + 2]], axis=0)
        far_ref[j // 2] = jnp.where(first, to_last, to_next).astype(BF16)
        near_ref[j // 2] = jnp.where(first, to_next, to_last).astype(BF16)
    far_ref[len(tall) // 2] = own[band_rows].astype(BF16)
    near_ref[len(tall) // 2] = own[band_rows].astype(BF16)


def features_kernel(weight_ref, hid_ref, own_ref, lifted_ref, side_lifted_ref, *refs, first):
    feat_ref = refs[-1]
    rows, cols, _ = feat_ref.shape
    cells = own_ref.shape[1] // 6
    step = 4
    for n in range(0, rows // 2, step):
        top = first + n
        blocks = []
        for b in range(3):
            for i in range(4):
                start = (top + i // 2) * cols
                blocks.append(hid_ref[b, i % 2, start : start + step * cols])
        out = jnp.dot(jnp.concatenate(blocks, axis=1), weight_ref[...], preferred_element_type=F32)
        right = []
        for r in range(2 * top, 2 * (top + step)):
            part = slice((r + 2) * cells, (r + 3) * cells)
            right.append(stacked(jnp.concatenate([lifted_ref[part], side_lifted_ref[part]], axis=0)))
        lift = jnp.dot(own_ref[...], jnp.concatenate(right, axis=1), preferred_element_type=F32)
        for m in range(step):
            for q in range(2):
                piece = out[m * cols : (m + 1) * cols, q * LANES : (q + 1) * LANES]
                own = lift[:, (2 * m + q) * LANES : (2 * m + q + 1) * LANES]
                feat_ref[2 * (n + m) + q] = (own + piece).astype(BF16)


def reduce_kernel(in_ref, out_ref):
    total = in_ref[0].astype(F32)
    for d in range(1, in_ref.shape[0]):
        total = total + in_ref[d].astype(F32)
    total = total.astype(BF16)
    for d in range(out_ref.shape[0]):
        out_ref[d] = total


def padded_embed(embed_ref, space_ref):
    fields = embed_ref.shape[0]
    space_ref[0, :LANES] = jnp.zeros((LANES, LANES), F32)
    space_ref[0, :fields] = embed_ref[...].astype(F32)
    return space_ref[0, :LANES].astype(BF16)


def last_kernel(
    mine_ref, other_ref, embed_ref, first_ref, upper_ref, lower_ref, feat_hbm, ge_hbm, g1_hbm, g2_hbm,
    sum_ref, ge_ref, g1_ref, g2_ref, sems, *, scale
):
    core = lax.axis_index("core")
    half_rows = mine_ref.shape[0]
    copies = []

    def leave(source, target):
        copies.append(pltpu.make_async_copy(source, target, sems.at[len(copies)]))
        copies[-1].start()

    count = upper_ref.shape[0]
    leave(upper_ref, feat_hbm.at[pl.ds(0, count)])
    leave(lower_ref, feat_hbm.at[pl.ds(count, count)])
    sum_ref[core] = mine_ref[...]
    sum_ref[1 - core] = other_ref[...]

    def read(at, count):
        return sum_ref[at // half_rows, at % half_rows : at % half_rows + count]

    for a in range(3):
        for tap in range(3 * a, 3 * a + 3):
            g2_ref[tap] = read(tap * LANES, LANES).astype(F32) * scale
        leave(g2_ref.at[pl.ds(3 * a, 3)], g2_hbm.at[pl.ds(3 * a, 3)])
    embed_t = embed_ref[...].astype(F32).T.astype(BF16)[:, :GRAD_ROWS]
    base = 9 * LANES
    g = jnp.concatenate([read(base + tap * GRAD_ROWS, GRAD_ROWS) for tap in range(9)], axis=1)
    for a in range(3):
        part = g[:, 3 * a * LANES : (3 * a + 3) * LANES]
        out = jnp.dot(embed_t, part, preferred_element_type=F32) * scale
        for b in range(3):
            g1_ref[3 * a + b] = out[:, b * LANES : (b + 1) * LANES]
        leave(g1_ref.at[pl.ds(3 * a, 3)], g1_hbm.at[pl.ds(3 * a, 3)])
    lift = read(base + 9 * GRAD_ROWS, GRAD_ROWS).astype(F32)
    lift = lift + jnp.dot(g, first_ref[...], preferred_element_type=F32)
    ge_ref[...] = lift[: ge_ref.shape[0]] * scale
    leave(ge_ref, ge_hbm)
    for copy in copies:
        copy.wait()


def from_hbm(value):
    return pltpu.with_memory_space_constraint(value, pltpu.HBM)


def on_device(
    coarse,
    row_src,
    row_frac,
    col_src,
    col_frac,
    embed_weight,
    conv1_weight,
    conv2_weight,
    cotangent,
):
    lat_count = lax.axis_size("lat")
    ring_count = lax.axis_size("ring")
    core_count = lax.axis_size("core")
    lon_count = ring_count * core_count
    fields, band_rows, band_cols = coarse.shape
    rows, cols, hidden = cotangent.shape
    group = lat_count * ring_count
    wide = cols + 16
    pairs = rows // 2 + 1
    depth = band_rows + 2 * ROW_HALO
    params = pltpu.CompilerParams(vmem_limit_bytes=VMEM_BYTES)
    vmem = pl.BlockSpec(memory_space=pltpu.VMEM)
    far = pl.BlockSpec(memory_space=pltpu.HBM)

    w1 = conv1_weight.reshape(9, hidden, hidden)
    w2 = conv2_weight.reshape(9, hidden, hidden)
    row_line = (row_src.reshape(1, rows), row_frac.reshape(1, rows))
    col_line = (col_src.reshape(1, cols), col_frac.reshape(1, cols))

    pack_inputs = (
        jnp.transpose(coarse, (1, 2, 0)),
        *row_line,
        *col_line,
    )
    own, to_outer, to_inner, *lines = pl.pallas_call(
        pack_kernel,
        in_specs=[far] * 5,
        out_shape=[jax.ShapeDtypeStruct((band_rows + 1, band_cols, LANES), BF16)]
        + [jax.ShapeDtypeStruct((ROW_HALO + 1, band_cols, LANES), BF16)] * 2
        + [jax.ShapeDtypeStruct(x.shape, x.dtype) for x in pack_inputs[1:]],
        scratch_shapes=[
            pltpu.VMEM(pack_inputs[0].shape, BF16),
            pltpu.VMEM((band_rows + 1, band_cols, LANES), F32),
            pltpu.SemaphoreType.DMA((5,)),
        ],
        compiler_params=params,
        name="pack",
    )(*(from_hbm(x) for x in pack_inputs))
    row_line, col_line = lines[:2], lines[2:]
    inner = [(i, i ^ 1) for i in range(lat_count)]
    outer = [(i, i + 1) for i in range(1, lat_count - 1, 2)]
    outer = outer + [(j, i) for i, j in outer]
    got_outer = lax.ppermute(to_outer, "lat", outer)
    got_inner = lax.ppermute(to_inner, "lat", inner)

    shift, back_weight, fore_weight, turned, first_weight, cot, near_w1, embed = pl.pallas_call(
        prepare_kernel,
        out_shape=[
            jax.ShapeDtypeStruct((3, 2, (pairs + 1) * wide, hidden), BF16),
            jax.ShapeDtypeStruct((12 * hidden, 2 * hidden), BF16),
            jax.ShapeDtypeStruct((12 * hidden, 2 * hidden), BF16),
            jax.ShapeDtypeStruct((2 * hidden, rows // 2 * cols), BF16),
            jax.ShapeDtypeStruct((9 * hidden, hidden), BF16),
            jax.ShapeDtypeStruct((rows, cols, hidden), BF16),
            jax.ShapeDtypeStruct((9, hidden, hidden), BF16),
            jax.ShapeDtypeStruct((LANES, hidden), BF16),
        ],
        in_specs=[far] * 4,
        scratch_shapes=[
            pltpu.VMEM((9, hidden, hidden), BF16),
            pltpu.VMEM((fields, hidden), BF16),
            pltpu.VMEM((4, wide + 16, hidden), F32),
            pltpu.SemaphoreType.DMA((11,)),
        ],
        compiler_params=params,
        name="prepare",
    )(from_hbm(cotangent), from_hbm(w2), from_hbm(w1), from_hbm(embed_weight))
    before, after, far_message, near_message = pl.pallas_call(
        join_kernel,
        out_shape=[jax.ShapeDtypeStruct((ROW_HALO + 1, band_cols, LANES), BF16)] * 2
        + [jax.ShapeDtypeStruct((depth // 2 + 1, band_cols, LANES), BF16)] * 2,
        compiler_params=params,
        name="join",
    )(own, got_outer, got_inner, embed)
    lon = ("ring", "core")
    inner = [(i, i ^ 1) for i in range(lon_count)]
    outer = [(i, (i + (1 if i % 2 else -1)) % lon_count) for i in range(lon_count)]
    got_far = lax.ppermute(far_message, lon, outer)
    got_near = lax.ppermute(near_message, lon, inner)

    def back_body(*refs):
        back_kernel(*refs, lat_count=lat_count, coarse_cols=band_cols * lon_count)

    reach = rows + 4
    width = -(-reach * band_cols // LANES) * LANES
    bh, mixed, lifted, tap, cot_col, blend = pl.pallas_call(
        back_body,
        out_shape=[
            jax.ShapeDtypeStruct((2 * pairs, wide, hidden), F32),
            jax.ShapeDtypeStruct((2, 3 * GRAD_ROWS, width), BF16),
            jax.ShapeDtypeStruct((reach * band_cols, hidden), F32),
            jax.ShapeDtypeStruct(((reach - 2) * band_cols, 3 * hidden), F32),
            jax.ShapeDtypeStruct((rows, SPAN, hidden), F32),
            jax.ShapeDtypeStruct((reach * band_cols, 2 * LANES), BF16),
        ],
        compiler_params=params,
        name="back_hidden",
    )(
        *row_line, shift, back_weight, before, own, after, *col_line,
        embed, near_w1, cot,
    )

    blocks = 9 * LANES + 10 * GRAD_ROWS
    chunk = -(-blocks // (core_count * group * 16)) * 16
    half_rows = max(group * chunk, -(-blocks // (2 * LANES)) * LANES)

    def body(*refs):
        main_kernel(
            *refs,
            lat_count=lat_count,
            coarse_cols=band_cols * lon_count,
            band_cols=band_cols,
        )

    hid, own_blend, side_lifted, message = pl.pallas_call(
        body,
        out_specs=[vmem] * 4,
        out_shape=[
            jax.ShapeDtypeStruct((3, 2, pairs * cols, hidden), BF16),
            jax.ShapeDtypeStruct((cols, 3 * SPAN), BF16),
            jax.ShapeDtypeStruct((reach * band_cols, hidden), F32),
            jax.ShapeDtypeStruct((2, half_rows, LANES), BF16),
        ],
        scratch_shapes=[
            pltpu.VMEM(((reach - 2) * band_cols, 3 * hidden), F32),
            pltpu.VMEM((2 * pairs, wide, hidden), F32),
            pltpu.VMEM((9 * SPAN, 2 * pairs * hidden), BF16),
            pltpu.VMEM((wide, 2 * pairs * hidden), BF16),
            pltpu.VMEM((2, 2 * width, 4 * hidden), BF16),
        ],
        compiler_params=params,
        name="tile",
    )(
        got_far, got_near, *col_line,
        embed, near_w1, turned, bh, mixed, tap, cot_col, blend,
    )

    def half_features(first, *arrays):
        def body(*refs):
            features_kernel(*refs, first=first)

        return pl.pallas_call(
            body,
            out_shape=jax.ShapeDtypeStruct((rows // 2, cols, hidden), BF16),
            compiler_params=params,
            name=f"features_{first}",
        )(*arrays)

    swap = [(0, 1), (1, 0)]
    received = lax.ppermute(message[1], "core", swap)
    middle = rows // 4
    part = half_features(0, fore_weight, hid, own_blend, lifted, side_lifted)
    received, part = lax.optimization_barrier((received, part))
    pair = (message[0].astype(F32) + received.astype(F32)).astype(BF16)
    axes = ("lat", "ring")
    chunk = half_rows // group
    parts = lax.all_to_all(pair, axes, 0, 0, tiled=True)
    copies = pl.pallas_call(
        reduce_kernel,
        out_shape=jax.ShapeDtypeStruct((group, chunk, LANES), BF16),
        compiler_params=params,
        name="sum_chunks",
    )(parts.reshape(group, chunk, LANES))
    mine = lax.all_to_all(copies.reshape(half_rows, LANES), axes, 0, 0, tiled=True)
    other = lax.ppermute(mine, "core", swap)
    last_part = half_features(middle, fore_weight, hid, own_blend, lifted, side_lifted, mine)
    scale = 1.0 / math.sqrt(rows * lat_count * cols * lon_count)

    def finish(*refs):
        last_kernel(*refs, scale=scale)

    features, grad_embed, grad_first, grad_second = pl.pallas_call(
        finish,
        out_specs=[far] * 4,
        out_shape=[
            jax.ShapeDtypeStruct((rows, cols, hidden), BF16),
            jax.ShapeDtypeStruct((fields, hidden), F32),
            jax.ShapeDtypeStruct((9, hidden, hidden), F32),
            jax.ShapeDtypeStruct((9, hidden, hidden), F32),
        ],
        scratch_shapes=[
            pltpu.VMEM((2, half_rows, LANES), BF16),
            pltpu.VMEM((fields, hidden), F32),
            pltpu.VMEM((9, hidden, hidden), F32),
            pltpu.VMEM((9, hidden, hidden), F32),
            pltpu.SemaphoreType.DMA((9,)),
        ],
        compiler_params=params,
        name="finish",
    )(mine, other, embed, first_weight, part, last_part)
    shape = (3, 3, hidden, hidden)
    return (features, grad_embed, grad_first.reshape(shape), grad_second.reshape(shape))


def solution(mesh):
    lat_count, lon_count = mesh.devices.shape
    inner = jax.sharding.Mesh(
        mesh.devices.reshape(lat_count, lon_count // 2, 2), ("lat", "ring", "core")
    )
    lon = ("ring", "core")
    in_specs = (
        P(None, "lat", lon),
        P("lat"),
        P("lat"),
        P(lon),
        P(lon),
        P(),
        P(),
        P(),
        P("lat", lon, None),
    )
    out_specs = (P("lat", lon, None), P(), P(), P())
    return jax.shard_map(
        on_device, mesh=inner, in_specs=in_specs, out_specs=out_specs, check_vma=False
    )
```

```python
import math

import jax
import jax.numpy as jnp
from jax import lax
from jax.experimental import pallas as pl
from jax.experimental.pallas import tpu as pltpu
from jax.sharding import PartitionSpec as P

F32 = jnp.float32
BF16 = jnp.bfloat16
LANES = 128
ROW_HALO = 3
COL_HALO = 4
SPAN = 16
GRAD_ROWS = 80
VMEM_BYTES = 24 * 1024 * 1024


def split_two(value):
    high = value.astype(BF16)
    return high, (value - high.astype(F32)).astype(BF16)


def prepare_kernel(
    cot_hbm, w2_hbm, w1_hbm, embed_hbm,
    shift_ref, back_ref, fore_ref, turned_ref, first_ref, cot_ref, w1_ref, padded_ref,
    w2_ref, embed_ref, line_ref, sems
):
    rows, cols, _ = cot_ref.shape
    wide = cols + 16
    pairs = rows // 2 + 1
    chunks = sems.shape[0] - 3
    share = rows // chunks
    weight_copy = pltpu.make_async_copy(w2_hbm, w2_ref, sems.at[chunks])
    weight_copy.start()
    copies = []
    for n in range(chunks):
        part = pl.ds(n * share, share)
        copies.append(pltpu.make_async_copy(cot_hbm.at[part], cot_ref.at[part], sems.at[n]))
        copies[-1].start()
    other_copy = pltpu.make_async_copy(w1_hbm, w1_ref, sems.at[chunks + 1])
    other_copy.start()
    embed_copy = pltpu.make_async_copy(embed_hbm, embed_ref, sems.at[chunks + 2])
    embed_copy.start()
    line_ref[...] = jnp.zeros_like(line_ref)
    back_ref[...] = jnp.zeros_like(back_ref)
    fore_ref[...] = jnp.zeros_like(fore_ref)
    blank = jnp.zeros((wide, LANES), BF16)
    for b in range(3):
        for parity in range(2):
            shift_ref[b, parity, 0:wide] = blank
            shift_ref[b, parity, pairs * wide : (pairs + 1) * wide] = blank
    weight_copy.wait()
    for a in range(3):
        for b in range(3):
            straight = w2_ref[a * 3 + b]
            turned = straight.astype(F32).T.astype(BF16)
            for q in range(2):
                column = slice(q * LANES, (q + 1) * LANES)
                at = (b * 4 + 2 + q - a) * LANES
                back_ref[at : at + LANES, column] = turned
                at = (b * 4 + a + q) * LANES
                fore_ref[at : at + LANES, column] = straight
    for r in range(rows):
        slot = r % 4
        if r % share == 0:
            copies[r // share].wait()
        line = cot_ref[r].astype(F32)
        line_ref[slot, 8 : 8 + cols] = line
        start = (r // 2 + 1) * wide
        for b in range(3):
            shift_ref[b, r % 2, start : start + wide] = line_ref[slot, 8 - b : 8 - b + wide].astype(BF16)
        turned_ref[(r % 2) * LANES : (r % 2 + 1) * LANES, (r // 2) * cols : (r // 2 + 1) * cols] = line.T.astype(BF16)
    embed_copy.wait()
    padded_ref[...] = padded_embed(embed_ref, line_ref)
    other_copy.wait()
    for tap in range(9):
        first_ref[tap * LANES : (tap + 1) * LANES] = w1_ref[tap].astype(F32).T.astype(BF16)


def edge_line(block, at):
    index = block[at : at + 1]
    return index, block[at + 1 : at + 2] + block[at + 2 : at + 3] + block[at + 3 : at + 4]


def joined_line(first, own, last, width):
    lane_count = 2 * LANES
    lane = lax.broadcasted_iota(jnp.int32, (1, lane_count), 1)
    out = []
    for part, shift in zip((first, own, last), (lane_count - width + 2, 2, width + 2)):
        part = jnp.concatenate([part[:, :width], jnp.zeros((1, lane_count - width), F32)], axis=1)
        out.append(pltpu.roll(jnp.broadcast_to(part, (8, lane_count)), shift, 1)[:1])
    return jnp.where(lane < 2, out[0], jnp.where(lane < width + 2, out[1], out[2]))


def row_blend(rsrc_ref, rfrac_ref, before_ref, after_ref, lat, lat_count, band_rows):
    rows = rsrc_ref.shape[1]
    cells = 2 * COL_HALO
    before_line = edge_line(before_ref[ROW_HALO].astype(F32), 0)
    after_line = edge_line(after_ref[ROW_HALO].astype(F32), 0)
    own_line = (rsrc_ref[...].astype(F32), rfrac_ref[...])
    src, frac = (
        joined_line(*lines, rows) for lines in zip(before_line, own_line, after_line)
    )
    spot = (src - (lat * band_rows - ROW_HALO).astype(F32)) * cells
    shape = (cells, LANES)
    at = lax.broadcasted_iota(jnp.int32, shape, 1) - lax.broadcasted_iota(jnp.int32, shape, 0)
    at = at.astype(F32)
    parts = []
    for q in range(rows + 4):
        here = jnp.broadcast_to(spot[:, q : q + 1], shape)
        f = jnp.broadcast_to(frac[:, q : q + 1], shape)
        part = jnp.where(at == here, 1.0 - f, 0.0) + jnp.where(at == here + cells, f, 0.0)
        if q < 2:
            part = part * jnp.where(lat > 0, 1.0, 0.0)
        elif q >= rows + 2:
            part = part * jnp.where(lat < lat_count - 1, 1.0, 0.0)
        parts.append(part)
    return jnp.concatenate(list(split_two(jnp.concatenate(parts, axis=0))), axis=1)


def blend_rows(matrix, cells):
    fill = jnp.zeros((LANES - sum(c.shape[0] for c in cells), LANES), F32)
    column = jnp.concatenate(list(cells) + [fill], axis=0).astype(BF16)
    return jnp.dot(matrix, jnp.concatenate([column, column], axis=0), preferred_element_type=F32)


def stacked(value):
    one, two = split_two(value)
    return jnp.concatenate([one, one, two], axis=0)


def lift_rows(mixed, embed):
    pair = jnp.concatenate(list(split_two(mixed)), axis=1)
    return jnp.dot(pair, jnp.concatenate([embed, embed], axis=0), preferred_element_type=F32)


def turned_rows(mixed, width):
    fill = jnp.zeros((width - mixed.shape[0], LANES), F32)
    turned = jnp.concatenate([mixed, fill], axis=0).T[:GRAD_ROWS]
    step = 2 * COL_HALO
    lines = [turned] + [pltpu.roll(turned, width - a * step, 1) for a in (1, 2)]
    return split_two(jnp.concatenate(lines, axis=0))


def tap_rows(lifted, w1_ref, cells):
    count = lifted.shape[0] - 2 * cells
    pairs = [split_two(lifted[a * cells : a * cells + count]) for a in range(3)]
    left = jnp.concatenate([p[0] for p in pairs] + [p[1] for p in pairs], axis=1)
    lines = [jnp.concatenate([w1_ref[a * 3 + b] for b in range(3)], axis=1) for a in range(3)]
    return jnp.dot(left, jnp.concatenate(lines + lines, axis=0), preferred_element_type=F32)


def blend_cols(src, frac, lon, band_cols, coarse_cols):
    shape = (SPAN, src.shape[1])
    local = jnp.broadcast_to(src, shape) - lon * band_cols
    frac = jnp.broadcast_to(frac, shape)
    local = jnp.where(local < -COL_HALO, local + coarse_cols, local)
    local = jnp.where(local >= band_cols + COL_HALO, local - coarse_cols, local)
    line = lax.broadcasted_iota(jnp.int32, shape, 0)

    def spot(at):
        east = jnp.where(at >= band_cols, at + COL_HALO, at)
        return jnp.where(at < 0, at + band_cols + COL_HALO, east)

    return jnp.where(line == spot(local), 1.0 - frac, 0.0) + jnp.where(
        line == spot(local + 1), frac, 0.0
    )


def back_kernel(
    rsrc_ref,
    rfrac_ref,
    shift_ref,
    weight_ref,
    before_ref,
    own_ref,
    after_ref,
    csrc_ref,
    cfrac_ref,
    embed_ref,
    w1_ref,
    cot_ref,
    bh_ref,
    rows_ref,
    lifted_ref,
    tap_ref,
    cot_col_ref,
    blend_ref,
    *,
    lat_count,
    coarse_cols,
):
    rows, cols, _ = cot_ref.shape
    wide = bh_ref.shape[1]
    pairs = bh_ref.shape[0] // 2
    band_rows, band_cols = own_ref.shape[0] - 1, own_ref.shape[1]
    step = 6
    for first in range(0, pairs, step):
        count = min(step, pairs - first)
        blocks = []
        for b in range(3):
            for i in range(4):
                start = (first + i // 2) * wide
                blocks.append(shift_ref[b, i % 2, start : start + count * wide])
        out = jnp.dot(jnp.concatenate(blocks, axis=1), weight_ref[...], preferred_element_type=F32)
        for m in range(count):
            for q in range(2):
                bh_ref[2 * (first + m) + q] = out[m * wide : (m + 1) * wide, q * LANES : (q + 1) * LANES]

    lat = lax.axis_index("lat")
    lon = lax.axis_index("ring") * 2 + lax.axis_index("core")
    matrix = row_blend(rsrc_ref, rfrac_ref, before_ref, after_ref, lat, lat_count, band_rows)
    blend_ref[...] = matrix
    cells = [before_ref[j] for j in range(ROW_HALO)] + [own_ref[j] for j in range(band_rows)]
    cells += [after_ref[j] for j in range(ROW_HALO)]
    mixed = blend_rows(matrix, [c.astype(F32) for c in cells])
    rows_ref[0], rows_ref[1] = turned_rows(mixed, rows_ref.shape[2])
    lifted = lift_rows(mixed, embed_ref[...])
    lifted_ref[...] = lifted
    tap_ref[...] = tap_rows(lifted, w1_ref, band_cols)

    blend = blend_cols(csrc_ref[...], cfrac_ref[...], lon, band_cols, coarse_cols)
    own_t = jnp.concatenate(list(split_two(blend)), axis=0)
    every = jnp.concatenate([cot_ref[r] for r in range(rows)], axis=1)
    back = jnp.dot(own_t, every, preferred_element_type=F32)
    back = back[:SPAN] + back[SPAN:]
    for r in range(rows):
        cot_col_ref[r] = back[:, r * LANES : (r + 1) * LANES]


def pack_kernel(cells_hbm, rsrc_hbm, rfrac_hbm, csrc_hbm, cfrac_hbm, *space):
    sources = (cells_hbm, rsrc_hbm, rfrac_hbm, csrc_hbm, cfrac_hbm)
    own_ref, outer_ref, inner_ref, *lines, cells_ref, out_ref, sems = space
    targets = (cells_ref, *lines)
    copies = [
        pltpu.make_async_copy(source, target, sems.at[n])
        for n, (source, target) in enumerate(zip(sources, targets))
    ]
    for copy in copies:
        copy.start()
    cells_ref, rsrc_ref, rfrac_ref, csrc_ref, cfrac_ref = targets
    depth, span, fields = cells_ref.shape
    out_ref[...] = jnp.zeros_like(out_ref)
    for copy in copies:
        copy.wait()
    for j in range(depth):
        out_ref[j, :, :fields] = cells_ref[j].astype(F32)
    at = 0
    for index_ref, fraction_ref in ((rsrc_ref, rfrac_ref), (csrc_ref, cfrac_ref)):
        width = index_ref.shape[1]
        fraction = fraction_ref[...]
        one = fraction.astype(BF16).astype(F32)
        two = (fraction - one).astype(BF16).astype(F32)
        for value in (index_ref[...].astype(F32), one, two, fraction - one - two):
            out_ref[depth, at : at + 1, :width] = value
            at += 1
    lat = lax.axis_index("lat")
    even = lax.rem(lat, 2) == 0
    own = [out_ref[j] for j in range(depth + 1)]
    to_next = own[depth - ROW_HALO :]
    to_last = own[:ROW_HALO] + own[depth:]
    for j in range(depth + 1):
        own_ref[j] = own[j].astype(BF16)
    for j in range(ROW_HALO + 1):
        outer_ref[j] = jnp.where(even, to_last[j], to_next[j]).astype(BF16)
        inner_ref[j] = jnp.where(even, to_next[j], to_last[j]).astype(BF16)


def main_kernel(
    far_ref,
    near_ref,
    csrc_ref,
    cfrac_ref,
    embed_ref,
    w1_ref,
    turned_ref,
    bh_ref,
    rows_ref,
    tap_ref,
    cot_col_ref,
    blend_ref,
    hid_ref,
    own_ref,
    side_lifted_ref,
    msg_ref,
    side_tap_ref,
    line_ref,
    right_ref,
    delta_ref,
    back_ref,
    *,
    lat_count,
    coarse_cols,
    band_cols,
):
    rows, cols = cot_col_ref.shape[0], own_ref.shape[0]
    wide = bh_ref.shape[1]
    pairs = bh_ref.shape[0] // 2
    depth = 2 * (far_ref.shape[0] - 1)
    half_rows = msg_ref.shape[1]
    lat = lax.axis_index("lat")
    core = lax.axis_index("core")
    lon = lax.axis_index("ring") * 2 + core
    taps = 3 * SPAN

    def send(at, value):
        side = lax.rem(at // half_rows + core, 2)
        at = at % half_rows
        msg_ref[side, at : at + value.shape[0]] = value.astype(BF16)

    sides = []
    for j in range(depth // 2 + 1):
        far, near = far_ref[j].astype(F32), near_ref[j].astype(F32)
        sides.append((jnp.where(core == 1, near, far), jnp.where(core == 1, far, near)))
    cells = []
    for j in range(depth):
        part = slice(j % 2 * COL_HALO, (j % 2 + 1) * COL_HALO)
        cells += [v[part] for v in sides[j // 2]]
    side_mixed = blend_rows(blend_ref[...], cells)
    side_lifted = lift_rows(side_mixed, embed_ref[...])
    side_lifted_ref[...] = side_lifted
    side_tap_ref[...] = tap_rows(side_lifted, w1_ref, band_cols)

    lane_count = 2 * LANES
    lane = lax.broadcasted_iota(jnp.int32, (1, lane_count), 1)
    west_line, east_line = (edge_line(v, 4) for v in sides[depth // 2])
    own_line = (csrc_ref[...].astype(F32), cfrac_ref[...])
    lines = [joined_line(*v, cols) for v in zip(west_line, own_line, east_line)]
    known = lane < cols + 4
    src = jnp.where(known, lines[0], -1e6).astype(jnp.int32)
    blend = blend_cols(src, jnp.where(known, lines[1], 0.0), lon, band_cols, coarse_cols)
    rolled = [blend] + [pltpu.roll(blend, lane_count - b, 1) for b in (1, 2)]
    stack = jnp.concatenate(rolled, axis=0)[:, :wide]
    high, low = split_two(stack)
    high_f, low_f = high.astype(F32), low.astype(F32)
    col_t = jnp.concatenate([high_f, low_f], axis=0).astype(BF16)
    col_lhs = jnp.concatenate([high_f.T, low_f.T, high_f.T], axis=1).astype(BF16)
    own_hi, own_lo = split_two(rolled[2][:, :cols])
    own_hi, own_lo = own_hi.astype(F32).T, own_lo.astype(F32).T
    own_ref[...] = jnp.concatenate([own_hi, own_lo, own_hi], axis=1).astype(BF16)

    for t in range(2 * pairs):
        part = slice(t * band_cols, (t + 1) * band_cols)
        blocks = []
        for b in range(3):
            column = slice(b * LANES, (b + 1) * LANES)
            blocks += [tap_ref[part, column], side_tap_ref[part, column]]
        right_ref[:, t * LANES : (t + 1) * LANES] = stacked(jnp.concatenate(blocks, axis=0))
    half = rows // 2 + 2
    spans = ((0, half), (half, 2 * pairs))
    cells_half = rows // 4 * cols

    def first_product(n):
        span = slice(spans[n][0] * LANES, spans[n][1] * LANES)
        return jnp.dot(col_lhs, right_ref[:, span], preferred_element_type=F32)

    def activate(pre, first, t):
        v = pre[:, (t - first) * LANES : (t - first + 1) * LANES]
        s = 0.5 + 0.5 * jnp.tanh(0.5 * v)
        if t == 0:
            s = s * jnp.where(lat > 0, 1.0, 0.0)
        elif t == 2 * pairs - 1:
            s = s * jnp.where(lat < lat_count - 1, 1.0, 0.0)
        h = v * s
        slope = s + h * (1.0 - s)
        line_ref[t] = h
        delta_ref[:, t * LANES : (t + 1) * LANES] = (bh_ref[t] * slope).astype(BF16)

    def place_hidden(t):
        at = (t // 2) * cols
        for b in range(3):
            hid_ref[b, t % 2, at : at + cols] = line_ref[t, b : b + cols].astype(BF16)

    def second_gradient(n, b):
        right = []
        for i in range(4):
            start = (i // 2) * cols + n * cells_half
            right.append(hid_ref[b, i % 2, start : start + cells_half])
        left = turned_ref[:, n * cells_half : (n + 1) * cells_half]
        return jnp.dot(left, jnp.concatenate(right, axis=1), preferred_element_type=F32)

    pre = first_product(0)
    for t in range(*spans[0]):
        activate(pre, 0, t)
    pre = first_product(1)
    for t in range(*spans[0]):
        place_hidden(t)
    grads = []
    rest = list(range(*spans[1]))
    share = -(-len(rest) // 3)
    for b in range(3):
        grads.append(second_gradient(0, b))
        for t in rest[b * share : (b + 1) * share]:
            activate(pre, spans[1][0], t)
            place_hidden(t)
    back = jnp.dot(col_t, delta_ref[...], preferred_element_type=F32)
    back = back[:taps] + back[taps:]
    width = rows_ref.shape[2]
    used = 2 * pairs * band_cols
    blank = jnp.zeros((2, width - used, back_ref.shape[2]), BF16)
    back_ref[:, used:width] = blank
    back_ref[:, width + used :] = blank
    nothing = jnp.zeros((SPAN, LANES), F32)

    def place_back(p):
        for b in range(4):
            lines = []
            for t in (2 * p, 2 * p + 1):
                if b < 3:
                    lines.append(back[b * SPAN : (b + 1) * SPAN, t * LANES : (t + 1) * LANES])
                else:
                    lines.append(cot_col_ref[t - 1] if 1 <= t <= rows else nothing)
            column = slice(b * LANES, (b + 1) * LANES)
            for side in range(2):
                cells = slice(side * band_cols, (side + 1) * band_cols)
                one, two = split_two(jnp.concatenate([v[cells] for v in lines], axis=0))
                at = side * width + p * SPAN
                back_ref[0, at : at + SPAN, column] = one
                back_ref[1, at : at + SPAN, column] = two

    def send_second(b):
        for a in range(3):
            upper = grads[b][:LANES, a * LANES : (a + 1) * LANES]
            lower = grads[b][LANES:, (a + 1) * LANES : (a + 2) * LANES]
            send((a * 3 + b) * LANES, (upper + lower).T)

    share = -(-pairs // 3)
    side_hi, side_lo = turned_rows(side_mixed, width)
    for b in range(3):
        grads[b] = grads[b] + second_gradient(1, b)
        for p in range(b * share, min((b + 1) * share, pairs)):
            place_back(p)
    upper = jnp.concatenate([rows_ref[0], side_hi], axis=1)
    lower = jnp.concatenate([rows_ref[1], side_lo], axis=1)
    g = jnp.dot(jnp.concatenate([upper, lower], axis=0), back_ref[0], preferred_element_type=F32)
    send_second(0)
    send_second(1)
    g = g[: 3 * GRAD_ROWS] + g[3 * GRAD_ROWS :]
    g = g + jnp.dot(upper, back_ref[1], preferred_element_type=F32)
    send_second(2)
    for a in range(3):
        line = g[a * GRAD_ROWS : (a + 1) * GRAD_ROWS]
        for b in range(3):
            send(9 * LANES + (a * 3 + b) * GRAD_ROWS, line[:, b * LANES : (b + 1) * LANES])
    send(9 * LANES + 9 * GRAD_ROWS, g[GRAD_ROWS : 2 * GRAD_ROWS, 3 * LANES:])
    tail = 9 * LANES + 10 * GRAD_ROWS
    if 2 * half_rows > tail:
        send(tail, jnp.zeros((2 * half_rows - tail, LANES), F32))


def join_kernel(own_ref, outer_ref, inner_ref, ready_ref, before_ref, after_ref, far_ref, near_ref):
    band_rows, band_cols = own_ref.shape[0] - 1, own_ref.shape[1]
    lat = lax.axis_index("lat")
    even = lax.rem(lat, 2) == 0
    first = lax.axis_index("core") == 0
    outer = [outer_ref[j].astype(F32) for j in range(ROW_HALO + 1)]
    inner = [inner_ref[j].astype(F32) for j in range(ROW_HALO + 1)]
    before = [jnp.where(even, v, w) for v, w in zip(outer, inner)]
    after = [jnp.where(even, w, v) for v, w in zip(outer, inner)]
    own = [own_ref[j].astype(F32) for j in range(band_rows + 1)]
    for j in range(ROW_HALO + 1):
        before_ref[j] = before[j].astype(BF16)
        after_ref[j] = after[j].astype(BF16)
    tall = before[:ROW_HALO] + own[:band_rows] + after[:ROW_HALO]
    for j in range(0, len(tall), 2):
        to_last = jnp.concatenate([v[:COL_HALO] for v in tall[j : j + 2]], axis=0)
        to_next = jnp.concatenate([v[band_cols - COL_HALO :] for v in tall[j : j + 2]], axis=0)
        far_ref[j // 2] = jnp.where(first, to_last, to_next).astype(BF16)
        near_ref[j // 2] = jnp.where(first, to_next, to_last).astype(BF16)
    far_ref[len(tall) // 2] = own[band_rows].astype(BF16)
    near_ref[len(tall) // 2] = own[band_rows].astype(BF16)


def leave_parts(source, target, sems, at):
    count = sems.shape[0]
    share = source.shape[0] // count
    copies = [
        pltpu.make_async_copy(
            source.at[pl.ds(n * share, share)], target.at[pl.ds(at + n * share, share)], sems.at[n]
        )
        for n in range(count)
    ]
    for copy in copies:
        copy.start()
    return copies


def features_kernel(weight_ref, hid_ref, own_ref, lifted_ref, side_lifted_ref, *refs, first):
    copies = []
    if first:
        _, earlier_ref, feat_ref, out_hbm, sems = refs
        copies = leave_parts(earlier_ref, out_hbm, sems, 0)
    else:
        (feat_ref,) = refs
    rows, cols, _ = feat_ref.shape
    cells = own_ref.shape[1] // 6
    step = 4
    for n in range(0, rows // 2, step):
        top = first + n
        blocks = []
        for b in range(3):
            for i in range(4):
                start = (top + i // 2) * cols
                blocks.append(hid_ref[b, i % 2, start : start + step * cols])
        out = jnp.dot(jnp.concatenate(blocks, axis=1), weight_ref[...], preferred_element_type=F32)
        right = []
        for r in range(2 * top, 2 * (top + step)):
            part = slice((r + 2) * cells, (r + 3) * cells)
            right.append(stacked(jnp.concatenate([lifted_ref[part], side_lifted_ref[part]], axis=0)))
        lift = jnp.dot(own_ref[...], jnp.concatenate(right, axis=1), preferred_element_type=F32)
        for m in range(step):
            for q in range(2):
                piece = out[m * cols : (m + 1) * cols, q * LANES : (q + 1) * LANES]
                own = lift[:, (2 * m + q) * LANES : (2 * m + q + 1) * LANES]
                feat_ref[2 * (n + m) + q] = (own + piece).astype(BF16)
    for copy in copies:
        copy.wait()


def reduce_kernel(in_ref, out_ref):
    total = in_ref[0].astype(F32)
    for d in range(1, in_ref.shape[0]):
        total = total + in_ref[d].astype(F32)
    total = total.astype(BF16)
    for d in range(out_ref.shape[0]):
        out_ref[d] = total


def padded_embed(embed_ref, space_ref):
    fields = embed_ref.shape[0]
    space_ref[0, :LANES] = jnp.zeros((LANES, LANES), F32)
    space_ref[0, :fields] = embed_ref[...].astype(F32)
    return space_ref[0, :LANES].astype(BF16)


def last_kernel(
    mine_ref, other_ref, embed_ref, first_ref, part_ref, begun_hbm, feat_hbm, ge_hbm, g1_hbm, g2_hbm,
    sum_ref, ge_ref, g1_ref, g2_ref, feat_sems, g1_sems, g2_sems, ge_sem, *, scale
):
    core = lax.axis_index("core")
    half_rows = mine_ref.shape[0]
    copies = leave_parts(part_ref, feat_hbm, feat_sems, part_ref.shape[0])
    sum_ref[core] = mine_ref[...]
    sum_ref[1 - core] = other_ref[...]

    def read(at, count):
        return sum_ref[at // half_rows, at % half_rows : at % half_rows + count]

    def leave(source, target, sem):
        copies.append(pltpu.make_async_copy(source, target, sem))
        copies[-1].start()

    for tap in range(9):
        g2_ref[tap] = read(tap * LANES, LANES).astype(F32) * scale
        leave(g2_ref.at[tap], g2_hbm.at[tap], g2_sems.at[tap])
    embed_t = embed_ref[...].astype(F32).T.astype(BF16)[:, :GRAD_ROWS]
    base = 9 * LANES
    g = jnp.concatenate([read(base + tap * GRAD_ROWS, GRAD_ROWS) for tap in range(9)], axis=1)
    lift = read(base + 9 * GRAD_ROWS, GRAD_ROWS).astype(F32)
    lift = lift + jnp.dot(g, first_ref[...], preferred_element_type=F32)
    ge_ref[...] = lift[: ge_ref.shape[0]] * scale
    leave(ge_ref, ge_hbm, ge_sem)
    out = jnp.dot(embed_t, g, preferred_element_type=F32) * scale
    for tap in range(9):
        g1_ref[tap] = out[:, tap * LANES : (tap + 1) * LANES]
        leave(g1_ref.at[tap], g1_hbm.at[tap], g1_sems.at[tap])
    for copy in copies:
        copy.wait()


def from_hbm(value):
    return pltpu.with_memory_space_constraint(value, pltpu.HBM)


def on_device(
    coarse,
    row_src,
    row_frac,
    col_src,
    col_frac,
    embed_weight,
    conv1_weight,
    conv2_weight,
    cotangent,
):
    lat_count = lax.axis_size("lat")
    ring_count = lax.axis_size("ring")
    core_count = lax.axis_size("core")
    lon_count = ring_count * core_count
    fields, band_rows, band_cols = coarse.shape
    rows, cols, hidden = cotangent.shape
    group = lat_count * ring_count
    wide = cols + 16
    pairs = rows // 2 + 1
    depth = band_rows + 2 * ROW_HALO
    params = pltpu.CompilerParams(vmem_limit_bytes=VMEM_BYTES)
    vmem = pl.BlockSpec(memory_space=pltpu.VMEM)
    far = pl.BlockSpec(memory_space=pltpu.HBM)

    w1 = conv1_weight.reshape(9, hidden, hidden)
    w2 = conv2_weight.reshape(9, hidden, hidden)
    row_line = (row_src.reshape(1, rows), row_frac.reshape(1, rows))
    col_line = (col_src.reshape(1, cols), col_frac.reshape(1, cols))

    pack_inputs = (
        jnp.transpose(coarse, (1, 2, 0)),
        *row_line,
        *col_line,
    )
    own, to_outer, to_inner, *lines = pl.pallas_call(
        pack_kernel,
        in_specs=[far] * 5,
        out_shape=[jax.ShapeDtypeStruct((band_rows + 1, band_cols, LANES), BF16)]
        + [jax.ShapeDtypeStruct((ROW_HALO + 1, band_cols, LANES), BF16)] * 2
        + [jax.ShapeDtypeStruct(x.shape, x.dtype) for x in pack_inputs[1:]],
        scratch_shapes=[
            pltpu.VMEM(pack_inputs[0].shape, BF16),
            pltpu.VMEM((band_rows + 1, band_cols, LANES), F32),
            pltpu.SemaphoreType.DMA((5,)),
        ],
        compiler_params=params,
        name="pack",
    )(*(from_hbm(x) for x in pack_inputs))
    row_line, col_line = lines[:2], lines[2:]
    inner = [(i, i ^ 1) for i in range(lat_count)]
    outer = [(i, i + 1) for i in range(1, lat_count - 1, 2)]
    outer = outer + [(j, i) for i, j in outer]
    got_outer = lax.ppermute(to_outer, "lat", outer)
    got_inner = lax.ppermute(to_inner, "lat", inner)

    shift, back_weight, fore_weight, turned, first_weight, cot, near_w1, embed = pl.pallas_call(
        prepare_kernel,
        out_shape=[
            jax.ShapeDtypeStruct((3, 2, (pairs + 1) * wide, hidden), BF16),
            jax.ShapeDtypeStruct((12 * hidden, 2 * hidden), BF16),
            jax.ShapeDtypeStruct((12 * hidden, 2 * hidden), BF16),
            jax.ShapeDtypeStruct((2 * hidden, rows // 2 * cols), BF16),
            jax.ShapeDtypeStruct((9 * hidden, hidden), BF16),
            jax.ShapeDtypeStruct((rows, cols, hidden), BF16),
            jax.ShapeDtypeStruct((9, hidden, hidden), BF16),
            jax.ShapeDtypeStruct((LANES, hidden), BF16),
        ],
        in_specs=[far] * 4,
        scratch_shapes=[
            pltpu.VMEM((9, hidden, hidden), BF16),
            pltpu.VMEM((fields, hidden), BF16),
            pltpu.VMEM((4, wide + 16, hidden), F32),
            pltpu.SemaphoreType.DMA((11,)),
        ],
        compiler_params=params,
        name="prepare",
    )(from_hbm(cotangent), from_hbm(w2), from_hbm(w1), from_hbm(embed_weight))
    before, after, far_message, near_message = pl.pallas_call(
        join_kernel,
        out_shape=[jax.ShapeDtypeStruct((ROW_HALO + 1, band_cols, LANES), BF16)] * 2
        + [jax.ShapeDtypeStruct((depth // 2 + 1, band_cols, LANES), BF16)] * 2,
        compiler_params=params,
        name="join",
    )(own, got_outer, got_inner, embed)
    lon = ("ring", "core")
    inner = [(i, i ^ 1) for i in range(lon_count)]
    outer = [(i, (i + (1 if i % 2 else -1)) % lon_count) for i in range(lon_count)]
    got_far = lax.ppermute(far_message, lon, outer)
    got_near = lax.ppermute(near_message, lon, inner)

    def back_body(*refs):
        back_kernel(*refs, lat_count=lat_count, coarse_cols=band_cols * lon_count)

    reach = rows + 4
    width = -(-reach * band_cols // LANES) * LANES
    bh, mixed, lifted, tap, cot_col, blend = pl.pallas_call(
        back_body,
        out_shape=[
            jax.ShapeDtypeStruct((2 * pairs, wide, hidden), F32),
            jax.ShapeDtypeStruct((2, 3 * GRAD_ROWS, width), BF16),
            jax.ShapeDtypeStruct((reach * band_cols, hidden), F32),
            jax.ShapeDtypeStruct(((reach - 2) * band_cols, 3 * hidden), F32),
            jax.ShapeDtypeStruct((rows, SPAN, hidden), F32),
            jax.ShapeDtypeStruct((reach * band_cols, 2 * LANES), BF16),
        ],
        compiler_params=params,
        name="back_hidden",
    )(
        *row_line, shift, back_weight, before, own, after, *col_line,
        embed, near_w1, cot,
    )

    blocks = 9 * LANES + 10 * GRAD_ROWS
    chunk = -(-blocks // (core_count * group * 16)) * 16
    half_rows = max(group * chunk, -(-blocks // (2 * LANES)) * LANES)

    def body(*refs):
        main_kernel(
            *refs,
            lat_count=lat_count,
            coarse_cols=band_cols * lon_count,
            band_cols=band_cols,
        )

    hid, own_blend, side_lifted, message = pl.pallas_call(
        body,
        out_specs=[vmem] * 4,
        out_shape=[
            jax.ShapeDtypeStruct((3, 2, pairs * cols, hidden), BF16),
            jax.ShapeDtypeStruct((cols, 3 * SPAN), BF16),
            jax.ShapeDtypeStruct((reach * band_cols, hidden), F32),
            jax.ShapeDtypeStruct((2, half_rows, LANES), BF16),
        ],
        scratch_shapes=[
            pltpu.VMEM(((reach - 2) * band_cols, 3 * hidden), F32),
            pltpu.VMEM((2 * pairs, wide, hidden), F32),
            pltpu.VMEM((9 * SPAN, 2 * pairs * hidden), BF16),
            pltpu.VMEM((wide, 2 * pairs * hidden), BF16),
            pltpu.VMEM((2, 2 * width, 4 * hidden), BF16),
        ],
        compiler_params=params,
        name="tile",
    )(
        got_far, got_near, *col_line,
        embed, near_w1, turned, bh, mixed, tap, cot_col, blend,
    )

    def half_features(first, *arrays):
        def body(*refs):
            features_kernel(*refs, first=first)

        half = jax.ShapeDtypeStruct((rows // 2, cols, hidden), BF16)
        whole = jax.ShapeDtypeStruct((rows, cols, hidden), BF16)
        return pl.pallas_call(
            body,
            out_specs=[vmem, far] if first else vmem,
            out_shape=[half, whole] if first else half,
            scratch_shapes=[pltpu.SemaphoreType.DMA((4,))] if first else [],
            compiler_params=params,
            name=f"features_{first}",
        )(*arrays)

    swap = [(0, 1), (1, 0)]
    received = lax.ppermute(message[1], "core", swap)
    middle = rows // 4
    part = half_features(0, fore_weight, hid, own_blend, lifted, side_lifted)
    received, part = lax.optimization_barrier((received, part))
    pair = (message[0].astype(F32) + received.astype(F32)).astype(BF16)
    axes = ("lat", "ring")
    chunk = half_rows // group
    parts = lax.all_to_all(pair, axes, 0, 0, tiled=True)
    copies = pl.pallas_call(
        reduce_kernel,
        out_shape=jax.ShapeDtypeStruct((group, chunk, LANES), BF16),
        compiler_params=params,
        name="sum_chunks",
    )(parts.reshape(group, chunk, LANES))
    mine = lax.all_to_all(copies.reshape(half_rows, LANES), axes, 0, 0, tiled=True)
    other = lax.ppermute(mine, "core", swap)
    last_part, features = half_features(
        middle, fore_weight, hid, own_blend, lifted, side_lifted, mine, part
    )
    scale = 1.0 / math.sqrt(rows * lat_count * cols * lon_count)

    def finish(*refs):
        last_kernel(*refs, scale=scale)

    features, grad_embed, grad_first, grad_second = pl.pallas_call(
        finish,
        in_specs=[vmem] * 5 + [far],
        out_specs=[far] * 4,
        input_output_aliases={5: 0},
        out_shape=[
            jax.ShapeDtypeStruct((rows, cols, hidden), BF16),
            jax.ShapeDtypeStruct((fields, hidden), F32),
            jax.ShapeDtypeStruct((9, hidden, hidden), F32),
            jax.ShapeDtypeStruct((9, hidden, hidden), F32),
        ],
        scratch_shapes=[
            pltpu.VMEM((2, half_rows, LANES), BF16),
            pltpu.VMEM((fields, hidden), F32),
            pltpu.VMEM((9, hidden, hidden), F32),
            pltpu.VMEM((9, hidden, hidden), F32),
            pltpu.SemaphoreType.DMA((4,)),
            pltpu.SemaphoreType.DMA((9,)),
            pltpu.SemaphoreType.DMA((9,)),
            pltpu.SemaphoreType.DMA,
        ],
        compiler_params=params,
        name="finish",
    )(mine, other, embed, first_weight, last_part, features)
    shape = (3, 3, hidden, hidden)
    return (features, grad_embed, grad_first.reshape(shape), grad_second.reshape(shape))


def solution(mesh):
    lat_count, lon_count = mesh.devices.shape
    inner = jax.sharding.Mesh(
        mesh.devices.reshape(lat_count, lon_count // 2, 2), ("lat", "ring", "core")
    )
    lon = ("ring", "core")
    in_specs = (
        P(None, "lat", lon),
        P("lat"),
        P("lat"),
        P(lon),
        P(lon),
        P(),
        P(),
        P(),
        P("lat", lon, None),
    )
    out_specs = (P("lat", lon, None), P(), P(), P())
    return jax.shard_map(
        on_device, mesh=inner, in_specs=in_specs, out_specs=out_specs, check_vma=False
    )
```

```python
import math

import jax
import jax.numpy as jnp
from jax import lax
from jax.experimental import pallas as pl
from jax.experimental.pallas import tpu as pltpu
from jax.sharding import PartitionSpec as P

F32 = jnp.float32
BF16 = jnp.bfloat16
LANES = 128
ROW_HALO = 3
COL_HALO = 4
SPAN = 16
GRAD_ROWS = 80
VMEM_BYTES = 24 * 1024 * 1024


def split_two(value):
    high = value.astype(BF16)
    return high, (value - high.astype(F32)).astype(BF16)


def prepare_kernel(
    cot_hbm, w2_hbm, w1_hbm, embed_hbm,
    shift_ref, back_ref, fore_ref, turned_ref, first_ref, cot_ref, w1_ref, padded_ref,
    w2_ref, embed_ref, line_ref, sems
):
    rows, cols, _ = cot_ref.shape
    wide = cols + 16
    pairs = rows // 2 + 1
    chunks = sems.shape[0] - 3
    share = rows // chunks
    weight_copy = pltpu.make_async_copy(w2_hbm, w2_ref, sems.at[chunks])
    weight_copy.start()
    copies = []
    for n in range(chunks):
        part = pl.ds(n * share, share)
        copies.append(pltpu.make_async_copy(cot_hbm.at[part], cot_ref.at[part], sems.at[n]))
        copies[-1].start()
    other_copy = pltpu.make_async_copy(w1_hbm, w1_ref, sems.at[chunks + 1])
    other_copy.start()
    embed_copy = pltpu.make_async_copy(embed_hbm, embed_ref, sems.at[chunks + 2])
    embed_copy.start()
    line_ref[...] = jnp.zeros_like(line_ref)
    back_ref[...] = jnp.zeros_like(back_ref)
    fore_ref[...] = jnp.zeros_like(fore_ref)
    blank = jnp.zeros((wide, LANES), BF16)
    for b in range(3):
        for parity in range(2):
            shift_ref[b, parity, 0:wide] = blank
            shift_ref[b, parity, pairs * wide : (pairs + 1) * wide] = blank
    weight_copy.wait()
    for a in range(3):
        for b in range(3):
            straight = w2_ref[a * 3 + b]
            turned = straight.astype(F32).T.astype(BF16)
            for q in range(2):
                column = slice(q * LANES, (q + 1) * LANES)
                at = (b * 4 + 2 + q - a) * LANES
                back_ref[at : at + LANES, column] = turned
                at = (b * 4 + a + q) * LANES
                fore_ref[at : at + LANES, column] = straight
    for r in range(rows):
        slot = r % 4
        if r % share == 0:
            copies[r // share].wait()
        line = cot_ref[r].astype(F32)
        line_ref[slot, 8 : 8 + cols] = line
        start = (r // 2 + 1) * wide
        for b in range(3):
            shift_ref[b, r % 2, start : start + wide] = line_ref[slot, 8 - b : 8 - b + wide].astype(BF16)
        turned_ref[(r % 2) * LANES : (r % 2 + 1) * LANES, (r // 2) * cols : (r // 2 + 1) * cols] = line.T.astype(BF16)
    embed_copy.wait()
    padded_ref[...] = padded_embed(embed_ref, line_ref)
    other_copy.wait()
    for tap in range(9):
        first_ref[tap * LANES : (tap + 1) * LANES] = w1_ref[tap].astype(F32).T.astype(BF16)


def edge_line(block, at):
    index = block[at : at + 1]
    return index, block[at + 1 : at + 2] + block[at + 2 : at + 3] + block[at + 3 : at + 4]


def joined_line(first, own, last, width):
    lane_count = 2 * LANES
    lane = lax.broadcasted_iota(jnp.int32, (1, lane_count), 1)
    out = []
    for part, shift in zip((first, own, last), (lane_count - width + 2, 2, width + 2)):
        part = jnp.concatenate([part[:, :width], jnp.zeros((1, lane_count - width), F32)], axis=1)
        out.append(pltpu.roll(jnp.broadcast_to(part, (8, lane_count)), shift, 1)[:1])
    return jnp.where(lane < 2, out[0], jnp.where(lane < width + 2, out[1], out[2]))


def row_blend(rsrc_ref, rfrac_ref, before_ref, after_ref, lat, lat_count, band_rows):
    rows = rsrc_ref.shape[1]
    cells = 2 * COL_HALO
    before_line = edge_line(before_ref[ROW_HALO].astype(F32), 0)
    after_line = edge_line(after_ref[ROW_HALO].astype(F32), 0)
    own_line = (rsrc_ref[...].astype(F32), rfrac_ref[...])
    src, frac = (
        joined_line(*lines, rows) for lines in zip(before_line, own_line, after_line)
    )
    spot = (src - (lat * band_rows - ROW_HALO).astype(F32)) * cells
    shape = (cells, LANES)
    at = lax.broadcasted_iota(jnp.int32, shape, 1) - lax.broadcasted_iota(jnp.int32, shape, 0)
    at = at.astype(F32)
    parts = []
    for q in range(rows + 4):
        here = jnp.broadcast_to(spot[:, q : q + 1], shape)
        f = jnp.broadcast_to(frac[:, q : q + 1], shape)
        part = jnp.where(at == here, 1.0 - f, 0.0) + jnp.where(at == here + cells, f, 0.0)
        if q < 2:
            part = part * jnp.where(lat > 0, 1.0, 0.0)
        elif q >= rows + 2:
            part = part * jnp.where(lat < lat_count - 1, 1.0, 0.0)
        parts.append(part)
    return jnp.concatenate(list(split_two(jnp.concatenate(parts, axis=0))), axis=1)


def blend_rows(matrix, cells):
    fill = jnp.zeros((LANES - sum(c.shape[0] for c in cells), LANES), F32)
    column = jnp.concatenate(list(cells) + [fill], axis=0).astype(BF16)
    return jnp.dot(matrix, jnp.concatenate([column, column], axis=0), preferred_element_type=F32)


def stacked(value):
    one, two = split_two(value)
    return jnp.concatenate([one, one, two], axis=0)


def lift_rows(mixed, embed):
    pair = jnp.concatenate(list(split_two(mixed)), axis=1)
    return jnp.dot(pair, jnp.concatenate([embed, embed], axis=0), preferred_element_type=F32)


def turned_rows(mixed, width):
    fill = jnp.zeros((width - mixed.shape[0], LANES), F32)
    turned = jnp.concatenate([mixed, fill], axis=0).T[:GRAD_ROWS]
    step = 2 * COL_HALO
    lines = [turned] + [pltpu.roll(turned, width - a * step, 1) for a in (1, 2)]
    return split_two(jnp.concatenate(lines, axis=0))


def tap_rows(lifted, w1_ref, cells):
    count = lifted.shape[0] - 2 * cells
    pairs = [split_two(lifted[a * cells : a * cells + count]) for a in range(3)]
    left = jnp.concatenate([p[0] for p in pairs] + [p[1] for p in pairs], axis=1)
    lines = [jnp.concatenate([w1_ref[a * 3 + b] for b in range(3)], axis=1) for a in range(3)]
    return jnp.dot(left, jnp.concatenate(lines + lines, axis=0), preferred_element_type=F32)


def blend_cols(src, frac, lon, band_cols, coarse_cols):
    shape = (SPAN, src.shape[1])
    local = jnp.broadcast_to(src, shape) - lon * band_cols
    frac = jnp.broadcast_to(frac, shape)
    local = jnp.where(local < -COL_HALO, local + coarse_cols, local)
    local = jnp.where(local >= band_cols + COL_HALO, local - coarse_cols, local)
    line = lax.broadcasted_iota(jnp.int32, shape, 0)

    def spot(at):
        east = jnp.where(at >= band_cols, at + COL_HALO, at)
        return jnp.where(at < 0, at + band_cols + COL_HALO, east)

    return jnp.where(line == spot(local), 1.0 - frac, 0.0) + jnp.where(
        line == spot(local + 1), frac, 0.0
    )


def back_kernel(
    rsrc_ref,
    rfrac_ref,
    shift_ref,
    weight_ref,
    before_ref,
    own_ref,
    after_ref,
    csrc_ref,
    cfrac_ref,
    embed_ref,
    w1_ref,
    cot_ref,
    bh_ref,
    rows_ref,
    lifted_ref,
    tap_ref,
    cot_col_ref,
    blend_ref,
    *,
    lat_count,
    coarse_cols,
):
    rows, cols, _ = cot_ref.shape
    wide = bh_ref.shape[1]
    pairs = bh_ref.shape[0] // 2
    band_rows, band_cols = own_ref.shape[0] - 1, own_ref.shape[1]
    step = 6
    for first in range(0, pairs, step):
        count = min(step, pairs - first)
        blocks = []
        for b in range(3):
            for i in range(4):
                start = (first + i // 2) * wide
                blocks.append(shift_ref[b, i % 2, start : start + count * wide])
        out = jnp.dot(jnp.concatenate(blocks, axis=1), weight_ref[...], preferred_element_type=F32)
        for m in range(count):
            for q in range(2):
                bh_ref[2 * (first + m) + q] = out[m * wide : (m + 1) * wide, q * LANES : (q + 1) * LANES]

    lat = lax.axis_index("lat")
    lon = lax.axis_index("ring") * 2 + lax.axis_index("core")
    matrix = row_blend(rsrc_ref, rfrac_ref, before_ref, after_ref, lat, lat_count, band_rows)
    blend_ref[...] = matrix
    cells = [before_ref[j] for j in range(ROW_HALO)] + [own_ref[j] for j in range(band_rows)]
    cells += [after_ref[j] for j in range(ROW_HALO)]
    mixed = blend_rows(matrix, [c.astype(F32) for c in cells])
    rows_ref[0], rows_ref[1] = turned_rows(mixed, rows_ref.shape[2])
    lifted = lift_rows(mixed, embed_ref[...])
    lifted_ref[...] = lifted
    tap_ref[...] = tap_rows(lifted, w1_ref, band_cols)

    blend = blend_cols(csrc_ref[...], cfrac_ref[...], lon, band_cols, coarse_cols)
    own_t = jnp.concatenate(list(split_two(blend)), axis=0)
    every = jnp.concatenate([cot_ref[r] for r in range(rows)], axis=1)
    back = jnp.dot(own_t, every, preferred_element_type=F32)
    back = back[:SPAN] + back[SPAN:]
    for r in range(rows):
        cot_col_ref[r] = back[:, r * LANES : (r + 1) * LANES]


def pack_kernel(cells_hbm, rsrc_hbm, rfrac_hbm, csrc_hbm, cfrac_hbm, *space):
    sources = (cells_hbm, rsrc_hbm, rfrac_hbm, csrc_hbm, cfrac_hbm)
    own_ref, outer_ref, inner_ref, *lines, cells_ref, out_ref, sems = space
    targets = (cells_ref, *lines)
    copies = [
        pltpu.make_async_copy(source, target, sems.at[n])
        for n, (source, target) in enumerate(zip(sources, targets))
    ]
    for copy in copies:
        copy.start()
    cells_ref, rsrc_ref, rfrac_ref, csrc_ref, cfrac_ref = targets
    depth, span, fields = cells_ref.shape
    out_ref[...] = jnp.zeros_like(out_ref)
    for copy in copies:
        copy.wait()
    for j in range(depth):
        out_ref[j, :, :fields] = cells_ref[j].astype(F32)
    at = 0
    for index_ref, fraction_ref in ((rsrc_ref, rfrac_ref), (csrc_ref, cfrac_ref)):
        width = index_ref.shape[1]
        fraction = fraction_ref[...]
        one = fraction.astype(BF16).astype(F32)
        two = (fraction - one).astype(BF16).astype(F32)
        for value in (index_ref[...].astype(F32), one, two, fraction - one - two):
            out_ref[depth, at : at + 1, :width] = value
            at += 1
    lat = lax.axis_index("lat")
    even = lax.rem(lat, 2) == 0
    own = [out_ref[j] for j in range(depth + 1)]
    to_next = own[depth - ROW_HALO :]
    to_last = own[:ROW_HALO] + own[depth:]
    for j in range(depth + 1):
        own_ref[j] = own[j].astype(BF16)
    for j in range(ROW_HALO + 1):
        outer_ref[j] = jnp.where(even, to_last[j], to_next[j]).astype(BF16)
        inner_ref[j] = jnp.where(even, to_next[j], to_last[j]).astype(BF16)


def main_kernel(
    far_ref,
    near_ref,
    csrc_ref,
    cfrac_ref,
    embed_ref,
    w1_ref,
    turned_ref,
    bh_ref,
    rows_ref,
    tap_ref,
    cot_col_ref,
    blend_ref,
    hid_ref,
    own_ref,
    side_lifted_ref,
    msg_ref,
    side_tap_ref,
    line_ref,
    right_ref,
    delta_ref,
    back_ref,
    *,
    lat_count,
    coarse_cols,
    band_cols,
):
    rows, cols = cot_col_ref.shape[0], own_ref.shape[0]
    wide = bh_ref.shape[1]
    pairs = bh_ref.shape[0] // 2
    depth = 2 * (far_ref.shape[0] - 1)
    half_rows = msg_ref.shape[1]
    lat = lax.axis_index("lat")
    core = lax.axis_index("core")
    lon = lax.axis_index("ring") * 2 + core
    taps = 3 * SPAN

    def send(at, value):
        side = lax.rem(at // half_rows + core, 2)
        at = at % half_rows
        msg_ref[side, at : at + value.shape[0]] = value.astype(BF16)

    sides = []
    for j in range(depth // 2 + 1):
        far, near = far_ref[j].astype(F32), near_ref[j].astype(F32)
        sides.append((jnp.where(core == 1, near, far), jnp.where(core == 1, far, near)))
    cells = []
    for j in range(depth):
        part = slice(j % 2 * COL_HALO, (j % 2 + 1) * COL_HALO)
        cells += [v[part] for v in sides[j // 2]]
    side_mixed = blend_rows(blend_ref[...], cells)
    side_lifted = lift_rows(side_mixed, embed_ref[...])
    side_lifted_ref[...] = side_lifted
    side_tap_ref[...] = tap_rows(side_lifted, w1_ref, band_cols)

    lane_count = 2 * LANES
    lane = lax.broadcasted_iota(jnp.int32, (1, lane_count), 1)
    west_line, east_line = (edge_line(v, 4) for v in sides[depth // 2])
    own_line = (csrc_ref[...].astype(F32), cfrac_ref[...])
    lines = [joined_line(*v, cols) for v in zip(west_line, own_line, east_line)]
    known = lane < cols + 4
    src = jnp.where(known, lines[0], -1e6).astype(jnp.int32)
    blend = blend_cols(src, jnp.where(known, lines[1], 0.0), lon, band_cols, coarse_cols)
    rolled = [blend] + [pltpu.roll(blend, lane_count - b, 1) for b in (1, 2)]
    stack = jnp.concatenate(rolled, axis=0)[:, :wide]
    high, low = split_two(stack)
    high_f, low_f = high.astype(F32), low.astype(F32)
    col_t = jnp.concatenate([high_f, low_f], axis=0).astype(BF16)
    col_lhs = jnp.concatenate([high_f.T, low_f.T, high_f.T], axis=1).astype(BF16)
    own_hi, own_lo = split_two(rolled[2][:, :cols])
    own_hi, own_lo = own_hi.astype(F32).T, own_lo.astype(F32).T
    own_ref[...] = jnp.concatenate([own_hi, own_lo, own_hi], axis=1).astype(BF16)

    for t in range(2 * pairs):
        part = slice(t * band_cols, (t + 1) * band_cols)
        blocks = []
        for b in range(3):
            column = slice(b * LANES, (b + 1) * LANES)
            blocks += [tap_ref[part, column], side_tap_ref[part, column]]
        right_ref[:, t * LANES : (t + 1) * LANES] = stacked(jnp.concatenate(blocks, axis=0))
    half = rows // 2 + 2
    spans = ((0, half), (half, 2 * pairs))
    cells_half = rows // 4 * cols

    def first_product(n):
        span = slice(spans[n][0] * LANES, spans[n][1] * LANES)
        return jnp.dot(col_lhs, right_ref[:, span], preferred_element_type=F32)

    def activate(pre, first, t):
        v = pre[:, (t - first) * LANES : (t - first + 1) * LANES]
        s = 0.5 + 0.5 * jnp.tanh(0.5 * v)
        if t == 0:
            s = s * jnp.where(lat > 0, 1.0, 0.0)
        elif t == 2 * pairs - 1:
            s = s * jnp.where(lat < lat_count - 1, 1.0, 0.0)
        h = v * s
        slope = s + h * (1.0 - s)
        line_ref[t] = h
        delta_ref[:, t * LANES : (t + 1) * LANES] = (bh_ref[t] * slope).astype(BF16)

    def place_hidden(t):
        at = (t // 2) * cols
        for b in range(3):
            hid_ref[b, t % 2, at : at + cols] = line_ref[t, b : b + cols].astype(BF16)

    def second_gradient(n, b):
        right = []
        for i in range(4):
            start = (i // 2) * cols + n * cells_half
            right.append(hid_ref[b, i % 2, start : start + cells_half])
        left = turned_ref[:, n * cells_half : (n + 1) * cells_half]
        return jnp.dot(left, jnp.concatenate(right, axis=1), preferred_element_type=F32)

    pre = first_product(0)
    for t in range(*spans[0]):
        activate(pre, 0, t)
    pre = first_product(1)
    for t in range(*spans[0]):
        place_hidden(t)
    grads = []
    rest = list(range(*spans[1]))
    share = -(-len(rest) // 3)
    for b in range(3):
        grads.append(second_gradient(0, b))
        for t in rest[b * share : (b + 1) * share]:
            activate(pre, spans[1][0], t)
            place_hidden(t)
    back = jnp.dot(col_t, delta_ref[...], preferred_element_type=F32)
    back = back[:taps] + back[taps:]
    width = rows_ref.shape[2]
    used = 2 * pairs * band_cols
    blank = jnp.zeros((2, width - used, back_ref.shape[2]), BF16)
    back_ref[:, used:width] = blank
    back_ref[:, width + used :] = blank
    nothing = jnp.zeros((SPAN, LANES), F32)

    def place_back(p):
        for b in range(4):
            lines = []
            for t in (2 * p, 2 * p + 1):
                if b < 3:
                    lines.append(back[b * SPAN : (b + 1) * SPAN, t * LANES : (t + 1) * LANES])
                else:
                    lines.append(cot_col_ref[t - 1] if 1 <= t <= rows else nothing)
            column = slice(b * LANES, (b + 1) * LANES)
            for side in range(2):
                cells = slice(side * band_cols, (side + 1) * band_cols)
                one, two = split_two(jnp.concatenate([v[cells] for v in lines], axis=0))
                at = side * width + p * SPAN
                back_ref[0, at : at + SPAN, column] = one
                back_ref[1, at : at + SPAN, column] = two

    def send_second(b):
        for a in range(3):
            upper = grads[b][:LANES, a * LANES : (a + 1) * LANES]
            lower = grads[b][LANES:, (a + 1) * LANES : (a + 2) * LANES]
            send((a * 3 + b) * LANES, (upper + lower).T)

    share = -(-pairs // 3)
    side_hi, side_lo = turned_rows(side_mixed, width)
    for b in range(3):
        grads[b] = grads[b] + second_gradient(1, b)
        for p in range(b * share, min((b + 1) * share, pairs)):
            place_back(p)
    upper = jnp.concatenate([rows_ref[0], side_hi], axis=1)
    lower = jnp.concatenate([rows_ref[1], side_lo], axis=1)
    g = jnp.dot(jnp.concatenate([upper, lower], axis=0), back_ref[0], preferred_element_type=F32)
    send_second(0)
    send_second(1)
    g = g[: 3 * GRAD_ROWS] + g[3 * GRAD_ROWS :]
    g = g + jnp.dot(upper, back_ref[1], preferred_element_type=F32)
    send_second(2)
    for a in range(3):
        line = g[a * GRAD_ROWS : (a + 1) * GRAD_ROWS]
        for b in range(3):
            send(9 * LANES + (a * 3 + b) * GRAD_ROWS, line[:, b * LANES : (b + 1) * LANES])
    send(9 * LANES + 9 * GRAD_ROWS, g[GRAD_ROWS : 2 * GRAD_ROWS, 3 * LANES:])
    tail = 9 * LANES + 10 * GRAD_ROWS
    if 2 * half_rows > tail:
        send(tail, jnp.zeros((2 * half_rows - tail, LANES), F32))


def join_kernel(own_ref, outer_ref, inner_ref, ready_ref, before_ref, after_ref, far_ref, near_ref):
    band_rows, band_cols = own_ref.shape[0] - 1, own_ref.shape[1]
    lat = lax.axis_index("lat")
    even = lax.rem(lat, 2) == 0
    first = lax.axis_index("core") == 0
    outer = [outer_ref[j].astype(F32) for j in range(ROW_HALO + 1)]
    inner = [inner_ref[j].astype(F32) for j in range(ROW_HALO + 1)]
    before = [jnp.where(even, v, w) for v, w in zip(outer, inner)]
    after = [jnp.where(even, w, v) for v, w in zip(outer, inner)]
    own = [own_ref[j].astype(F32) for j in range(band_rows + 1)]
    for j in range(ROW_HALO + 1):
        before_ref[j] = before[j].astype(BF16)
        after_ref[j] = after[j].astype(BF16)
    tall = before[:ROW_HALO] + own[:band_rows] + after[:ROW_HALO]
    for j in range(0, len(tall), 2):
        to_last = jnp.concatenate([v[:COL_HALO] for v in tall[j : j + 2]], axis=0)
        to_next = jnp.concatenate([v[band_cols - COL_HALO :] for v in tall[j : j + 2]], axis=0)
        far_ref[j // 2] = jnp.where(first, to_last, to_next).astype(BF16)
        near_ref[j // 2] = jnp.where(first, to_next, to_last).astype(BF16)
    far_ref[len(tall) // 2] = own[band_rows].astype(BF16)
    near_ref[len(tall) // 2] = own[band_rows].astype(BF16)


def features_kernel(weight_ref, hid_ref, own_ref, lifted_ref, side_lifted_ref, *refs, first):
    feat_ref = refs[-1]
    rows, cols, _ = feat_ref.shape
    cells = own_ref.shape[1] // 6
    step = 4
    for n in range(0, rows // 2, step):
        top = first + n
        blocks = []
        for b in range(3):
            for i in range(4):
                start = (top + i // 2) * cols
                blocks.append(hid_ref[b, i % 2, start : start + step * cols])
        out = jnp.dot(jnp.concatenate(blocks, axis=1), weight_ref[...], preferred_element_type=F32)
        right = []
        for r in range(2 * top, 2 * (top + step)):
            part = slice((r + 2) * cells, (r + 3) * cells)
            right.append(stacked(jnp.concatenate([lifted_ref[part], side_lifted_ref[part]], axis=0)))
        lift = jnp.dot(own_ref[...], jnp.concatenate(right, axis=1), preferred_element_type=F32)
        for m in range(step):
            for q in range(2):
                piece = out[m * cols : (m + 1) * cols, q * LANES : (q + 1) * LANES]
                own = lift[:, (2 * m + q) * LANES : (2 * m + q + 1) * LANES]
                feat_ref[2 * (n + m) + q] = (own + piece).astype(BF16)


def reduce_kernel(in_ref, out_ref):
    total = in_ref[0].astype(F32)
    for d in range(1, in_ref.shape[0]):
        total = total + in_ref[d].astype(F32)
    total = total.astype(BF16)
    for d in range(out_ref.shape[0]):
        out_ref[d] = total


def padded_embed(embed_ref, space_ref):
    fields = embed_ref.shape[0]
    space_ref[0, :LANES] = jnp.zeros((LANES, LANES), F32)
    space_ref[0, :fields] = embed_ref[...].astype(F32)
    return space_ref[0, :LANES].astype(BF16)


def last_kernel(
    mine_ref, near_ref, next_ref, embed_ref, first_ref, upper_ref, lower_ref, feat_hbm, ge_hbm, g1_hbm, g2_hbm,
    sum_ref, ge_ref, g1_ref, g2_ref, sems, *, scale
):
    core = lax.axis_index("core")
    half_rows = mine_ref.shape[0]
    copies = []

    def leave(source, target):
        copies.append(pltpu.make_async_copy(source, target, sems.at[len(copies)]))
        copies[-1].start()

    count = upper_ref.shape[0]
    leave(upper_ref, feat_hbm.at[pl.ds(0, count)])
    leave(lower_ref, feat_hbm.at[pl.ds(count, count)])
    sum_ref[core] = mine_ref[...]
    quarter = near_ref.shape[0]
    sum_ref[1 - core, :quarter] = near_ref[...]
    sum_ref[1 - core, quarter:] = next_ref[...]

    def read(at, count):
        return sum_ref[at // half_rows, at % half_rows : at % half_rows + count]

    for a in range(3):
        for tap in range(3 * a, 3 * a + 3):
            g2_ref[tap] = read(tap * LANES, LANES).astype(F32) * scale
        leave(g2_ref.at[pl.ds(3 * a, 3)], g2_hbm.at[pl.ds(3 * a, 3)])
    embed_t = embed_ref[...].astype(F32).T.astype(BF16)[:, :GRAD_ROWS]
    base = 9 * LANES
    g = jnp.concatenate([read(base + tap * GRAD_ROWS, GRAD_ROWS) for tap in range(9)], axis=1)
    for a in range(3):
        part = g[:, 3 * a * LANES : (3 * a + 3) * LANES]
        out = jnp.dot(embed_t, part, preferred_element_type=F32) * scale
        for b in range(3):
            g1_ref[3 * a + b] = out[:, b * LANES : (b + 1) * LANES]
        leave(g1_ref.at[pl.ds(3 * a, 3)], g1_hbm.at[pl.ds(3 * a, 3)])
    lift = read(base + 9 * GRAD_ROWS, GRAD_ROWS).astype(F32)
    lift = lift + jnp.dot(g, first_ref[...], preferred_element_type=F32)
    ge_ref[...] = lift[: ge_ref.shape[0]] * scale
    leave(ge_ref, ge_hbm)
    for copy in copies:
        copy.wait()


def from_hbm(value):
    return pltpu.with_memory_space_constraint(value, pltpu.HBM)


def on_device(
    coarse,
    row_src,
    row_frac,
    col_src,
    col_frac,
    embed_weight,
    conv1_weight,
    conv2_weight,
    cotangent,
):
    lat_count = lax.axis_size("lat")
    ring_count = lax.axis_size("ring")
    core_count = lax.axis_size("core")
    lon_count = ring_count * core_count
    fields, band_rows, band_cols = coarse.shape
    rows, cols, hidden = cotangent.shape
    group = lat_count * ring_count
    wide = cols + 16
    pairs = rows // 2 + 1
    depth = band_rows + 2 * ROW_HALO
    params = pltpu.CompilerParams(vmem_limit_bytes=VMEM_BYTES)
    vmem = pl.BlockSpec(memory_space=pltpu.VMEM)
    far = pl.BlockSpec(memory_space=pltpu.HBM)

    w1 = conv1_weight.reshape(9, hidden, hidden)
    w2 = conv2_weight.reshape(9, hidden, hidden)
    row_line = (row_src.reshape(1, rows), row_frac.reshape(1, rows))
    col_line = (col_src.reshape(1, cols), col_frac.reshape(1, cols))

    pack_inputs = (
        jnp.transpose(coarse, (1, 2, 0)),
        *row_line,
        *col_line,
    )
    own, to_outer, to_inner, *lines = pl.pallas_call(
        pack_kernel,
        in_specs=[far] * 5,
        out_shape=[jax.ShapeDtypeStruct((band_rows + 1, band_cols, LANES), BF16)]
        + [jax.ShapeDtypeStruct((ROW_HALO + 1, band_cols, LANES), BF16)] * 2
        + [jax.ShapeDtypeStruct(x.shape, x.dtype) for x in pack_inputs[1:]],
        scratch_shapes=[
            pltpu.VMEM(pack_inputs[0].shape, BF16),
            pltpu.VMEM((band_rows + 1, band_cols, LANES), F32),
            pltpu.SemaphoreType.DMA((5,)),
        ],
        compiler_params=params,
        name="pack",
    )(*(from_hbm(x) for x in pack_inputs))
    row_line, col_line = lines[:2], lines[2:]
    inner = [(i, i ^ 1) for i in range(lat_count)]
    outer = [(i, i + 1) for i in range(1, lat_count - 1, 2)]
    outer = outer + [(j, i) for i, j in outer]
    got_outer = lax.ppermute(to_outer, "lat", outer)
    got_inner = lax.ppermute(to_inner, "lat", inner)

    shift, back_weight, fore_weight, turned, first_weight, cot, near_w1, embed = pl.pallas_call(
        prepare_kernel,
        out_shape=[
            jax.ShapeDtypeStruct((3, 2, (pairs + 1) * wide, hidden), BF16),
            jax.ShapeDtypeStruct((12 * hidden, 2 * hidden), BF16),
            jax.ShapeDtypeStruct((12 * hidden, 2 * hidden), BF16),
            jax.ShapeDtypeStruct((2 * hidden, rows // 2 * cols), BF16),
            jax.ShapeDtypeStruct((9 * hidden, hidden), BF16),
            jax.ShapeDtypeStruct((rows, cols, hidden), BF16),
            jax.ShapeDtypeStruct((9, hidden, hidden), BF16),
            jax.ShapeDtypeStruct((LANES, hidden), BF16),
        ],
        in_specs=[far] * 4,
        scratch_shapes=[
            pltpu.VMEM((9, hidden, hidden), BF16),
            pltpu.VMEM((fields, hidden), BF16),
            pltpu.VMEM((4, wide + 16, hidden), F32),
            pltpu.SemaphoreType.DMA((11,)),
        ],
        compiler_params=params,
        name="prepare",
    )(from_hbm(cotangent), from_hbm(w2), from_hbm(w1), from_hbm(embed_weight))
    before, after, far_message, near_message = pl.pallas_call(
        join_kernel,
        out_shape=[jax.ShapeDtypeStruct((ROW_HALO + 1, band_cols, LANES), BF16)] * 2
        + [jax.ShapeDtypeStruct((depth // 2 + 1, band_cols, LANES), BF16)] * 2,
        compiler_params=params,
        name="join",
    )(own, got_outer, got_inner, embed)
    lon = ("ring", "core")
    inner = [(i, i ^ 1) for i in range(lon_count)]
    outer = [(i, (i + (1 if i % 2 else -1)) % lon_count) for i in range(lon_count)]
    got_far = lax.ppermute(far_message, lon, outer)
    got_near = lax.ppermute(near_message, lon, inner)

    def back_body(*refs):
        back_kernel(*refs, lat_count=lat_count, coarse_cols=band_cols * lon_count)

    reach = rows + 4
    width = -(-reach * band_cols // LANES) * LANES
    bh, mixed, lifted, tap, cot_col, blend = pl.pallas_call(
        back_body,
        out_shape=[
            jax.ShapeDtypeStruct((2 * pairs, wide, hidden), F32),
            jax.ShapeDtypeStruct((2, 3 * GRAD_ROWS, width), BF16),
            jax.ShapeDtypeStruct((reach * band_cols, hidden), F32),
            jax.ShapeDtypeStruct(((reach - 2) * band_cols, 3 * hidden), F32),
            jax.ShapeDtypeStruct((rows, SPAN, hidden), F32),
            jax.ShapeDtypeStruct((reach * band_cols, 2 * LANES), BF16),
        ],
        compiler_params=params,
        name="back_hidden",
    )(
        *row_line, shift, back_weight, before, own, after, *col_line,
        embed, near_w1, cot,
    )

    blocks = 9 * LANES + 10 * GRAD_ROWS
    chunk = -(-blocks // (core_count * group * 16)) * 16
    half_rows = max(group * chunk, -(-blocks // (2 * LANES)) * LANES)

    def body(*refs):
        main_kernel(
            *refs,
            lat_count=lat_count,
            coarse_cols=band_cols * lon_count,
            band_cols=band_cols,
        )

    hid, own_blend, side_lifted, message = pl.pallas_call(
        body,
        out_specs=[vmem] * 4,
        out_shape=[
            jax.ShapeDtypeStruct((3, 2, pairs * cols, hidden), BF16),
            jax.ShapeDtypeStruct((cols, 3 * SPAN), BF16),
            jax.ShapeDtypeStruct((reach * band_cols, hidden), F32),
            jax.ShapeDtypeStruct((2, half_rows, LANES), BF16),
        ],
        scratch_shapes=[
            pltpu.VMEM(((reach - 2) * band_cols, 3 * hidden), F32),
            pltpu.VMEM((2 * pairs, wide, hidden), F32),
            pltpu.VMEM((9 * SPAN, 2 * pairs * hidden), BF16),
            pltpu.VMEM((wide, 2 * pairs * hidden), BF16),
            pltpu.VMEM((2, 2 * width, 4 * hidden), BF16),
        ],
        compiler_params=params,
        name="tile",
    )(
        got_far, got_near, *col_line,
        embed, near_w1, turned, bh, mixed, tap, cot_col, blend,
    )

    def half_features(first, *arrays):
        def body(*refs):
            features_kernel(*refs, first=first)

        return pl.pallas_call(
            body,
            out_shape=jax.ShapeDtypeStruct((rows // 2, cols, hidden), BF16),
            compiler_params=params,
            name=f"features_{first}",
        )(*arrays)

    swap = [(0, 1), (1, 0)]
    quarter = half_rows // 2

    def swapped(value):
        return [lax.ppermute(v, "core", swap) for v in (value[:quarter], value[quarter:])]

    received = swapped(message[1])
    middle = rows // 4
    part = half_features(0, fore_weight, hid, own_blend, lifted, side_lifted)
    *received, part = lax.optimization_barrier((*received, part))
    received = jnp.concatenate(received)
    pair = (message[0].astype(F32) + received.astype(F32)).astype(BF16)
    axes = ("lat", "ring")
    chunk = half_rows // group
    parts = lax.all_to_all(pair, axes, 0, 0, tiled=True)
    copies = pl.pallas_call(
        reduce_kernel,
        out_shape=jax.ShapeDtypeStruct((group, chunk, LANES), BF16),
        compiler_params=params,
        name="sum_chunks",
    )(parts.reshape(group, chunk, LANES))
    mine = lax.all_to_all(copies.reshape(half_rows, LANES), axes, 0, 0, tiled=True)
    other = swapped(mine)
    last_part = half_features(middle, fore_weight, hid, own_blend, lifted, side_lifted, mine)
    scale = 1.0 / math.sqrt(rows * lat_count * cols * lon_count)

    def finish(*refs):
        last_kernel(*refs, scale=scale)

    features, grad_embed, grad_first, grad_second = pl.pallas_call(
        finish,
        out_specs=[far] * 4,
        out_shape=[
            jax.ShapeDtypeStruct((rows, cols, hidden), BF16),
            jax.ShapeDtypeStruct((fields, hidden), F32),
            jax.ShapeDtypeStruct((9, hidden, hidden), F32),
            jax.ShapeDtypeStruct((9, hidden, hidden), F32),
        ],
        scratch_shapes=[
            pltpu.VMEM((2, half_rows, LANES), BF16),
            pltpu.VMEM((fields, hidden), F32),
            pltpu.VMEM((9, hidden, hidden), F32),
            pltpu.VMEM((9, hidden, hidden), F32),
            pltpu.SemaphoreType.DMA((9,)),
        ],
        compiler_params=params,
        name="finish",
    )(mine, *other, embed, first_weight, part, last_part)
    shape = (3, 3, hidden, hidden)
    return (features, grad_embed, grad_first.reshape(shape), grad_second.reshape(shape))


def solution(mesh):
    lat_count, lon_count = mesh.devices.shape
    inner = jax.sharding.Mesh(
        mesh.devices.reshape(lat_count, lon_count // 2, 2), ("lat", "ring", "core")
    )
    lon = ("ring", "core")
    in_specs = (
        P(None, "lat", lon),
        P("lat"),
        P("lat"),
        P(lon),
        P(lon),
        P(),
        P(),
        P(),
        P("lat", lon, None),
    )
    out_specs = (P("lat", lon, None), P(), P(), P())
    return jax.shard_map(
        on_device, mesh=inner, in_specs=in_specs, out_specs=out_specs, check_vma=False
    )
```

```python
import math

import jax
import jax.numpy as jnp
from jax import lax
from jax.experimental import pallas as pl
from jax.experimental.pallas import tpu as pltpu
from jax.sharding import PartitionSpec as P

F32 = jnp.float32
BF16 = jnp.bfloat16
LANES = 128
ROW_HALO = 3
COL_HALO = 4
SPAN = 16
GRAD_ROWS = 80
VMEM_BYTES = 24 * 1024 * 1024


def split_two(value):
    high = value.astype(BF16)
    return high, (value - high.astype(F32)).astype(BF16)


def prepare_kernel(
    cot_hbm, w2_hbm, w1_hbm, embed_hbm,
    shift_ref, back_ref, fore_ref, turned_ref, first_ref, cot_ref, w1_ref, padded_ref,
    w2_ref, embed_ref, line_ref, sems
):
    rows, cols, _ = cot_ref.shape
    wide = cols + 16
    pairs = rows // 2 + 1
    chunks = sems.shape[0] - 3
    share = rows // chunks
    weight_copy = pltpu.make_async_copy(w2_hbm, w2_ref, sems.at[chunks])
    weight_copy.start()
    copies = []
    for n in range(chunks):
        part = pl.ds(n * share, share)
        copies.append(pltpu.make_async_copy(cot_hbm.at[part], cot_ref.at[part], sems.at[n]))
        copies[-1].start()
    other_copy = pltpu.make_async_copy(w1_hbm, w1_ref, sems.at[chunks + 1])
    other_copy.start()
    embed_copy = pltpu.make_async_copy(embed_hbm, embed_ref, sems.at[chunks + 2])
    embed_copy.start()
    line_ref[...] = jnp.zeros_like(line_ref)
    back_ref[...] = jnp.zeros_like(back_ref)
    fore_ref[...] = jnp.zeros_like(fore_ref)
    blank = jnp.zeros((wide, LANES), BF16)
    for b in range(3):
        for parity in range(2):
            shift_ref[b, parity, 0:wide] = blank
            shift_ref[b, parity, pairs * wide : (pairs + 1) * wide] = blank
    weight_copy.wait()
    for a in range(3):
        for b in range(3):
            straight = w2_ref[a * 3 + b]
            turned = straight.astype(F32).T.astype(BF16)
            for q in range(2):
                column = slice(q * LANES, (q + 1) * LANES)
                at = (b * 4 + 2 + q - a) * LANES
                back_ref[at : at + LANES, column] = turned
                at = (b * 4 + a + q) * LANES
                fore_ref[at : at + LANES, column] = straight
    for r in range(rows):
        slot = r % 4
        if r % share == 0:
            copies[r // share].wait()
        line = cot_ref[r].astype(F32)
        line_ref[slot, 8 : 8 + cols] = line
        start = (r // 2 + 1) * wide
        for b in range(3):
            shift_ref[b, r % 2, start : start + wide] = line_ref[slot, 8 - b : 8 - b + wide].astype(BF16)
        turned_ref[(r % 2) * LANES : (r % 2 + 1) * LANES, (r // 2) * cols : (r // 2 + 1) * cols] = line.T.astype(BF16)
    embed_copy.wait()
    padded_ref[...] = padded_embed(embed_ref, line_ref)
    other_copy.wait()
    for tap in range(9):
        first_ref[tap * LANES : (tap + 1) * LANES] = w1_ref[tap].astype(F32).T.astype(BF16)


def edge_line(block, at):
    index = block[at : at + 1]
    return index, block[at + 1 : at + 2] + block[at + 2 : at + 3] + block[at + 3 : at + 4]


def joined_line(first, own, last, width):
    lane_count = 2 * LANES
    lane = lax.broadcasted_iota(jnp.int32, (1, lane_count), 1)
    out = []
    for part, shift in zip((first, own, last), (lane_count - width + 2, 2, width + 2)):
        part = jnp.concatenate([part[:, :width], jnp.zeros((1, lane_count - width), F32)], axis=1)
        out.append(pltpu.roll(jnp.broadcast_to(part, (8, lane_count)), shift, 1)[:1])
    return jnp.where(lane < 2, out[0], jnp.where(lane < width + 2, out[1], out[2]))


def row_blend(rsrc_ref, rfrac_ref, before_ref, after_ref, lat, lat_count, band_rows):
    rows = rsrc_ref.shape[1]
    cells = 2 * COL_HALO
    before_line = edge_line(before_ref[ROW_HALO].astype(F32), 0)
    after_line = edge_line(after_ref[ROW_HALO].astype(F32), 0)
    own_line = (rsrc_ref[...].astype(F32), rfrac_ref[...])
    src, frac = (
        joined_line(*lines, rows) for lines in zip(before_line, own_line, after_line)
    )
    spot = (src - (lat * band_rows - ROW_HALO).astype(F32)) * cells
    shape = (cells, LANES)
    at = lax.broadcasted_iota(jnp.int32, shape, 1) - lax.broadcasted_iota(jnp.int32, shape, 0)
    at = at.astype(F32)
    parts = []
    for q in range(rows + 4):
        here = jnp.broadcast_to(spot[:, q : q + 1], shape)
        f = jnp.broadcast_to(frac[:, q : q + 1], shape)
        part = jnp.where(at == here, 1.0 - f, 0.0) + jnp.where(at == here + cells, f, 0.0)
        if q < 2:
            part = part * jnp.where(lat > 0, 1.0, 0.0)
        elif q >= rows + 2:
            part = part * jnp.where(lat < lat_count - 1, 1.0, 0.0)
        parts.append(part)
    return jnp.concatenate(list(split_two(jnp.concatenate(parts, axis=0))), axis=1)


def blend_rows(matrix, cells):
    fill = jnp.zeros((LANES - sum(c.shape[0] for c in cells), LANES), F32)
    column = jnp.concatenate(list(cells) + [fill], axis=0).astype(BF16)
    return jnp.dot(matrix, jnp.concatenate([column, column], axis=0), preferred_element_type=F32)


def stacked(value):
    one, two = split_two(value)
    return jnp.concatenate([one, one, two], axis=0)


def lift_rows(mixed, embed):
    pair = jnp.concatenate(list(split_two(mixed)), axis=1)
    return jnp.dot(pair, jnp.concatenate([embed, embed], axis=0), preferred_element_type=F32)


def turned_rows(mixed, width):
    fill = jnp.zeros((width - mixed.shape[0], LANES), F32)
    turned = jnp.concatenate([mixed, fill], axis=0).T[:GRAD_ROWS]
    step = 2 * COL_HALO
    lines = [turned] + [pltpu.roll(turned, width - a * step, 1) for a in (1, 2)]
    return split_two(jnp.concatenate(lines, axis=0))


def tap_rows(lifted, w1_ref, cells):
    count = lifted.shape[0] - 2 * cells
    pairs = [split_two(lifted[a * cells : a * cells + count]) for a in range(3)]
    left = jnp.concatenate([p[0] for p in pairs] + [p[1] for p in pairs], axis=1)
    lines = [jnp.concatenate([w1_ref[a * 3 + b] for b in range(3)], axis=1) for a in range(3)]
    return jnp.dot(left, jnp.concatenate(lines + lines, axis=0), preferred_element_type=F32)


def blend_cols(src, frac, lon, band_cols, coarse_cols):
    shape = (SPAN, src.shape[1])
    local = jnp.broadcast_to(src, shape) - lon * band_cols
    frac = jnp.broadcast_to(frac, shape)
    local = jnp.where(local < -COL_HALO, local + coarse_cols, local)
    local = jnp.where(local >= band_cols + COL_HALO, local - coarse_cols, local)
    line = lax.broadcasted_iota(jnp.int32, shape, 0)

    def spot(at):
        east = jnp.where(at >= band_cols, at + COL_HALO, at)
        return jnp.where(at < 0, at + band_cols + COL_HALO, east)

    return jnp.where(line == spot(local), 1.0 - frac, 0.0) + jnp.where(
        line == spot(local + 1), frac, 0.0
    )


def back_kernel(
    rsrc_ref,
    rfrac_ref,
    shift_ref,
    weight_ref,
    before_ref,
    own_ref,
    after_ref,
    csrc_ref,
    cfrac_ref,
    embed_ref,
    w1_ref,
    cot_ref,
    bh_ref,
    rows_ref,
    lifted_ref,
    tap_ref,
    cot_col_ref,
    blend_ref,
    *,
    lat_count,
    coarse_cols,
):
    rows, cols, _ = cot_ref.shape
    wide = bh_ref.shape[1]
    pairs = bh_ref.shape[0] // 2
    band_rows, band_cols = own_ref.shape[0] - 1, own_ref.shape[1]
    step = 6
    for first in range(0, pairs, step):
        count = min(step, pairs - first)
        blocks = []
        for b in range(3):
            for i in range(4):
                start = (first + i // 2) * wide
                blocks.append(shift_ref[b, i % 2, start : start + count * wide])
        out = jnp.dot(jnp.concatenate(blocks, axis=1), weight_ref[...], preferred_element_type=F32)
        for m in range(count):
            for q in range(2):
                bh_ref[2 * (first + m) + q] = out[m * wide : (m + 1) * wide, q * LANES : (q + 1) * LANES]

    lat = lax.axis_index("lat")
    lon = lax.axis_index("ring") * 2 + lax.axis_index("core")
    matrix = row_blend(rsrc_ref, rfrac_ref, before_ref, after_ref, lat, lat_count, band_rows)
    blend_ref[...] = matrix
    cells = [before_ref[j] for j in range(ROW_HALO)] + [own_ref[j] for j in range(band_rows)]
    cells += [after_ref[j] for j in range(ROW_HALO)]
    mixed = blend_rows(matrix, [c.astype(F32) for c in cells])
    rows_ref[0], rows_ref[1] = turned_rows(mixed, rows_ref.shape[2])
    lifted = lift_rows(mixed, embed_ref[...])
    lifted_ref[...] = lifted
    tap_ref[...] = tap_rows(lifted, w1_ref, band_cols)

    blend = blend_cols(csrc_ref[...], cfrac_ref[...], lon, band_cols, coarse_cols)
    own_t = jnp.concatenate(list(split_two(blend)), axis=0)
    every = jnp.concatenate([cot_ref[r] for r in range(rows)], axis=1)
    back = jnp.dot(own_t, every, preferred_element_type=F32)
    back = back[:SPAN] + back[SPAN:]
    for r in range(rows):
        cot_col_ref[r] = back[:, r * LANES : (r + 1) * LANES]


def pack_kernel(cells_hbm, rsrc_hbm, rfrac_hbm, csrc_hbm, cfrac_hbm, *space):
    sources = (cells_hbm, rsrc_hbm, rfrac_hbm, csrc_hbm, cfrac_hbm)
    own_ref, outer_ref, inner_ref, *lines, cells_ref, out_ref, sems = space
    targets = (cells_ref, *lines)
    copies = [
        pltpu.make_async_copy(source, target, sems.at[n])
        for n, (source, target) in enumerate(zip(sources, targets))
    ]
    for copy in copies:
        copy.start()
    cells_ref, rsrc_ref, rfrac_ref, csrc_ref, cfrac_ref = targets
    depth, span, fields = cells_ref.shape
    out_ref[...] = jnp.zeros_like(out_ref)
    for copy in copies:
        copy.wait()
    for j in range(depth):
        out_ref[j, :, :fields] = cells_ref[j].astype(F32)
    at = 0
    for index_ref, fraction_ref in ((rsrc_ref, rfrac_ref), (csrc_ref, cfrac_ref)):
        width = index_ref.shape[1]
        fraction = fraction_ref[...]
        one = fraction.astype(BF16).astype(F32)
        two = (fraction - one).astype(BF16).astype(F32)
        for value in (index_ref[...].astype(F32), one, two, fraction - one - two):
            out_ref[depth, at : at + 1, :width] = value
            at += 1
    lat = lax.axis_index("lat")
    even = lax.rem(lat, 2) == 0
    own = [out_ref[j] for j in range(depth + 1)]
    to_next = own[depth - ROW_HALO :]
    to_last = own[:ROW_HALO] + own[depth:]
    for j in range(depth + 1):
        own_ref[j] = own[j].astype(BF16)
    for j in range(ROW_HALO + 1):
        outer_ref[j] = jnp.where(even, to_last[j], to_next[j]).astype(BF16)
        inner_ref[j] = jnp.where(even, to_next[j], to_last[j]).astype(BF16)


def main_kernel(
    far_ref,
    near_ref,
    csrc_ref,
    cfrac_ref,
    embed_ref,
    w1_ref,
    turned_ref,
    bh_ref,
    rows_ref,
    tap_ref,
    cot_col_ref,
    blend_ref,
    hid_ref,
    own_ref,
    side_lifted_ref,
    msg_ref,
    side_tap_ref,
    line_ref,
    right_ref,
    delta_ref,
    back_ref,
    *,
    lat_count,
    coarse_cols,
    band_cols,
):
    rows, cols = cot_col_ref.shape[0], own_ref.shape[0]
    wide = bh_ref.shape[1]
    pairs = bh_ref.shape[0] // 2
    depth = 2 * (far_ref.shape[0] - 1)
    half_rows = msg_ref.shape[1]
    lat = lax.axis_index("lat")
    core = lax.axis_index("core")
    lon = lax.axis_index("ring") * 2 + core
    taps = 3 * SPAN

    def send(at, value):
        side = lax.rem(at // half_rows + core, 2)
        at = at % half_rows
        msg_ref[side, at : at + value.shape[0]] = value.astype(BF16)

    sides = []
    for j in range(depth // 2 + 1):
        far, near = far_ref[j].astype(F32), near_ref[j].astype(F32)
        sides.append((jnp.where(core == 1, near, far), jnp.where(core == 1, far, near)))
    cells = []
    for j in range(depth):
        part = slice(j % 2 * COL_HALO, (j % 2 + 1) * COL_HALO)
        cells += [v[part] for v in sides[j // 2]]
    side_mixed = blend_rows(blend_ref[...], cells)
    side_lifted = lift_rows(side_mixed, embed_ref[...])
    side_lifted_ref[...] = side_lifted
    side_tap_ref[...] = tap_rows(side_lifted, w1_ref, band_cols)

    lane_count = 2 * LANES
    lane = lax.broadcasted_iota(jnp.int32, (1, lane_count), 1)
    west_line, east_line = (edge_line(v, 4) for v in sides[depth // 2])
    own_line = (csrc_ref[...].astype(F32), cfrac_ref[...])
    lines = [joined_line(*v, cols) for v in zip(west_line, own_line, east_line)]
    known = lane < cols + 4
    src = jnp.where(known, lines[0], -1e6).astype(jnp.int32)
    blend = blend_cols(src, jnp.where(known, lines[1], 0.0), lon, band_cols, coarse_cols)
    rolled = [blend] + [pltpu.roll(blend, lane_count - b, 1) for b in (1, 2)]
    stack = jnp.concatenate(rolled, axis=0)[:, :wide]
    high, low = split_two(stack)
    high_f, low_f = high.astype(F32), low.astype(F32)
    col_t = jnp.concatenate([high_f, low_f], axis=0).astype(BF16)
    col_lhs = jnp.concatenate([high_f.T, low_f.T, high_f.T], axis=1).astype(BF16)
    own_hi, own_lo = split_two(rolled[2][:, :cols])
    own_hi, own_lo = own_hi.astype(F32).T, own_lo.astype(F32).T
    own_ref[...] = jnp.concatenate([own_hi, own_lo, own_hi], axis=1).astype(BF16)

    for t in range(2 * pairs):
        part = slice(t * band_cols, (t + 1) * band_cols)
        blocks = []
        for b in range(3):
            column = slice(b * LANES, (b + 1) * LANES)
            blocks += [tap_ref[part, column], side_tap_ref[part, column]]
        right_ref[:, t * LANES : (t + 1) * LANES] = stacked(jnp.concatenate(blocks, axis=0))
    half = rows // 2 + 2
    spans = ((0, half), (half, 2 * pairs))

    def first_product(n):
        span = slice(spans[n][0] * LANES, spans[n][1] * LANES)
        return jnp.dot(col_lhs, right_ref[:, span], preferred_element_type=F32)

    def activate(pre, first, t):
        v = pre[:, (t - first) * LANES : (t - first + 1) * LANES]
        s = 0.5 + 0.5 * jnp.tanh(0.5 * v)
        if t == 0:
            s = s * jnp.where(lat > 0, 1.0, 0.0)
        elif t == 2 * pairs - 1:
            s = s * jnp.where(lat < lat_count - 1, 1.0, 0.0)
        h = v * s
        slope = s + h * (1.0 - s)
        line_ref[t] = h
        delta_ref[:, t * LANES : (t + 1) * LANES] = (bh_ref[t] * slope).astype(BF16)

    def place_hidden(t):
        at = (t // 2) * cols
        for b in range(3):
            hid_ref[b, t % 2, at : at + cols] = line_ref[t, b : b + cols].astype(BF16)

    def second_gradient(b):
        right = []
        for i in range(4):
            start = (i // 2) * cols
            right.append(hid_ref[b, i % 2, start : start + rows // 2 * cols])
        return jnp.dot(turned_ref[...], jnp.concatenate(right, axis=1), preferred_element_type=F32)

    pre = first_product(0)
    for t in range(*spans[0]):
        activate(pre, 0, t)
    pre = first_product(1)
    for t in range(*spans[0]):
        place_hidden(t)
    for t in range(*spans[1]):
        activate(pre, spans[1][0], t)
        place_hidden(t)
    back = jnp.dot(col_t, delta_ref[...], preferred_element_type=F32)
    back = back[:taps] + back[taps:]
    grads = []

    width = rows_ref.shape[2]
    used = 2 * pairs * band_cols
    blank = jnp.zeros((2, width - used, back_ref.shape[2]), BF16)
    back_ref[:, used:width] = blank
    back_ref[:, width + used :] = blank
    nothing = jnp.zeros((SPAN, LANES), F32)

    def place_back(p):
        for b in range(4):
            lines = []
            for t in (2 * p, 2 * p + 1):
                if b < 3:
                    lines.append(back[b * SPAN : (b + 1) * SPAN, t * LANES : (t + 1) * LANES])
                else:
                    lines.append(cot_col_ref[t - 1] if 1 <= t <= rows else nothing)
            column = slice(b * LANES, (b + 1) * LANES)
            for side in range(2):
                cells = slice(side * band_cols, (side + 1) * band_cols)
                one, two = split_two(jnp.concatenate([v[cells] for v in lines], axis=0))
                at = side * width + p * SPAN
                back_ref[0, at : at + SPAN, column] = one
                back_ref[1, at : at + SPAN, column] = two

    def send_second(b):
        for a in range(3):
            upper = grads[b][:LANES, a * LANES : (a + 1) * LANES]
            lower = grads[b][LANES:, (a + 1) * LANES : (a + 2) * LANES]
            send((a * 3 + b) * LANES, (upper + lower).T)

    share = -(-pairs // 3)
    side_hi, side_lo = turned_rows(side_mixed, width)
    for b in range(3):
        grads.append(second_gradient(b))
        for p in range(b * share, min((b + 1) * share, pairs)):
            place_back(p)
    upper = jnp.concatenate([rows_ref[0], side_hi], axis=1)
    lower = jnp.concatenate([rows_ref[1], side_lo], axis=1)
    g = jnp.dot(jnp.concatenate([upper, lower], axis=0), back_ref[0], preferred_element_type=F32)
    send_second(0)
    send_second(1)
    g = g[: 3 * GRAD_ROWS] + g[3 * GRAD_ROWS :]
    g = g + jnp.dot(upper, back_ref[1], preferred_element_type=F32)
    send_second(2)
    for a in range(3):
        line = g[a * GRAD_ROWS : (a + 1) * GRAD_ROWS]
        for b in range(3):
            send(9 * LANES + (a * 3 + b) * GRAD_ROWS, line[:, b * LANES : (b + 1) * LANES])
    send(9 * LANES + 9 * GRAD_ROWS, g[GRAD_ROWS : 2 * GRAD_ROWS, 3 * LANES:])
    tail = 9 * LANES + 10 * GRAD_ROWS
    if 2 * half_rows > tail:
        send(tail, jnp.zeros((2 * half_rows - tail, LANES), F32))


def join_kernel(own_ref, outer_ref, inner_ref, ready_ref, before_ref, after_ref, far_ref, near_ref):
    band_rows, band_cols = own_ref.shape[0] - 1, own_ref.shape[1]
    lat = lax.axis_index("lat")
    even = lax.rem(lat, 2) == 0
    first = lax.axis_index("core") == 0
    outer = [outer_ref[j].astype(F32) for j in range(ROW_HALO + 1)]
    inner = [inner_ref[j].astype(F32) for j in range(ROW_HALO + 1)]
    before = [jnp.where(even, v, w) for v, w in zip(outer, inner)]
    after = [jnp.where(even, w, v) for v, w in zip(outer, inner)]
    own = [own_ref[j].astype(F32) for j in range(band_rows + 1)]
    for j in range(ROW_HALO + 1):
        before_ref[j] = before[j].astype(BF16)
        after_ref[j] = after[j].astype(BF16)
    tall = before[:ROW_HALO] + own[:band_rows] + after[:ROW_HALO]
    for j in range(0, len(tall), 2):
        to_last = jnp.concatenate([v[:COL_HALO] for v in tall[j : j + 2]], axis=0)
        to_next = jnp.concatenate([v[band_cols - COL_HALO :] for v in tall[j : j + 2]], axis=0)
        far_ref[j // 2] = jnp.where(first, to_last, to_next).astype(BF16)
        near_ref[j // 2] = jnp.where(first, to_next, to_last).astype(BF16)
    far_ref[len(tall) // 2] = own[band_rows].astype(BF16)
    near_ref[len(tall) // 2] = own[band_rows].astype(BF16)


def features_kernel(weight_ref, hid_ref, own_ref, lifted_ref, side_lifted_ref, *refs, first):
    feat_ref = refs[-1]
    rows, cols, _ = feat_ref.shape
    cells = own_ref.shape[1] // 6
    step = 4
    for n in range(0, rows // 2, step):
        top = first + n
        blocks = []
        for b in range(3):
            for i in range(4):
                start = (top + i // 2) * cols
                blocks.append(hid_ref[b, i % 2, start : start + step * cols])
        out = jnp.dot(jnp.concatenate(blocks, axis=1), weight_ref[...], preferred_element_type=F32)
        right = []
        for r in range(2 * top, 2 * (top + step)):
            part = slice((r + 2) * cells, (r + 3) * cells)
            right.append(stacked(jnp.concatenate([lifted_ref[part], side_lifted_ref[part]], axis=0)))
        lift = jnp.dot(own_ref[...], jnp.concatenate(right, axis=1), preferred_element_type=F32)
        for m in range(step):
            for q in range(2):
                piece = out[m * cols : (m + 1) * cols, q * LANES : (q + 1) * LANES]
                own = lift[:, (2 * m + q) * LANES : (2 * m + q + 1) * LANES]
                feat_ref[2 * (n + m) + q] = (own + piece).astype(BF16)


def reduce_kernel(in_ref, out_ref):
    total = in_ref[0].astype(F32)
    for d in range(1, in_ref.shape[0]):
        total = total + in_ref[d].astype(F32)
    total = total.astype(BF16)
    for d in range(out_ref.shape[0]):
        out_ref[d] = total


def padded_embed(embed_ref, space_ref):
    fields = embed_ref.shape[0]
    space_ref[0, :LANES] = jnp.zeros((LANES, LANES), F32)
    space_ref[0, :fields] = embed_ref[...].astype(F32)
    return space_ref[0, :LANES].astype(BF16)


def last_kernel(
    mine_ref, other_ref, embed_ref, first_ref, upper_ref, lower_ref, feat_hbm, ge_hbm, g1_hbm, g2_hbm,
    sum_ref, ge_ref, g1_ref, g2_ref, sems, *, scale
):
    core = lax.axis_index("core")
    half_rows = mine_ref.shape[0]
    copies = []

    def leave(source, target):
        copies.append(pltpu.make_async_copy(source, target, sems.at[len(copies)]))
        copies[-1].start()

    count = upper_ref.shape[0]
    leave(upper_ref, feat_hbm.at[pl.ds(0, count)])
    leave(lower_ref, feat_hbm.at[pl.ds(count, count)])
    sum_ref[core] = mine_ref[...]
    sum_ref[1 - core] = other_ref[...]

    def read(at, count):
        return sum_ref[at // half_rows, at % half_rows : at % half_rows + count]

    for a in range(3):
        for tap in range(3 * a, 3 * a + 3):
            g2_ref[tap] = read(tap * LANES, LANES).astype(F32) * scale
        leave(g2_ref.at[pl.ds(3 * a, 3)], g2_hbm.at[pl.ds(3 * a, 3)])
    embed_t = embed_ref[...].astype(F32).T.astype(BF16)[:, :GRAD_ROWS]
    base = 9 * LANES
    g = jnp.concatenate([read(base + tap * GRAD_ROWS, GRAD_ROWS) for tap in range(9)], axis=1)
    for a in range(3):
        part = g[:, 3 * a * LANES : (3 * a + 3) * LANES]
        out = jnp.dot(embed_t, part, preferred_element_type=F32) * scale
        for b in range(3):
            g1_ref[3 * a + b] = out[:, b * LANES : (b + 1) * LANES]
        leave(g1_ref.at[pl.ds(3 * a, 3)], g1_hbm.at[pl.ds(3 * a, 3)])
    lift = read(base + 9 * GRAD_ROWS, GRAD_ROWS).astype(F32)
    lift = lift + jnp.dot(g, first_ref[...], preferred_element_type=F32)
    ge_ref[...] = lift[: ge_ref.shape[0]] * scale
    leave(ge_ref, ge_hbm)
    for copy in copies:
        copy.wait()


def from_hbm(value):
    return pltpu.with_memory_space_constraint(value, pltpu.HBM)


def on_device(
    coarse,
    row_src,
    row_frac,
    col_src,
    col_frac,
    embed_weight,
    conv1_weight,
    conv2_weight,
    cotangent,
):
    lat_count = lax.axis_size("lat")
    ring_count = lax.axis_size("ring")
    core_count = lax.axis_size("core")
    lon_count = ring_count * core_count
    fields, band_rows, band_cols = coarse.shape
    rows, cols, hidden = cotangent.shape
    group = lat_count * ring_count
    wide = cols + 16
    pairs = rows // 2 + 1
    depth = band_rows + 2 * ROW_HALO
    params = pltpu.CompilerParams(vmem_limit_bytes=VMEM_BYTES)
    vmem = pl.BlockSpec(memory_space=pltpu.VMEM)
    far = pl.BlockSpec(memory_space=pltpu.HBM)

    w1 = conv1_weight.reshape(9, hidden, hidden)
    w2 = conv2_weight.reshape(9, hidden, hidden)
    row_line = (row_src.reshape(1, rows), row_frac.reshape(1, rows))
    col_line = (col_src.reshape(1, cols), col_frac.reshape(1, cols))

    pack_inputs = (
        jnp.transpose(coarse, (1, 2, 0)),
        *row_line,
        *col_line,
    )
    own, to_outer, to_inner, *lines = pl.pallas_call(
        pack_kernel,
        in_specs=[far] * 5,
        out_shape=[jax.ShapeDtypeStruct((band_rows + 1, band_cols, LANES), BF16)]
        + [jax.ShapeDtypeStruct((ROW_HALO + 1, band_cols, LANES), BF16)] * 2
        + [jax.ShapeDtypeStruct(x.shape, x.dtype) for x in pack_inputs[1:]],
        scratch_shapes=[
            pltpu.VMEM(pack_inputs[0].shape, BF16),
            pltpu.VMEM((band_rows + 1, band_cols, LANES), F32),
            pltpu.SemaphoreType.DMA((5,)),
        ],
        compiler_params=params,
        name="pack",
    )(*(from_hbm(x) for x in pack_inputs))
    row_line, col_line = lines[:2], lines[2:]
    inner = [(i, i ^ 1) for i in range(lat_count)]
    outer = [(i, i + 1) for i in range(1, lat_count - 1, 2)]
    outer = outer + [(j, i) for i, j in outer]
    got_outer = lax.ppermute(to_outer, "lat", outer)
    got_inner = lax.ppermute(to_inner, "lat", inner)

    shift, back_weight, fore_weight, turned, first_weight, cot, near_w1, embed = pl.pallas_call(
        prepare_kernel,
        out_shape=[
            jax.ShapeDtypeStruct((3, 2, (pairs + 1) * wide, hidden), BF16),
            jax.ShapeDtypeStruct((12 * hidden, 2 * hidden), BF16),
            jax.ShapeDtypeStruct((12 * hidden, 2 * hidden), BF16),
            jax.ShapeDtypeStruct((2 * hidden, rows // 2 * cols), BF16),
            jax.ShapeDtypeStruct((9 * hidden, hidden), BF16),
            jax.ShapeDtypeStruct((rows, cols, hidden), BF16),
            jax.ShapeDtypeStruct((9, hidden, hidden), BF16),
            jax.ShapeDtypeStruct((LANES, hidden), BF16),
        ],
        in_specs=[far] * 4,
        scratch_shapes=[
            pltpu.VMEM((9, hidden, hidden), BF16),
            pltpu.VMEM((fields, hidden), BF16),
            pltpu.VMEM((4, wide + 16, hidden), F32),
            pltpu.SemaphoreType.DMA((11,)),
        ],
        compiler_params=params,
        name="prepare",
    )(from_hbm(cotangent), from_hbm(w2), from_hbm(w1), from_hbm(embed_weight))
    before, after, far_message, near_message = pl.pallas_call(
        join_kernel,
        out_shape=[jax.ShapeDtypeStruct((ROW_HALO + 1, band_cols, LANES), BF16)] * 2
        + [jax.ShapeDtypeStruct((depth // 2 + 1, band_cols, LANES), BF16)] * 2,
        compiler_params=params,
        name="join",
    )(own, got_outer, got_inner, embed)
    lon = ("ring", "core")
    inner = [(i, i ^ 1) for i in range(lon_count)]
    outer = [(i, (i + (1 if i % 2 else -1)) % lon_count) for i in range(lon_count)]
    got_far = lax.ppermute(far_message, lon, outer)
    got_near = lax.ppermute(near_message, lon, inner)

    def back_body(*refs):
        back_kernel(*refs, lat_count=lat_count, coarse_cols=band_cols * lon_count)

    reach = rows + 4
    width = -(-reach * band_cols // LANES) * LANES
    bh, mixed, lifted, tap, cot_col, blend = pl.pallas_call(
        back_body,
        out_shape=[
            jax.ShapeDtypeStruct((2 * pairs, wide, hidden), F32),
            jax.ShapeDtypeStruct((2, 3 * GRAD_ROWS, width), BF16),
            jax.ShapeDtypeStruct((reach * band_cols, hidden), F32),
            jax.ShapeDtypeStruct(((reach - 2) * band_cols, 3 * hidden), F32),
            jax.ShapeDtypeStruct((rows, SPAN, hidden), F32),
            jax.ShapeDtypeStruct((reach * band_cols, 2 * LANES), BF16),
        ],
        compiler_params=params,
        name="back_hidden",
    )(
        *row_line, shift, back_weight, before, own, after, *col_line,
        embed, near_w1, cot,
    )

    blocks = 9 * LANES + 10 * GRAD_ROWS
    chunk = -(-blocks // (core_count * group * 16)) * 16
    half_rows = max(group * chunk, -(-blocks // (2 * LANES)) * LANES)

    def body(*refs):
        main_kernel(
            *refs,
            lat_count=lat_count,
            coarse_cols=band_cols * lon_count,
            band_cols=band_cols,
        )

    hid, own_blend, side_lifted, message = pl.pallas_call(
        body,
        out_specs=[vmem] * 4,
        out_shape=[
            jax.ShapeDtypeStruct((3, 2, pairs * cols, hidden), BF16),
            jax.ShapeDtypeStruct((cols, 3 * SPAN), BF16),
            jax.ShapeDtypeStruct((reach * band_cols, hidden), F32),
            jax.ShapeDtypeStruct((2, half_rows, LANES), BF16),
        ],
        scratch_shapes=[
            pltpu.VMEM(((reach - 2) * band_cols, 3 * hidden), F32),
            pltpu.VMEM((2 * pairs, wide, hidden), F32),
            pltpu.VMEM((9 * SPAN, 2 * pairs * hidden), BF16),
            pltpu.VMEM((wide, 2 * pairs * hidden), BF16),
            pltpu.VMEM((2, 2 * width, 4 * hidden), BF16),
        ],
        compiler_params=params,
        name="tile",
    )(
        got_far, got_near, *col_line,
        embed, near_w1, turned, bh, mixed, tap, cot_col, blend,
    )

    def half_features(first, *arrays):
        def body(*refs):
            features_kernel(*refs, first=first)

        return pl.pallas_call(
            body,
            out_shape=jax.ShapeDtypeStruct((rows // 2, cols, hidden), BF16),
            compiler_params=params,
            name=f"features_{first}",
        )(*arrays)

    swap = [(0, 1), (1, 0)]
    received = lax.ppermute(message[1], "core", swap)
    middle = rows // 4
    part = half_features(0, fore_weight, hid, own_blend, lifted, side_lifted)
    received, part = lax.optimization_barrier((received, part))
    pair = (message[0].astype(F32) + received.astype(F32)).astype(BF16)
    axes = ("lat", "ring")
    chunk = half_rows // group
    parts = lax.all_to_all(pair, axes, 0, 0, tiled=True)
    copies = pl.pallas_call(
        reduce_kernel,
        out_shape=jax.ShapeDtypeStruct((group, chunk, LANES), BF16),
        compiler_params=params,
        name="sum_chunks",
    )(parts.reshape(group, chunk, LANES))
    mine = lax.all_to_all(copies.reshape(half_rows, LANES), axes, 0, 0, tiled=True)
    other = lax.ppermute(mine, "core", swap)
    last_part = half_features(middle, fore_weight, hid, own_blend, lifted, side_lifted, mine)
    scale = 1.0 / math.sqrt(rows * lat_count * cols * lon_count)

    def finish(*refs):
        last_kernel(*refs, scale=scale)

    features, grad_embed, grad_first, grad_second = pl.pallas_call(
        finish,
        out_specs=[far] * 4,
        out_shape=[
            jax.ShapeDtypeStruct((rows, cols, hidden), BF16),
            jax.ShapeDtypeStruct((fields, hidden), F32),
            jax.ShapeDtypeStruct((9, hidden, hidden), F32),
            jax.ShapeDtypeStruct((9, hidden, hidden), F32),
        ],
        scratch_shapes=[
            pltpu.VMEM((2, half_rows, LANES), BF16),
            pltpu.VMEM((fields, hidden), F32),
            pltpu.VMEM((9, hidden, hidden), F32),
            pltpu.VMEM((9, hidden, hidden), F32),
            pltpu.SemaphoreType.DMA((9,)),
        ],
        compiler_params=params,
        name="finish",
    )(mine, other, embed, first_weight, part, last_part)
    shape = (3, 3, hidden, hidden)
    return (features, grad_embed, grad_first.reshape(shape), grad_second.reshape(shape))


def solution(mesh):
    lat_count, lon_count = mesh.devices.shape
    inner = jax.sharding.Mesh(
        mesh.devices.reshape(lat_count, lon_count // 2, 2), ("lat", "ring", "core")
    )
    lon = ("ring", "core")
    in_specs = (
        P(None, "lat", lon),
        P("lat"),
        P("lat"),
        P(lon),
        P(lon),
        P(),
        P(),
        P(),
        P("lat", lon, None),
    )
    out_specs = (P("lat", lon, None), P(), P(), P())
    return jax.shard_map(
        on_device, mesh=inner, in_specs=in_specs, out_specs=out_specs, check_vma=False
    )
```

```python
import math

import jax
import jax.numpy as jnp
from jax import lax
from jax.experimental import pallas as pl
from jax.experimental.pallas import tpu as pltpu
from jax.sharding import PartitionSpec as P

F32 = jnp.float32
BF16 = jnp.bfloat16
LANES = 128
ROW_HALO = 3
COL_HALO = 4
SPAN = 16
GRAD_ROWS = 80
VMEM_BYTES = 24 * 1024 * 1024


def split_two(value):
    high = value.astype(BF16)
    return high, (value - high.astype(F32)).astype(BF16)


def back_rows(shift_ref, weight_ref, out_ref, start_pair):
    wide = out_ref.shape[1]
    pairs = out_ref.shape[0] // 2
    step = 7
    for first in range(0, pairs, step):
        count = min(step, pairs - first)
        blocks = []
        for b in range(3):
            for i in range(4):
                start = (start_pair + first + i // 2) * wide
                blocks.append(shift_ref[b, i % 2, start : start + count * wide])
        out = jnp.dot(jnp.concatenate(blocks, axis=1), weight_ref[...], preferred_element_type=F32)
        for m in range(count):
            for q in range(2):
                out_ref[2 * (first + m) + q] = out[m * wide : (m + 1) * wide, q * LANES : (q + 1) * LANES]


def prepare_kernel(
    cot_hbm, w2_hbm, w1_hbm, embed_hbm,
    shift_ref, back_ref, turned_ref, cot_ref, w1_ref, w2_ref, padded_ref, begun_ref,
    embed_ref, line_ref, sems
):
    rows, cols, _ = cot_ref.shape
    wide = cols + 16
    pairs = rows // 2 + 1
    chunks = sems.shape[0] - 3
    share = rows // chunks
    weight_copy = pltpu.make_async_copy(w2_hbm, w2_ref, sems.at[chunks])
    weight_copy.start()
    copies = []
    for n in range(chunks):
        part = pl.ds(n * share, share)
        copies.append(pltpu.make_async_copy(cot_hbm.at[part], cot_ref.at[part], sems.at[n]))
        copies[-1].start()
    other_copy = pltpu.make_async_copy(w1_hbm, w1_ref, sems.at[chunks + 1])
    other_copy.start()
    embed_copy = pltpu.make_async_copy(embed_hbm, embed_ref, sems.at[chunks + 2])
    embed_copy.start()
    line_ref[...] = jnp.zeros_like(line_ref)
    back_ref[...] = jnp.zeros_like(back_ref)
    blank = jnp.zeros((wide, LANES), BF16)
    for b in range(3):
        for parity in range(2):
            shift_ref[b, parity, 0:wide] = blank
            shift_ref[b, parity, pairs * wide : (pairs + 1) * wide] = blank
    weight_copy.wait()
    for a in range(3):
        for b in range(3):
            turned = w2_ref[a * 3 + b].astype(F32).T.astype(BF16)
            for q in range(2):
                at = (b * 4 + 2 + q - a) * LANES
                back_ref[at : at + LANES, q * LANES : (q + 1) * LANES] = turned
    for r in range(rows):
        slot = r % 4
        if r % share == 0:
            copies[r // share].wait()
        line = cot_ref[r].astype(F32)
        line_ref[slot, 8 : 8 + cols] = line
        start = (r // 2 + 1) * wide
        for b in range(3):
            shift_ref[b, r % 2, start : start + wide] = line_ref[slot, 8 - b : 8 - b + wide].astype(BF16)
        turned_ref[(r % 2) * LANES : (r % 2 + 1) * LANES, (r // 2) * cols : (r // 2 + 1) * cols] = line.T.astype(BF16)
    embed_copy.wait()
    padded_ref[...] = padded_embed(embed_ref, line_ref)
    other_copy.wait()
    back_rows(shift_ref, back_ref, begun_ref, 0)


def edge_line(block, at):
    index = block[at : at + 1]
    return index, block[at + 1 : at + 2] + block[at + 2 : at + 3] + block[at + 3 : at + 4]


def joined_line(first, own, last, width):
    lane_count = 2 * LANES
    lane = lax.broadcasted_iota(jnp.int32, (1, lane_count), 1)
    out = []
    for part, shift in zip((first, own, last), (lane_count - width + 2, 2, width + 2)):
        part = jnp.concatenate([part[:, :width], jnp.zeros((1, lane_count - width), F32)], axis=1)
        out.append(pltpu.roll(jnp.broadcast_to(part, (8, lane_count)), shift, 1)[:1])
    return jnp.where(lane < 2, out[0], jnp.where(lane < width + 2, out[1], out[2]))


def row_blend(rsrc_ref, rfrac_ref, before_ref, after_ref, lat, lat_count, band_rows):
    rows = rsrc_ref.shape[1]
    cells = 2 * COL_HALO
    before_line = edge_line(before_ref[ROW_HALO].astype(F32), 0)
    after_line = edge_line(after_ref[ROW_HALO].astype(F32), 0)
    own_line = (rsrc_ref[...].astype(F32), rfrac_ref[...])
    src, frac = (
        joined_line(*lines, rows) for lines in zip(before_line, own_line, after_line)
    )
    spot = (src - (lat * band_rows - ROW_HALO).astype(F32)) * cells
    shape = (cells, LANES)
    at = lax.broadcasted_iota(jnp.int32, shape, 1) - lax.broadcasted_iota(jnp.int32, shape, 0)
    at = at.astype(F32)
    parts = []
    for q in range(rows + 4):
        here = jnp.broadcast_to(spot[:, q : q + 1], shape)
        f = jnp.broadcast_to(frac[:, q : q + 1], shape)
        part = jnp.where(at == here, 1.0 - f, 0.0) + jnp.where(at == here + cells, f, 0.0)
        if q < 2:
            part = part * jnp.where(lat > 0, 1.0, 0.0)
        elif q >= rows + 2:
            part = part * jnp.where(lat < lat_count - 1, 1.0, 0.0)
        parts.append(part)
    return jnp.concatenate(list(split_two(jnp.concatenate(parts, axis=0))), axis=1)


def blend_rows(matrix, cells):
    fill = jnp.zeros((LANES - sum(c.shape[0] for c in cells), LANES), F32)
    column = jnp.concatenate(list(cells) + [fill], axis=0).astype(BF16)
    return jnp.dot(matrix, jnp.concatenate([column, column], axis=0), preferred_element_type=F32)


def stacked(value):
    one, two = split_two(value)
    return jnp.concatenate([one, one, two], axis=0)


def lift_rows(mixed, embed):
    pair = jnp.concatenate(list(split_two(mixed)), axis=1)
    return jnp.dot(pair, jnp.concatenate([embed, embed], axis=0), preferred_element_type=F32)


def turned_rows(mixed, width):
    fill = jnp.zeros((width - mixed.shape[0], LANES), F32)
    turned = jnp.concatenate([mixed, fill], axis=0).T[:GRAD_ROWS]
    step = 2 * COL_HALO
    lines = [turned] + [pltpu.roll(turned, width - a * step, 1) for a in (1, 2)]
    return split_two(jnp.concatenate(lines, axis=0))


def tap_rows(lifted, w1_ref, cells):
    count = lifted.shape[0] - 2 * cells
    pairs = [split_two(lifted[a * cells : a * cells + count]) for a in range(3)]
    left = jnp.concatenate([p[0] for p in pairs] + [p[1] for p in pairs], axis=1)
    lines = [jnp.concatenate([w1_ref[a * 3 + b] for b in range(3)], axis=1) for a in range(3)]
    return jnp.dot(left, jnp.concatenate(lines + lines, axis=0), preferred_element_type=F32)


def blend_cols(src, frac, lon, band_cols, coarse_cols):
    shape = (SPAN, src.shape[1])
    local = jnp.broadcast_to(src, shape) - lon * band_cols
    frac = jnp.broadcast_to(frac, shape)
    local = jnp.where(local < -COL_HALO, local + coarse_cols, local)
    local = jnp.where(local >= band_cols + COL_HALO, local - coarse_cols, local)
    line = lax.broadcasted_iota(jnp.int32, shape, 0)

    def spot(at):
        east = jnp.where(at >= band_cols, at + COL_HALO, at)
        return jnp.where(at < 0, at + band_cols + COL_HALO, east)

    return jnp.where(line == spot(local), 1.0 - frac, 0.0) + jnp.where(
        line == spot(local + 1), frac, 0.0
    )


def back_kernel(
    rsrc_ref,
    rfrac_ref,
    shift_ref,
    weight_ref,
    before_ref,
    own_ref,
    after_ref,
    csrc_ref,
    cfrac_ref,
    embed_ref,
    w1_ref,
    cot_ref,
    bh_ref,
    rows_ref,
    lifted_ref,
    tap_ref,
    cot_col_ref,
    blend_ref,
    *,
    lat_count,
    coarse_cols,
):
    rows, cols, _ = cot_ref.shape
    band_rows, band_cols = own_ref.shape[0] - 1, own_ref.shape[1]
    back_rows(shift_ref, weight_ref, bh_ref, rows // 2 + 1 - bh_ref.shape[0] // 2)

    lat = lax.axis_index("lat")
    lon = lax.axis_index("ring") * 2 + lax.axis_index("core")
    matrix = row_blend(rsrc_ref, rfrac_ref, before_ref, after_ref, lat, lat_count, band_rows)
    blend_ref[...] = matrix
    cells = [before_ref[j] for j in range(ROW_HALO)] + [own_ref[j] for j in range(band_rows)]
    cells += [after_ref[j] for j in range(ROW_HALO)]
    mixed = blend_rows(matrix, [c.astype(F32) for c in cells])
    rows_ref[0], rows_ref[1] = turned_rows(mixed, rows_ref.shape[2])
    lifted = lift_rows(mixed, embed_ref[...])
    lifted_ref[...] = lifted
    tap_ref[...] = tap_rows(lifted, w1_ref, band_cols)

    blend = blend_cols(csrc_ref[...], cfrac_ref[...], lon, band_cols, coarse_cols)
    own_t = jnp.concatenate(list(split_two(blend)), axis=0)
    every = jnp.concatenate([cot_ref[r] for r in range(rows)], axis=1)
    back = jnp.dot(own_t, every, preferred_element_type=F32)
    back = back[:SPAN] + back[SPAN:]
    for r in range(rows):
        cot_col_ref[r] = back[:, r * LANES : (r + 1) * LANES]


def pack_kernel(cells_hbm, rsrc_hbm, rfrac_hbm, csrc_hbm, cfrac_hbm, *space):
    sources = (cells_hbm, rsrc_hbm, rfrac_hbm, csrc_hbm, cfrac_hbm)
    own_ref, outer_ref, inner_ref, *lines, cells_ref, out_ref, sems = space
    targets = (cells_ref, *lines)
    copies = [
        pltpu.make_async_copy(source, target, sems.at[n])
        for n, (source, target) in enumerate(zip(sources, targets))
    ]
    for copy in copies:
        copy.start()
    cells_ref, rsrc_ref, rfrac_ref, csrc_ref, cfrac_ref = targets
    depth, span, fields = cells_ref.shape
    out_ref[...] = jnp.zeros_like(out_ref)
    for copy in copies:
        copy.wait()
    for j in range(depth):
        out_ref[j, :, :fields] = cells_ref[j].astype(F32)
    at = 0
    for index_ref, fraction_ref in ((rsrc_ref, rfrac_ref), (csrc_ref, cfrac_ref)):
        width = index_ref.shape[1]
        fraction = fraction_ref[...]
        one = fraction.astype(BF16).astype(F32)
        two = (fraction - one).astype(BF16).astype(F32)
        for value in (index_ref[...].astype(F32), one, two, fraction - one - two):
            out_ref[depth, at : at + 1, :width] = value
            at += 1
    lat = lax.axis_index("lat")
    even = lax.rem(lat, 2) == 0
    own = [out_ref[j] for j in range(depth + 1)]
    to_next = own[depth - ROW_HALO :]
    to_last = own[:ROW_HALO] + own[depth:]
    for j in range(depth + 1):
        own_ref[j] = own[j].astype(BF16)
    for j in range(ROW_HALO + 1):
        outer_ref[j] = jnp.where(even, to_last[j], to_next[j]).astype(BF16)
        inner_ref[j] = jnp.where(even, to_next[j], to_last[j]).astype(BF16)


def main_kernel(
    far_ref,
    near_ref,
    csrc_ref,
    cfrac_ref,
    embed_ref,
    w1_ref,
    turned_ref,
    begun_ref,
    bh_ref,
    rows_ref,
    tap_ref,
    cot_col_ref,
    blend_ref,
    hid_ref,
    own_ref,
    side_lifted_ref,
    msg_ref,
    side_tap_ref,
    line_ref,
    right_ref,
    delta_ref,
    back_ref,
    *,
    lat_count,
    coarse_cols,
    band_cols,
):
    rows, cols = cot_col_ref.shape[0], own_ref.shape[0]
    wide = bh_ref.shape[1]
    begun = begun_ref.shape[0]
    pairs = (begun + bh_ref.shape[0]) // 2
    depth = 2 * (far_ref.shape[0] - 1)
    half_rows = msg_ref.shape[1]
    lat = lax.axis_index("lat")
    core = lax.axis_index("core")
    lon = lax.axis_index("ring") * 2 + core
    taps = 3 * SPAN

    def send(at, value):
        side = lax.rem(at // half_rows + core, 2)
        at = at % half_rows
        msg_ref[side, at : at + value.shape[0]] = value.astype(BF16)

    sides = []
    for j in range(depth // 2 + 1):
        far, near = far_ref[j].astype(F32), near_ref[j].astype(F32)
        sides.append((jnp.where(core == 1, near, far), jnp.where(core == 1, far, near)))
    cells = []
    for j in range(depth):
        part = slice(j % 2 * COL_HALO, (j % 2 + 1) * COL_HALO)
        cells += [v[part] for v in sides[j // 2]]
    side_mixed = blend_rows(blend_ref[...], cells)
    side_lifted = lift_rows(side_mixed, embed_ref[...])
    side_lifted_ref[...] = side_lifted
    side_tap_ref[...] = tap_rows(side_lifted, w1_ref, band_cols)

    lane_count = 2 * LANES
    lane = lax.broadcasted_iota(jnp.int32, (1, lane_count), 1)
    west_line, east_line = (edge_line(v, 4) for v in sides[depth // 2])
    own_line = (csrc_ref[...].astype(F32), cfrac_ref[...])
    lines = [joined_line(*v, cols) for v in zip(west_line, own_line, east_line)]
    known = lane < cols + 4
    src = jnp.where(known, lines[0], -1e6).astype(jnp.int32)
    blend = blend_cols(src, jnp.where(known, lines[1], 0.0), lon, band_cols, coarse_cols)
    rolled = [blend] + [pltpu.roll(blend, lane_count - b, 1) for b in (1, 2)]
    stack = jnp.concatenate(rolled, axis=0)[:, :wide]
    high, low = split_two(stack)
    high_f, low_f = high.astype(F32), low.astype(F32)
    col_t = jnp.concatenate([high_f, low_f], axis=0).astype(BF16)
    col_lhs = jnp.concatenate([high_f.T, low_f.T, high_f.T], axis=1).astype(BF16)
    own_hi, own_lo = split_two(rolled[2][:, :cols])
    own_hi, own_lo = own_hi.astype(F32).T, own_lo.astype(F32).T
    own_ref[...] = jnp.concatenate([own_hi, own_lo, own_hi], axis=1).astype(BF16)

    for t in range(2 * pairs):
        part = slice(t * band_cols, (t + 1) * band_cols)
        blocks = []
        for b in range(3):
            column = slice(b * LANES, (b + 1) * LANES)
            blocks += [tap_ref[part, column], side_tap_ref[part, column]]
        right_ref[:, t * LANES : (t + 1) * LANES] = stacked(jnp.concatenate(blocks, axis=0))
    half = rows // 2 + 2
    spans = ((0, half), (half, 2 * pairs))

    def first_product(n):
        span = slice(spans[n][0] * LANES, spans[n][1] * LANES)
        return jnp.dot(col_lhs, right_ref[:, span], preferred_element_type=F32)

    def activate(pre, first, t):
        v = pre[:, (t - first) * LANES : (t - first + 1) * LANES]
        s = 0.5 + 0.5 * jnp.tanh(0.5 * v)
        if t == 0:
            s = s * jnp.where(lat > 0, 1.0, 0.0)
        elif t == 2 * pairs - 1:
            s = s * jnp.where(lat < lat_count - 1, 1.0, 0.0)
        h = v * s
        slope = s + h * (1.0 - s)
        line_ref[t] = h
        arrived = begun_ref[t] if t < begun else bh_ref[t - begun]
        delta_ref[:, t * LANES : (t + 1) * LANES] = (arrived * slope).astype(BF16)

    def place_hidden(t):
        at = (t // 2) * cols
        for b in range(3):
            hid_ref[b, t % 2, at : at + cols] = line_ref[t, b : b + cols].astype(BF16)

    def second_gradient(b):
        right = []
        for i in range(4):
            start = (i // 2) * cols
            right.append(hid_ref[b, i % 2, start : start + rows // 2 * cols])
        return jnp.dot(turned_ref[...], jnp.concatenate(right, axis=1), preferred_element_type=F32)

    pre = first_product(0)
    for t in range(*spans[0]):
        activate(pre, 0, t)
    pre = first_product(1)
    for t in range(*spans[0]):
        place_hidden(t)
    for t in range(*spans[1]):
        activate(pre, spans[1][0], t)
        place_hidden(t)
    back = jnp.dot(col_t, delta_ref[...], preferred_element_type=F32)
    back = back[:taps] + back[taps:]
    grads = []

    width = rows_ref.shape[2]
    used = 2 * pairs * band_cols
    blank = jnp.zeros((2, width - used, back_ref.shape[2]), BF16)
    back_ref[:, used:width] = blank
    back_ref[:, width + used :] = blank
    nothing = jnp.zeros((SPAN, LANES), F32)

    def place_back(p):
        for b in range(4):
            lines = []
            for t in (2 * p, 2 * p + 1):
                if b < 3:
                    lines.append(back[b * SPAN : (b + 1) * SPAN, t * LANES : (t + 1) * LANES])
                else:
                    lines.append(cot_col_ref[t - 1] if 1 <= t <= rows else nothing)
            column = slice(b * LANES, (b + 1) * LANES)
            for side in range(2):
                cells = slice(side * band_cols, (side + 1) * band_cols)
                one, two = split_two(jnp.concatenate([v[cells] for v in lines], axis=0))
                at = side * width + p * SPAN
                back_ref[0, at : at + SPAN, column] = one
                back_ref[1, at : at + SPAN, column] = two

    def send_second(b):
        for a in range(3):
            upper = grads[b][:LANES, a * LANES : (a + 1) * LANES]
            lower = grads[b][LANES:, (a + 1) * LANES : (a + 2) * LANES]
            send((a * 3 + b) * LANES, (upper + lower).T)

    share = -(-pairs // 3)
    side_hi, side_lo = turned_rows(side_mixed, width)
    for b in range(3):
        grads.append(second_gradient(b))
        for p in range(b * share, min((b + 1) * share, pairs)):
            place_back(p)
    upper = jnp.concatenate([rows_ref[0], side_hi], axis=1)
    lower = jnp.concatenate([rows_ref[1], side_lo], axis=1)
    g = jnp.dot(jnp.concatenate([upper, lower], axis=0), back_ref[0], preferred_element_type=F32)
    send_second(0)
    send_second(1)
    g = g[: 3 * GRAD_ROWS] + g[3 * GRAD_ROWS :]
    g = g + jnp.dot(upper, back_ref[1], preferred_element_type=F32)
    send_second(2)
    for a in range(3):
        line = g[a * GRAD_ROWS : (a + 1) * GRAD_ROWS]
        for b in range(3):
            send(9 * LANES + (a * 3 + b) * GRAD_ROWS, line[:, b * LANES : (b + 1) * LANES])
    send(9 * LANES + 9 * GRAD_ROWS, g[GRAD_ROWS : 2 * GRAD_ROWS, 3 * LANES:])
    tail = 9 * LANES + 10 * GRAD_ROWS
    if 2 * half_rows > tail:
        send(tail, jnp.zeros((2 * half_rows - tail, LANES), F32))


def join_kernel(own_ref, outer_ref, inner_ref, ready_ref, before_ref, after_ref, far_ref, near_ref):
    band_rows, band_cols = own_ref.shape[0] - 1, own_ref.shape[1]
    lat = lax.axis_index("lat")
    even = lax.rem(lat, 2) == 0
    first = lax.axis_index("core") == 0
    outer = [outer_ref[j].astype(F32) for j in range(ROW_HALO + 1)]
    inner = [inner_ref[j].astype(F32) for j in range(ROW_HALO + 1)]
    before = [jnp.where(even, v, w) for v, w in zip(outer, inner)]
    after = [jnp.where(even, w, v) for v, w in zip(outer, inner)]
    own = [own_ref[j].astype(F32) for j in range(band_rows + 1)]
    for j in range(ROW_HALO + 1):
        before_ref[j] = before[j].astype(BF16)
        after_ref[j] = after[j].astype(BF16)
    tall = before[:ROW_HALO] + own[:band_rows] + after[:ROW_HALO]
    for j in range(0, len(tall), 2):
        to_last = jnp.concatenate([v[:COL_HALO] for v in tall[j : j + 2]], axis=0)
        to_next = jnp.concatenate([v[band_cols - COL_HALO :] for v in tall[j : j + 2]], axis=0)
        far_ref[j // 2] = jnp.where(first, to_last, to_next).astype(BF16)
        near_ref[j // 2] = jnp.where(first, to_next, to_last).astype(BF16)
    far_ref[len(tall) // 2] = own[band_rows].astype(BF16)
    near_ref[len(tall) // 2] = own[band_rows].astype(BF16)


def features_kernel(given_ref, hid_ref, own_ref, lifted_ref, side_lifted_ref, *refs, first):
    if first:
        weight_ref = given_ref
        _, w1_ref, feat_ref, first_ref = refs
        for tap in range(9):
            first_ref[tap * LANES : (tap + 1) * LANES] = w1_ref[tap].astype(F32).T.astype(BF16)
    else:
        feat_ref, weight_ref = refs
        weight_ref[...] = jnp.zeros_like(weight_ref)
        for a in range(3):
            for b in range(3):
                for q in range(2):
                    at = (b * 4 + a + q) * LANES
                    weight_ref[at : at + LANES, q * LANES : (q + 1) * LANES] = given_ref[a * 3 + b]
    rows, cols, _ = feat_ref.shape
    cells = own_ref.shape[1] // 6
    step = 4
    for n in range(0, rows // 2, step):
        top = first + n
        blocks = []
        for b in range(3):
            for i in range(4):
                start = (top + i // 2) * cols
                blocks.append(hid_ref[b, i % 2, start : start + step * cols])
        out = jnp.dot(jnp.concatenate(blocks, axis=1), weight_ref[...], preferred_element_type=F32)
        right = []
        for r in range(2 * top, 2 * (top + step)):
            part = slice((r + 2) * cells, (r + 3) * cells)
            right.append(stacked(jnp.concatenate([lifted_ref[part], side_lifted_ref[part]], axis=0)))
        lift = jnp.dot(own_ref[...], jnp.concatenate(right, axis=1), preferred_element_type=F32)
        for m in range(step):
            for q in range(2):
                piece = out[m * cols : (m + 1) * cols, q * LANES : (q + 1) * LANES]
                own = lift[:, (2 * m + q) * LANES : (2 * m + q + 1) * LANES]
                feat_ref[2 * (n + m) + q] = (own + piece).astype(BF16)


def reduce_kernel(in_ref, out_ref):
    total = in_ref[0].astype(F32)
    for d in range(1, in_ref.shape[0]):
        total = total + in_ref[d].astype(F32)
    total = total.astype(BF16)
    for d in range(out_ref.shape[0]):
        out_ref[d] = total


def padded_embed(embed_ref, space_ref):
    fields = embed_ref.shape[0]
    space_ref[0, :LANES] = jnp.zeros((LANES, LANES), F32)
    space_ref[0, :fields] = embed_ref[...].astype(F32)
    return space_ref[0, :LANES].astype(BF16)


def last_kernel(
    mine_ref, other_ref, embed_ref, first_ref, upper_ref, lower_ref, feat_hbm, ge_hbm, g1_hbm, g2_hbm,
    sum_ref, ge_ref, g1_ref, g2_ref, sems, *, scale
):
    core = lax.axis_index("core")
    half_rows = mine_ref.shape[0]
    copies = []

    def leave(source, target):
        copies.append(pltpu.make_async_copy(source, target, sems.at[len(copies)]))
        copies[-1].start()

    count = upper_ref.shape[0]
    leave(upper_ref, feat_hbm.at[pl.ds(0, count)])
    leave(lower_ref, feat_hbm.at[pl.ds(count, count)])
    sum_ref[core] = mine_ref[...]
    sum_ref[1 - core] = other_ref[...]

    def read(at, count):
        return sum_ref[at // half_rows, at % half_rows : at % half_rows + count]

    for a in range(3):
        for tap in range(3 * a, 3 * a + 3):
            g2_ref[tap] = read(tap * LANES, LANES).astype(F32) * scale
        leave(g2_ref.at[pl.ds(3 * a, 3)], g2_hbm.at[pl.ds(3 * a, 3)])
    embed_t = embed_ref[...].astype(F32).T.astype(BF16)[:, :GRAD_ROWS]
    base = 9 * LANES
    g = jnp.concatenate([read(base + tap * GRAD_ROWS, GRAD_ROWS) for tap in range(9)], axis=1)
    for a in range(3):
        part = g[:, 3 * a * LANES : (3 * a + 3) * LANES]
        out = jnp.dot(embed_t, part, preferred_element_type=F32) * scale
        for b in range(3):
            g1_ref[3 * a + b] = out[:, b * LANES : (b + 1) * LANES]
        leave(g1_ref.at[pl.ds(3 * a, 3)], g1_hbm.at[pl.ds(3 * a, 3)])
    lift = read(base + 9 * GRAD_ROWS, GRAD_ROWS).astype(F32)
    lift = lift + jnp.dot(g, first_ref[...], preferred_element_type=F32)
    ge_ref[...] = lift[: ge_ref.shape[0]] * scale
    leave(ge_ref, ge_hbm)
    for copy in copies:
        copy.wait()


def from_hbm(value):
    return pltpu.with_memory_space_constraint(value, pltpu.HBM)


def on_device(
    coarse,
    row_src,
    row_frac,
    col_src,
    col_frac,
    embed_weight,
    conv1_weight,
    conv2_weight,
    cotangent,
):
    lat_count = lax.axis_size("lat")
    ring_count = lax.axis_size("ring")
    core_count = lax.axis_size("core")
    lon_count = ring_count * core_count
    fields, band_rows, band_cols = coarse.shape
    rows, cols, hidden = cotangent.shape
    group = lat_count * ring_count
    wide = cols + 16
    pairs = rows // 2 + 1
    early_pairs = pairs // 4
    depth = band_rows + 2 * ROW_HALO
    params = pltpu.CompilerParams(vmem_limit_bytes=VMEM_BYTES)
    vmem = pl.BlockSpec(memory_space=pltpu.VMEM)
    far = pl.BlockSpec(memory_space=pltpu.HBM)

    w1 = conv1_weight.reshape(9, hidden, hidden)
    w2 = conv2_weight.reshape(9, hidden, hidden)
    row_line = (row_src.reshape(1, rows), row_frac.reshape(1, rows))
    col_line = (col_src.reshape(1, cols), col_frac.reshape(1, cols))

    pack_inputs = (
        jnp.transpose(coarse, (1, 2, 0)),
        *row_line,
        *col_line,
    )
    own, to_outer, to_inner, *lines = pl.pallas_call(
        pack_kernel,
        in_specs=[far] * 5,
        out_shape=[jax.ShapeDtypeStruct((band_rows + 1, band_cols, LANES), BF16)]
        + [jax.ShapeDtypeStruct((ROW_HALO + 1, band_cols, LANES), BF16)] * 2
        + [jax.ShapeDtypeStruct(x.shape, x.dtype) for x in pack_inputs[1:]],
        scratch_shapes=[
            pltpu.VMEM(pack_inputs[0].shape, BF16),
            pltpu.VMEM((band_rows + 1, band_cols, LANES), F32),
            pltpu.SemaphoreType.DMA((5,)),
        ],
        compiler_params=params,
        name="pack",
    )(*(from_hbm(x) for x in pack_inputs))
    row_line, col_line = lines[:2], lines[2:]
    inner = [(i, i ^ 1) for i in range(lat_count)]
    outer = [(i, i + 1) for i in range(1, lat_count - 1, 2)]
    outer = outer + [(j, i) for i, j in outer]
    got_outer = lax.ppermute(to_outer, "lat", outer)
    got_inner = lax.ppermute(to_inner, "lat", inner)

    shift, back_weight, turned, cot, near_w1, near_w2, embed, begun = pl.pallas_call(
        prepare_kernel,
        out_shape=[
            jax.ShapeDtypeStruct((3, 2, (pairs + 1) * wide, hidden), BF16),
            jax.ShapeDtypeStruct((12 * hidden, 2 * hidden), BF16),
            jax.ShapeDtypeStruct((2 * hidden, rows // 2 * cols), BF16),
            jax.ShapeDtypeStruct((rows, cols, hidden), BF16),
            jax.ShapeDtypeStruct((9, hidden, hidden), BF16),
            jax.ShapeDtypeStruct((9, hidden, hidden), BF16),
            jax.ShapeDtypeStruct((LANES, hidden), BF16),
            jax.ShapeDtypeStruct((2 * early_pairs, wide, hidden), F32),
        ],
        in_specs=[far] * 4,
        scratch_shapes=[
            pltpu.VMEM((fields, hidden), BF16),
            pltpu.VMEM((4, wide + 16, hidden), F32),
            pltpu.SemaphoreType.DMA((11,)),
        ],
        compiler_params=params,
        name="prepare",
    )(from_hbm(cotangent), from_hbm(w2), from_hbm(w1), from_hbm(embed_weight))
    before, after, far_message, near_message = pl.pallas_call(
        join_kernel,
        out_shape=[jax.ShapeDtypeStruct((ROW_HALO + 1, band_cols, LANES), BF16)] * 2
        + [jax.ShapeDtypeStruct((depth // 2 + 1, band_cols, LANES), BF16)] * 2,
        compiler_params=params,
        name="join",
    )(own, got_outer, got_inner, embed)
    lon = ("ring", "core")
    inner = [(i, i ^ 1) for i in range(lon_count)]
    outer = [(i, (i + (1 if i % 2 else -1)) % lon_count) for i in range(lon_count)]
    got_far = lax.ppermute(far_message, lon, outer)
    got_near = lax.ppermute(near_message, lon, inner)

    def back_body(*refs):
        back_kernel(*refs, lat_count=lat_count, coarse_cols=band_cols * lon_count)

    reach = rows + 4
    width = -(-reach * band_cols // LANES) * LANES
    bh, mixed, lifted, tap, cot_col, blend = pl.pallas_call(
        back_body,
        out_shape=[
            jax.ShapeDtypeStruct((2 * (pairs - early_pairs), wide, hidden), F32),
            jax.ShapeDtypeStruct((2, 3 * GRAD_ROWS, width), BF16),
            jax.ShapeDtypeStruct((reach * band_cols, hidden), F32),
            jax.ShapeDtypeStruct(((reach - 2) * band_cols, 3 * hidden), F32),
            jax.ShapeDtypeStruct((rows, SPAN, hidden), F32),
            jax.ShapeDtypeStruct((reach * band_cols, 2 * LANES), BF16),
        ],
        compiler_params=params,
        name="back_hidden",
    )(
        *row_line, shift, back_weight, before, own, after, *col_line,
        embed, near_w1, cot,
    )

    blocks = 9 * LANES + 10 * GRAD_ROWS
    chunk = -(-blocks // (core_count * group * 16)) * 16
    half_rows = max(group * chunk, -(-blocks // (2 * LANES)) * LANES)

    def body(*refs):
        main_kernel(
            *refs,
            lat_count=lat_count,
            coarse_cols=band_cols * lon_count,
            band_cols=band_cols,
        )

    hid, own_blend, side_lifted, message = pl.pallas_call(
        body,
        out_specs=[vmem] * 4,
        out_shape=[
            jax.ShapeDtypeStruct((3, 2, pairs * cols, hidden), BF16),
            jax.ShapeDtypeStruct((cols, 3 * SPAN), BF16),
            jax.ShapeDtypeStruct((reach * band_cols, hidden), F32),
            jax.ShapeDtypeStruct((2, half_rows, LANES), BF16),
        ],
        scratch_shapes=[
            pltpu.VMEM(((reach - 2) * band_cols, 3 * hidden), F32),
            pltpu.VMEM((2 * pairs, wide, hidden), F32),
            pltpu.VMEM((9 * SPAN, 2 * pairs * hidden), BF16),
            pltpu.VMEM((wide, 2 * pairs * hidden), BF16),
            pltpu.VMEM((2, 2 * width, 4 * hidden), BF16),
        ],
        compiler_params=params,
        name="tile",
    )(
        got_far, got_near, *col_line,
        embed, near_w1, turned, begun, bh, mixed, tap, cot_col, blend,
    )

    def half_features(first, *arrays):
        def body(*refs):
            features_kernel(*refs, first=first)

        return pl.pallas_call(
            body,
            out_shape=[
                jax.ShapeDtypeStruct((rows // 2, cols, hidden), BF16),
                jax.ShapeDtypeStruct((9 * hidden, hidden), BF16)
                if first
                else jax.ShapeDtypeStruct((12 * hidden, 2 * hidden), BF16),
            ],
            compiler_params=params,
            name=f"features_{first}",
        )(*arrays)

    swap = [(0, 1), (1, 0)]
    received = lax.ppermute(message[1], "core", swap)
    middle = rows // 4
    part, fore_weight = half_features(0, near_w2, hid, own_blend, lifted, side_lifted)
    received, part = lax.optimization_barrier((received, part))
    pair = (message[0].astype(F32) + received.astype(F32)).astype(BF16)
    axes = ("lat", "ring")
    chunk = half_rows // group
    parts = lax.all_to_all(pair, axes, 0, 0, tiled=True)
    copies = pl.pallas_call(
        reduce_kernel,
        out_shape=jax.ShapeDtypeStruct((group, chunk, LANES), BF16),
        compiler_params=params,
        name="sum_chunks",
    )(parts.reshape(group, chunk, LANES))
    mine = lax.all_to_all(copies.reshape(half_rows, LANES), axes, 0, 0, tiled=True)
    other = lax.ppermute(mine, "core", swap)
    last_part, first_weight = half_features(
        middle, fore_weight, hid, own_blend, lifted, side_lifted, mine, near_w1
    )
    scale = 1.0 / math.sqrt(rows * lat_count * cols * lon_count)

    def finish(*refs):
        last_kernel(*refs, scale=scale)

    features, grad_embed, grad_first, grad_second = pl.pallas_call(
        finish,
        out_specs=[far] * 4,
        out_shape=[
            jax.ShapeDtypeStruct((rows, cols, hidden), BF16),
            jax.ShapeDtypeStruct((fields, hidden), F32),
            jax.ShapeDtypeStruct((9, hidden, hidden), F32),
            jax.ShapeDtypeStruct((9, hidden, hidden), F32),
        ],
        scratch_shapes=[
            pltpu.VMEM((2, half_rows, LANES), BF16),
            pltpu.VMEM((fields, hidden), F32),
            pltpu.VMEM((9, hidden, hidden), F32),
            pltpu.VMEM((9, hidden, hidden), F32),
            pltpu.SemaphoreType.DMA((9,)),
        ],
        compiler_params=params,
        name="finish",
    )(mine, other, embed, first_weight, part, last_part)
    shape = (3, 3, hidden, hidden)
    return (features, grad_embed, grad_first.reshape(shape), grad_second.reshape(shape))


def solution(mesh):
    lat_count, lon_count = mesh.devices.shape
    inner = jax.sharding.Mesh(
        mesh.devices.reshape(lat_count, lon_count // 2, 2), ("lat", "ring", "core")
    )
    lon = ("ring", "core")
    in_specs = (
        P(None, "lat", lon),
        P("lat"),
        P("lat"),
        P(lon),
        P(lon),
        P(),
        P(),
        P(),
        P("lat", lon, None),
    )
    out_specs = (P("lat", lon, None), P(), P(), P())
    return jax.shard_map(
        on_device, mesh=inner, in_specs=in_specs, out_specs=out_specs, check_vma=False
    )
```

```python
import math

import jax
import jax.numpy as jnp
from jax import lax
from jax.experimental import pallas as pl
from jax.experimental.pallas import tpu as pltpu
from jax.sharding import PartitionSpec as P

F32 = jnp.float32
BF16 = jnp.bfloat16
LANES = 128
ROW_HALO = 3
COL_HALO = 4
SPAN = 16
GRAD_ROWS = 80
VMEM_BYTES = 24 * 1024 * 1024


def split_two(value):
    high = value.astype(BF16)
    return high, (value - high.astype(F32)).astype(BF16)


def back_rows(shift_ref, weight_ref, out_ref, start_pair):
    wide = out_ref.shape[1]
    pairs = out_ref.shape[0] // 2
    step = 7
    for first in range(0, pairs, step):
        count = min(step, pairs - first)
        blocks = []
        for b in range(3):
            for i in range(4):
                start = (start_pair + first + i // 2) * wide
                blocks.append(shift_ref[b, i % 2, start : start + count * wide])
        out = jnp.dot(jnp.concatenate(blocks, axis=1), weight_ref[...], preferred_element_type=F32)
        for m in range(count):
            for q in range(2):
                out_ref[2 * (first + m) + q] = out[m * wide : (m + 1) * wide, q * LANES : (q + 1) * LANES]


def prepare_kernel(
    cot_hbm, w2_hbm, w1_hbm, embed_hbm,
    shift_ref, back_ref, turned_ref, cot_ref, w1_ref, w2_ref, padded_ref, begun_ref,
    embed_ref, line_ref, sems
):
    rows, cols, _ = cot_ref.shape
    wide = cols + 16
    pairs = rows // 2 + 1
    chunks = sems.shape[0] - 3
    share = rows // chunks
    weight_copy = pltpu.make_async_copy(w2_hbm, w2_ref, sems.at[chunks])
    weight_copy.start()
    copies = []
    for n in range(chunks):
        part = pl.ds(n * share, share)
        copies.append(pltpu.make_async_copy(cot_hbm.at[part], cot_ref.at[part], sems.at[n]))
        copies[-1].start()
    other_copy = pltpu.make_async_copy(w1_hbm, w1_ref, sems.at[chunks + 1])
    other_copy.start()
    embed_copy = pltpu.make_async_copy(embed_hbm, embed_ref, sems.at[chunks + 2])
    embed_copy.start()
    line_ref[...] = jnp.zeros_like(line_ref)
    back_ref[...] = jnp.zeros_like(back_ref)
    blank = jnp.zeros((wide, LANES), BF16)
    for b in range(3):
        for parity in range(2):
            shift_ref[b, parity, 0:wide] = blank
            shift_ref[b, parity, pairs * wide : (pairs + 1) * wide] = blank
    weight_copy.wait()
    for a in range(3):
        for b in range(3):
            turned = w2_ref[a * 3 + b].astype(F32).T.astype(BF16)
            for q in range(2):
                at = (b * 4 + 2 + q - a) * LANES
                back_ref[at : at + LANES, q * LANES : (q + 1) * LANES] = turned
    for r in range(rows):
        slot = r % 4
        if r % share == 0:
            copies[r // share].wait()
        line = cot_ref[r].astype(F32)
        line_ref[slot, 8 : 8 + cols] = line
        start = (r // 2 + 1) * wide
        for b in range(3):
            shift_ref[b, r % 2, start : start + wide] = line_ref[slot, 8 - b : 8 - b + wide].astype(BF16)
        turned_ref[(r % 2) * LANES : (r % 2 + 1) * LANES, (r // 2) * cols : (r // 2 + 1) * cols] = line.T.astype(BF16)
    embed_copy.wait()
    padded_ref[...] = padded_embed(embed_ref, line_ref)
    other_copy.wait()
    back_rows(shift_ref, back_ref, begun_ref, 0)


def edge_line(block, at):
    index = block[at : at + 1]
    return index, block[at + 1 : at + 2] + block[at + 2 : at + 3] + block[at + 3 : at + 4]


def joined_line(first, own, last, width):
    lane_count = 2 * LANES
    lane = lax.broadcasted_iota(jnp.int32, (1, lane_count), 1)
    out = []
    for part, shift in zip((first, own, last), (lane_count - width + 2, 2, width + 2)):
        part = jnp.concatenate([part[:, :width], jnp.zeros((1, lane_count - width), F32)], axis=1)
        out.append(pltpu.roll(jnp.broadcast_to(part, (8, lane_count)), shift, 1)[:1])
    return jnp.where(lane < 2, out[0], jnp.where(lane < width + 2, out[1], out[2]))


def row_blend(rsrc_ref, rfrac_ref, before_ref, after_ref, lat, lat_count, band_rows):
    rows = rsrc_ref.shape[1]
    cells = 2 * COL_HALO
    before_line = edge_line(before_ref[ROW_HALO].astype(F32), 0)
    after_line = edge_line(after_ref[ROW_HALO].astype(F32), 0)
    own_line = (rsrc_ref[...].astype(F32), rfrac_ref[...])
    src, frac = (
        joined_line(*lines, rows) for lines in zip(before_line, own_line, after_line)
    )
    spot = (src - (lat * band_rows - ROW_HALO).astype(F32)) * cells
    shape = (cells, LANES)
    at = lax.broadcasted_iota(jnp.int32, shape, 1) - lax.broadcasted_iota(jnp.int32, shape, 0)
    at = at.astype(F32)
    parts = []
    for q in range(rows + 4):
        here = jnp.broadcast_to(spot[:, q : q + 1], shape)
        f = jnp.broadcast_to(frac[:, q : q + 1], shape)
        part = jnp.where(at == here, 1.0 - f, 0.0) + jnp.where(at == here + cells, f, 0.0)
        if q < 2:
            part = part * jnp.where(lat > 0, 1.0, 0.0)
        elif q >= rows + 2:
            part = part * jnp.where(lat < lat_count - 1, 1.0, 0.0)
        parts.append(part)
    return jnp.concatenate(list(split_two(jnp.concatenate(parts, axis=0))), axis=1)


def blend_rows(matrix, cells):
    fill = jnp.zeros((LANES - sum(c.shape[0] for c in cells), LANES), F32)
    column = jnp.concatenate(list(cells) + [fill], axis=0).astype(BF16)
    return jnp.dot(matrix, jnp.concatenate([column, column], axis=0), preferred_element_type=F32)


def stacked(value):
    one, two = split_two(value)
    return jnp.concatenate([one, one, two], axis=0)


def lift_rows(mixed, embed):
    pair = jnp.concatenate(list(split_two(mixed)), axis=1)
    return jnp.dot(pair, jnp.concatenate([embed, embed], axis=0), preferred_element_type=F32)


def turned_rows(mixed, width):
    fill = jnp.zeros((width - mixed.shape[0], LANES), F32)
    turned = jnp.concatenate([mixed, fill], axis=0).T[:GRAD_ROWS]
    step = 2 * COL_HALO
    lines = [turned] + [pltpu.roll(turned, width - a * step, 1) for a in (1, 2)]
    return split_two(jnp.concatenate(lines, axis=0))


def tap_rows(lifted, w1_ref, cells):
    count = lifted.shape[0] - 2 * cells
    pairs = [split_two(lifted[a * cells : a * cells + count]) for a in range(3)]
    left = jnp.concatenate([p[0] for p in pairs] + [p[1] for p in pairs], axis=1)
    lines = [jnp.concatenate([w1_ref[a * 3 + b] for b in range(3)], axis=1) for a in range(3)]
    return jnp.dot(left, jnp.concatenate(lines + lines, axis=0), preferred_element_type=F32)


def blend_cols(src, frac, lon, band_cols, coarse_cols):
    shape = (SPAN, src.shape[1])
    local = jnp.broadcast_to(src, shape) - lon * band_cols
    frac = jnp.broadcast_to(frac, shape)
    local = jnp.where(local < -COL_HALO, local + coarse_cols, local)
    local = jnp.where(local >= band_cols + COL_HALO, local - coarse_cols, local)
    line = lax.broadcasted_iota(jnp.int32, shape, 0)

    def spot(at):
        east = jnp.where(at >= band_cols, at + COL_HALO, at)
        return jnp.where(at < 0, at + band_cols + COL_HALO, east)

    return jnp.where(line == spot(local), 1.0 - frac, 0.0) + jnp.where(
        line == spot(local + 1), frac, 0.0
    )


def back_kernel(
    rsrc_ref,
    rfrac_ref,
    shift_ref,
    weight_ref,
    before_ref,
    own_ref,
    after_ref,
    csrc_ref,
    cfrac_ref,
    embed_ref,
    w1_ref,
    cot_ref,
    bh_ref,
    rows_ref,
    lifted_ref,
    tap_ref,
    cot_col_ref,
    blend_ref,
    *,
    lat_count,
    coarse_cols,
):
    rows, cols, _ = cot_ref.shape
    band_rows, band_cols = own_ref.shape[0] - 1, own_ref.shape[1]
    back_rows(shift_ref, weight_ref, bh_ref, rows // 2 + 1 - bh_ref.shape[0] // 2)

    lat = lax.axis_index("lat")
    lon = lax.axis_index("ring") * 2 + lax.axis_index("core")
    matrix = row_blend(rsrc_ref, rfrac_ref, before_ref, after_ref, lat, lat_count, band_rows)
    blend_ref[...] = matrix
    cells = [before_ref[j] for j in range(ROW_HALO)] + [own_ref[j] for j in range(band_rows)]
    cells += [after_ref[j] for j in range(ROW_HALO)]
    mixed = blend_rows(matrix, [c.astype(F32) for c in cells])
    rows_ref[0], rows_ref[1] = turned_rows(mixed, rows_ref.shape[2])
    lifted = lift_rows(mixed, embed_ref[...])
    lifted_ref[...] = lifted
    tap_ref[...] = tap_rows(lifted, w1_ref, band_cols)

    blend = blend_cols(csrc_ref[...], cfrac_ref[...], lon, band_cols, coarse_cols)
    own_t = jnp.concatenate(list(split_two(blend)), axis=0)
    every = jnp.concatenate([cot_ref[r] for r in range(rows)], axis=1)
    back = jnp.dot(own_t, every, preferred_element_type=F32)
    back = back[:SPAN] + back[SPAN:]
    for r in range(rows):
        cot_col_ref[r] = back[:, r * LANES : (r + 1) * LANES]


def pack_kernel(cells_hbm, rsrc_hbm, rfrac_hbm, csrc_hbm, cfrac_hbm, *space):
    sources = (cells_hbm, rsrc_hbm, rfrac_hbm, csrc_hbm, cfrac_hbm)
    own_ref, outer_ref, inner_ref, *lines, cells_ref, out_ref, sems = space
    targets = (cells_ref, *lines)
    copies = [
        pltpu.make_async_copy(source, target, sems.at[n])
        for n, (source, target) in enumerate(zip(sources, targets))
    ]
    for copy in copies:
        copy.start()
    cells_ref, rsrc_ref, rfrac_ref, csrc_ref, cfrac_ref = targets
    depth, span, fields = cells_ref.shape
    out_ref[...] = jnp.zeros_like(out_ref)
    for copy in copies:
        copy.wait()
    for j in range(depth):
        out_ref[j, :, :fields] = cells_ref[j].astype(F32)
    at = 0
    for index_ref, fraction_ref in ((rsrc_ref, rfrac_ref), (csrc_ref, cfrac_ref)):
        width = index_ref.shape[1]
        fraction = fraction_ref[...]
        one = fraction.astype(BF16).astype(F32)
        two = (fraction - one).astype(BF16).astype(F32)
        for value in (index_ref[...].astype(F32), one, two, fraction - one - two):
            out_ref[depth, at : at + 1, :width] = value
            at += 1
    lat = lax.axis_index("lat")
    even = lax.rem(lat, 2) == 0
    own = [out_ref[j] for j in range(depth + 1)]
    to_next = own[depth - ROW_HALO :]
    to_last = own[:ROW_HALO] + own[depth:]
    for j in range(depth + 1):
        own_ref[j] = own[j].astype(BF16)
    for j in range(ROW_HALO + 1):
        outer_ref[j] = jnp.where(even, to_last[j], to_next[j]).astype(BF16)
        inner_ref[j] = jnp.where(even, to_next[j], to_last[j]).astype(BF16)


def main_kernel(
    far_ref,
    near_ref,
    csrc_ref,
    cfrac_ref,
    embed_ref,
    w1_ref,
    turned_ref,
    begun_ref,
    bh_ref,
    rows_ref,
    tap_ref,
    cot_col_ref,
    blend_ref,
    hid_ref,
    own_ref,
    side_lifted_ref,
    msg_ref,
    side_tap_ref,
    line_ref,
    right_ref,
    delta_ref,
    back_ref,
    *,
    lat_count,
    coarse_cols,
    band_cols,
):
    rows, cols = cot_col_ref.shape[0], own_ref.shape[0]
    wide = bh_ref.shape[1]
    begun = begun_ref.shape[0]
    pairs = (begun + bh_ref.shape[0]) // 2
    depth = 2 * (far_ref.shape[0] - 1)
    half_rows = msg_ref.shape[1]
    lat = lax.axis_index("lat")
    core = lax.axis_index("core")
    lon = lax.axis_index("ring") * 2 + core
    taps = 3 * SPAN

    def send(at, value):
        side = lax.rem(at // half_rows + core, 2)
        at = at % half_rows
        msg_ref[side, at : at + value.shape[0]] = value.astype(BF16)

    sides = []
    for j in range(depth // 2 + 1):
        far, near = far_ref[j].astype(F32), near_ref[j].astype(F32)
        sides.append((jnp.where(core == 1, near, far), jnp.where(core == 1, far, near)))
    cells = []
    for j in range(depth):
        part = slice(j % 2 * COL_HALO, (j % 2 + 1) * COL_HALO)
        cells += [v[part] for v in sides[j // 2]]
    side_mixed = blend_rows(blend_ref[...], cells)
    side_lifted = lift_rows(side_mixed, embed_ref[...])
    side_lifted_ref[...] = side_lifted
    side_tap_ref[...] = tap_rows(side_lifted, w1_ref, band_cols)

    lane_count = 2 * LANES
    lane = lax.broadcasted_iota(jnp.int32, (1, lane_count), 1)
    west_line, east_line = (edge_line(v, 4) for v in sides[depth // 2])
    own_line = (csrc_ref[...].astype(F32), cfrac_ref[...])
    lines = [joined_line(*v, cols) for v in zip(west_line, own_line, east_line)]
    known = lane < cols + 4
    src = jnp.where(known, lines[0], -1e6).astype(jnp.int32)
    blend = blend_cols(src, jnp.where(known, lines[1], 0.0), lon, band_cols, coarse_cols)
    rolled = [blend] + [pltpu.roll(blend, lane_count - b, 1) for b in (1, 2)]
    stack = jnp.concatenate(rolled, axis=0)[:, :wide]
    high, low = split_two(stack)
    high_f, low_f = high.astype(F32), low.astype(F32)
    col_t = jnp.concatenate([high_f, low_f], axis=0).astype(BF16)
    col_lhs = jnp.concatenate([high_f.T, low_f.T, high_f.T], axis=1).astype(BF16)
    own_hi, own_lo = split_two(rolled[2][:, :cols])
    own_hi, own_lo = own_hi.astype(F32).T, own_lo.astype(F32).T
    own_ref[...] = jnp.concatenate([own_hi, own_lo, own_hi], axis=1).astype(BF16)

    for t in range(2 * pairs):
        part = slice(t * band_cols, (t + 1) * band_cols)
        blocks = []
        for b in range(3):
            column = slice(b * LANES, (b + 1) * LANES)
            blocks += [tap_ref[part, column], side_tap_ref[part, column]]
        right_ref[:, t * LANES : (t + 1) * LANES] = stacked(jnp.concatenate(blocks, axis=0))
    half = rows // 2 + 2
    spans = ((0, half), (half, 2 * pairs))

    def first_product(n):
        span = slice(spans[n][0] * LANES, spans[n][1] * LANES)
        return jnp.dot(col_lhs, right_ref[:, span], preferred_element_type=F32)

    def activate(pre, first, t):
        v = pre[:, (t - first) * LANES : (t - first + 1) * LANES]
        s = 0.5 + 0.5 * jnp.tanh(0.5 * v)
        if t == 0:
            s = s * jnp.where(lat > 0, 1.0, 0.0)
        elif t == 2 * pairs - 1:
            s = s * jnp.where(lat < lat_count - 1, 1.0, 0.0)
        h = v * s
        slope = s + h * (1.0 - s)
        line_ref[t] = h
        arrived = begun_ref[t] if t < begun else bh_ref[t - begun]
        delta_ref[:, t * LANES : (t + 1) * LANES] = (arrived * slope).astype(BF16)

    def place_hidden(t):
        at = (t // 2) * cols
        for b in range(3):
            hid_ref[b, t % 2, at : at + cols] = line_ref[t, b : b + cols].astype(BF16)

    def second_gradient(b):
        right = []
        for i in range(4):
            start = (i // 2) * cols
            right.append(hid_ref[b, i % 2, start : start + rows // 2 * cols])
        return jnp.dot(turned_ref[...], jnp.concatenate(right, axis=1), preferred_element_type=F32)

    pre = first_product(0)
    for t in range(*spans[0]):
        activate(pre, 0, t)
    pre = first_product(1)
    for t in range(*spans[0]):
        place_hidden(t)
    for t in range(*spans[1]):
        activate(pre, spans[1][0], t)
        place_hidden(t)
    back = jnp.dot(col_t, delta_ref[...], preferred_element_type=F32)
    back = back[:taps] + back[taps:]
    grads = []

    width = rows_ref.shape[2]
    used = 2 * pairs * band_cols
    blank = jnp.zeros((2, width - used, back_ref.shape[2]), BF16)
    back_ref[:, used:width] = blank
    back_ref[:, width + used :] = blank
    nothing = jnp.zeros((SPAN, LANES), F32)

    def place_back(p):
        for b in range(4):
            lines = []
            for t in (2 * p, 2 * p + 1):
                if b < 3:
                    lines.append(back[b * SPAN : (b + 1) * SPAN, t * LANES : (t + 1) * LANES])
                else:
                    lines.append(cot_col_ref[t - 1] if 1 <= t <= rows else nothing)
            column = slice(b * LANES, (b + 1) * LANES)
            for side in range(2):
                cells = slice(side * band_cols, (side + 1) * band_cols)
                one, two = split_two(jnp.concatenate([v[cells] for v in lines], axis=0))
                at = side * width + p * SPAN
                back_ref[0, at : at + SPAN, column] = one
                back_ref[1, at : at + SPAN, column] = two

    def send_second(b):
        for a in range(3):
            upper = grads[b][:LANES, a * LANES : (a + 1) * LANES]
            lower = grads[b][LANES:, (a + 1) * LANES : (a + 2) * LANES]
            send((a * 3 + b) * LANES, (upper + lower).T)

    share = -(-pairs // 3)
    side_hi, side_lo = turned_rows(side_mixed, width)
    for b in range(3):
        grads.append(second_gradient(b))
        for p in range(b * share, min((b + 1) * share, pairs)):
            place_back(p)
    upper = jnp.concatenate([rows_ref[0], side_hi], axis=1)
    lower = jnp.concatenate([rows_ref[1], side_lo], axis=1)
    g = jnp.dot(jnp.concatenate([upper, lower], axis=0), back_ref[0], preferred_element_type=F32)
    send_second(0)
    send_second(1)
    g = g[: 3 * GRAD_ROWS] + g[3 * GRAD_ROWS :]
    g = g + jnp.dot(upper, back_ref[1], preferred_element_type=F32)
    send_second(2)
    for a in range(3):
        line = g[a * GRAD_ROWS : (a + 1) * GRAD_ROWS]
        for b in range(3):
            send(9 * LANES + (a * 3 + b) * GRAD_ROWS, line[:, b * LANES : (b + 1) * LANES])
    send(9 * LANES + 9 * GRAD_ROWS, g[GRAD_ROWS : 2 * GRAD_ROWS, 3 * LANES:])
    tail = 9 * LANES + 10 * GRAD_ROWS
    if 2 * half_rows > tail:
        send(tail, jnp.zeros((2 * half_rows - tail, LANES), F32))


def join_kernel(own_ref, outer_ref, inner_ref, ready_ref, before_ref, after_ref, far_ref, near_ref):
    band_rows, band_cols = own_ref.shape[0] - 1, own_ref.shape[1]
    lat = lax.axis_index("lat")
    even = lax.rem(lat, 2) == 0
    first = lax.axis_index("core") == 0
    outer = [outer_ref[j].astype(F32) for j in range(ROW_HALO + 1)]
    inner = [inner_ref[j].astype(F32) for j in range(ROW_HALO + 1)]
    before = [jnp.where(even, v, w) for v, w in zip(outer, inner)]
    after = [jnp.where(even, w, v) for v, w in zip(outer, inner)]
    own = [own_ref[j].astype(F32) for j in range(band_rows + 1)]
    for j in range(ROW_HALO + 1):
        before_ref[j] = before[j].astype(BF16)
        after_ref[j] = after[j].astype(BF16)
    tall = before[:ROW_HALO] + own[:band_rows] + after[:ROW_HALO]
    for j in range(0, len(tall), 2):
        to_last = jnp.concatenate([v[:COL_HALO] for v in tall[j : j + 2]], axis=0)
        to_next = jnp.concatenate([v[band_cols - COL_HALO :] for v in tall[j : j + 2]], axis=0)
        far_ref[j // 2] = jnp.where(first, to_last, to_next).astype(BF16)
        near_ref[j // 2] = jnp.where(first, to_next, to_last).astype(BF16)
    far_ref[len(tall) // 2] = own[band_rows].astype(BF16)
    near_ref[len(tall) // 2] = own[band_rows].astype(BF16)


def features_kernel(given_ref, hid_ref, own_ref, lifted_ref, side_lifted_ref, *refs, first):
    if first:
        weight_ref = given_ref
        _, w1_ref, feat_ref, first_ref = refs
        for tap in range(9):
            first_ref[tap * LANES : (tap + 1) * LANES] = w1_ref[tap].astype(F32).T.astype(BF16)
    else:
        feat_ref, weight_ref = refs
        weight_ref[...] = jnp.zeros_like(weight_ref)
        for a in range(3):
            for b in range(3):
                for q in range(2):
                    at = (b * 4 + a + q) * LANES
                    weight_ref[at : at + LANES, q * LANES : (q + 1) * LANES] = given_ref[a * 3 + b]
    rows, cols, _ = feat_ref.shape
    cells = own_ref.shape[1] // 6
    step = 4
    for n in range(0, rows // 2, step):
        top = first + n
        blocks = []
        for b in range(3):
            for i in range(4):
                start = (top + i // 2) * cols
                blocks.append(hid_ref[b, i % 2, start : start + step * cols])
        out = jnp.dot(jnp.concatenate(blocks, axis=1), weight_ref[...], preferred_element_type=F32)
        right = []
        for r in range(2 * top, 2 * (top + step)):
            part = slice((r + 2) * cells, (r + 3) * cells)
            right.append(stacked(jnp.concatenate([lifted_ref[part], side_lifted_ref[part]], axis=0)))
        lift = jnp.dot(own_ref[...], jnp.concatenate(right, axis=1), preferred_element_type=F32)
        for m in range(step):
            for q in range(2):
                piece = out[m * cols : (m + 1) * cols, q * LANES : (q + 1) * LANES]
                own = lift[:, (2 * m + q) * LANES : (2 * m + q + 1) * LANES]
                feat_ref[2 * (n + m) + q] = (own + piece).astype(BF16)


def reduce_kernel(in_ref, out_ref):
    total = in_ref[0].astype(F32)
    for d in range(1, in_ref.shape[0]):
        total = total + in_ref[d].astype(F32)
    total = total.astype(BF16)
    for d in range(out_ref.shape[0]):
        out_ref[d] = total


def padded_embed(embed_ref, space_ref):
    fields = embed_ref.shape[0]
    space_ref[0, :LANES] = jnp.zeros((LANES, LANES), F32)
    space_ref[0, :fields] = embed_ref[...].astype(F32)
    return space_ref[0, :LANES].astype(BF16)


def last_kernel(
    mine_ref, other_ref, embed_ref, first_ref, upper_ref, lower_ref, feat_hbm, ge_hbm, g1_hbm, g2_hbm,
    sum_ref, ge_ref, g1_ref, g2_ref, sems, *, scale
):
    core = lax.axis_index("core")
    half_rows = mine_ref.shape[0]
    copies = []

    def leave(source, target):
        copies.append(pltpu.make_async_copy(source, target, sems.at[len(copies)]))
        copies[-1].start()

    count = upper_ref.shape[0]
    leave(upper_ref, feat_hbm.at[pl.ds(0, count)])
    leave(lower_ref, feat_hbm.at[pl.ds(count, count)])
    sum_ref[core] = mine_ref[...]
    sum_ref[1 - core] = other_ref[...]

    def read(at, count):
        return sum_ref[at // half_rows, at % half_rows : at % half_rows + count]

    for a in range(3):
        for tap in range(3 * a, 3 * a + 3):
            g2_ref[tap] = read(tap * LANES, LANES).astype(F32) * scale
        leave(g2_ref.at[pl.ds(3 * a, 3)], g2_hbm.at[pl.ds(3 * a, 3)])
    embed_t = embed_ref[...].astype(F32).T.astype(BF16)[:, :GRAD_ROWS]
    base = 9 * LANES
    g = jnp.concatenate([read(base + tap * GRAD_ROWS, GRAD_ROWS) for tap in range(9)], axis=1)
    for a in range(3):
        part = g[:, 3 * a * LANES : (3 * a + 3) * LANES]
        out = jnp.dot(embed_t, part, preferred_element_type=F32) * scale
        for b in range(3):
            g1_ref[3 * a + b] = out[:, b * LANES : (b + 1) * LANES]
        leave(g1_ref.at[pl.ds(3 * a, 3)], g1_hbm.at[pl.ds(3 * a, 3)])
    lift = read(base + 9 * GRAD_ROWS, GRAD_ROWS).astype(F32)
    lift = lift + jnp.dot(g, first_ref[...], preferred_element_type=F32)
    ge_ref[...] = lift[: ge_ref.shape[0]] * scale
    leave(ge_ref, ge_hbm)
    for copy in copies:
        copy.wait()


def from_hbm(value):
    return pltpu.with_memory_space_constraint(value, pltpu.HBM)


def on_device(
    coarse,
    row_src,
    row_frac,
    col_src,
    col_frac,
    embed_weight,
    conv1_weight,
    conv2_weight,
    cotangent,
):
    lat_count = lax.axis_size("lat")
    ring_count = lax.axis_size("ring")
    core_count = lax.axis_size("core")
    lon_count = ring_count * core_count
    fields, band_rows, band_cols = coarse.shape
    rows, cols, hidden = cotangent.shape
    group = lat_count * ring_count
    wide = cols + 16
    pairs = rows // 2 + 1
    early_pairs = 1
    depth = band_rows + 2 * ROW_HALO
    params = pltpu.CompilerParams(vmem_limit_bytes=VMEM_BYTES)
    vmem = pl.BlockSpec(memory_space=pltpu.VMEM)
    far = pl.BlockSpec(memory_space=pltpu.HBM)

    w1 = conv1_weight.reshape(9, hidden, hidden)
    w2 = conv2_weight.reshape(9, hidden, hidden)
    row_line = (row_src.reshape(1, rows), row_frac.reshape(1, rows))
    col_line = (col_src.reshape(1, cols), col_frac.reshape(1, cols))

    pack_inputs = (
        jnp.transpose(coarse, (1, 2, 0)),
        *row_line,
        *col_line,
    )
    own, to_outer, to_inner, *lines = pl.pallas_call(
        pack_kernel,
        in_specs=[far] * 5,
        out_shape=[jax.ShapeDtypeStruct((band_rows + 1, band_cols, LANES), BF16)]
        + [jax.ShapeDtypeStruct((ROW_HALO + 1, band_cols, LANES), BF16)] * 2
        + [jax.ShapeDtypeStruct(x.shape, x.dtype) for x in pack_inputs[1:]],
        scratch_shapes=[
            pltpu.VMEM(pack_inputs[0].shape, BF16),
            pltpu.VMEM((band_rows + 1, band_cols, LANES), F32),
            pltpu.SemaphoreType.DMA((5,)),
        ],
        compiler_params=params,
        name="pack",
    )(*(from_hbm(x) for x in pack_inputs))
    row_line, col_line = lines[:2], lines[2:]
    inner = [(i, i ^ 1) for i in range(lat_count)]
    outer = [(i, i + 1) for i in range(1, lat_count - 1, 2)]
    outer = outer + [(j, i) for i, j in outer]
    got_outer = lax.ppermute(to_outer, "lat", outer)
    got_inner = lax.ppermute(to_inner, "lat", inner)

    shift, back_weight, turned, cot, near_w1, near_w2, embed, begun = pl.pallas_call(
        prepare_kernel,
        out_shape=[
            jax.ShapeDtypeStruct((3, 2, (pairs + 1) * wide, hidden), BF16),
            jax.ShapeDtypeStruct((12 * hidden, 2 * hidden), BF16),
            jax.ShapeDtypeStruct((2 * hidden, rows // 2 * cols), BF16),
            jax.ShapeDtypeStruct((rows, cols, hidden), BF16),
            jax.ShapeDtypeStruct((9, hidden, hidden), BF16),
            jax.ShapeDtypeStruct((9, hidden, hidden), BF16),
            jax.ShapeDtypeStruct((LANES, hidden), BF16),
            jax.ShapeDtypeStruct((2 * early_pairs, wide, hidden), F32),
        ],
        in_specs=[far] * 4,
        scratch_shapes=[
            pltpu.VMEM((fields, hidden), BF16),
            pltpu.VMEM((4, wide + 16, hidden), F32),
            pltpu.SemaphoreType.DMA((11,)),
        ],
        compiler_params=params,
        name="prepare",
    )(from_hbm(cotangent), from_hbm(w2), from_hbm(w1), from_hbm(embed_weight))
    before, after, far_message, near_message = pl.pallas_call(
        join_kernel,
        out_shape=[jax.ShapeDtypeStruct((ROW_HALO + 1, band_cols, LANES), BF16)] * 2
        + [jax.ShapeDtypeStruct((depth // 2 + 1, band_cols, LANES), BF16)] * 2,
        compiler_params=params,
        name="join",
    )(own, got_outer, got_inner, embed)
    lon = ("ring", "core")
    inner = [(i, i ^ 1) for i in range(lon_count)]
    outer = [(i, (i + (1 if i % 2 else -1)) % lon_count) for i in range(lon_count)]
    got_far = lax.ppermute(far_message, lon, outer)
    got_near = lax.ppermute(near_message, lon, inner)

    def back_body(*refs):
        back_kernel(*refs, lat_count=lat_count, coarse_cols=band_cols * lon_count)

    reach = rows + 4
    width = -(-reach * band_cols // LANES) * LANES
    bh, mixed, lifted, tap, cot_col, blend = pl.pallas_call(
        back_body,
        out_shape=[
            jax.ShapeDtypeStruct((2 * (pairs - early_pairs), wide, hidden), F32),
            jax.ShapeDtypeStruct((2, 3 * GRAD_ROWS, width), BF16),
            jax.ShapeDtypeStruct((reach * band_cols, hidden), F32),
            jax.ShapeDtypeStruct(((reach - 2) * band_cols, 3 * hidden), F32),
            jax.ShapeDtypeStruct((rows, SPAN, hidden), F32),
            jax.ShapeDtypeStruct((reach * band_cols, 2 * LANES), BF16),
        ],
        compiler_params=params,
        name="back_hidden",
    )(
        *row_line, shift, back_weight, before, own, after, *col_line,
        embed, near_w1, cot,
    )

    blocks = 9 * LANES + 10 * GRAD_ROWS
    chunk = -(-blocks // (core_count * group * 16)) * 16
    half_rows = max(group * chunk, -(-blocks // (2 * LANES)) * LANES)

    def body(*refs):
        main_kernel(
            *refs,
            lat_count=lat_count,
            coarse_cols=band_cols * lon_count,
            band_cols=band_cols,
        )

    hid, own_blend, side_lifted, message = pl.pallas_call(
        body,
        out_specs=[vmem] * 4,
        out_shape=[
            jax.ShapeDtypeStruct((3, 2, pairs * cols, hidden), BF16),
            jax.ShapeDtypeStruct((cols, 3 * SPAN), BF16),
            jax.ShapeDtypeStruct((reach * band_cols, hidden), F32),
            jax.ShapeDtypeStruct((2, half_rows, LANES), BF16),
        ],
        scratch_shapes=[
            pltpu.VMEM(((reach - 2) * band_cols, 3 * hidden), F32),
            pltpu.VMEM((2 * pairs, wide, hidden), F32),
            pltpu.VMEM((9 * SPAN, 2 * pairs * hidden), BF16),
            pltpu.VMEM((wide, 2 * pairs * hidden), BF16),
            pltpu.VMEM((2, 2 * width, 4 * hidden), BF16),
        ],
        compiler_params=params,
        name="tile",
    )(
        got_far, got_near, *col_line,
        embed, near_w1, turned, begun, bh, mixed, tap, cot_col, blend,
    )

    def half_features(first, *arrays):
        def body(*refs):
            features_kernel(*refs, first=first)

        return pl.pallas_call(
            body,
            out_shape=[
                jax.ShapeDtypeStruct((rows // 2, cols, hidden), BF16),
                jax.ShapeDtypeStruct((9 * hidden, hidden), BF16)
                if first
                else jax.ShapeDtypeStruct((12 * hidden, 2 * hidden), BF16),
            ],
            compiler_params=params,
            name=f"features_{first}",
        )(*arrays)

    swap = [(0, 1), (1, 0)]
    received = lax.ppermute(message[1], "core", swap)
    middle = rows // 4
    part, fore_weight = half_features(0, near_w2, hid, own_blend, lifted, side_lifted)
    received, part = lax.optimization_barrier((received, part))
    pair = (message[0].astype(F32) + received.astype(F32)).astype(BF16)
    axes = ("lat", "ring")
    chunk = half_rows // group
    parts = lax.all_to_all(pair, axes, 0, 0, tiled=True)
    copies = pl.pallas_call(
        reduce_kernel,
        out_shape=jax.ShapeDtypeStruct((group, chunk, LANES), BF16),
        compiler_params=params,
        name="sum_chunks",
    )(parts.reshape(group, chunk, LANES))
    mine = lax.all_to_all(copies.reshape(half_rows, LANES), axes, 0, 0, tiled=True)
    other = lax.ppermute(mine, "core", swap)
    last_part, first_weight = half_features(
        middle, fore_weight, hid, own_blend, lifted, side_lifted, mine, near_w1
    )
    scale = 1.0 / math.sqrt(rows * lat_count * cols * lon_count)

    def finish(*refs):
        last_kernel(*refs, scale=scale)

    features, grad_embed, grad_first, grad_second = pl.pallas_call(
        finish,
        out_specs=[far] * 4,
        out_shape=[
            jax.ShapeDtypeStruct((rows, cols, hidden), BF16),
            jax.ShapeDtypeStruct((fields, hidden), F32),
            jax.ShapeDtypeStruct((9, hidden, hidden), F32),
            jax.ShapeDtypeStruct((9, hidden, hidden), F32),
        ],
        scratch_shapes=[
            pltpu.VMEM((2, half_rows, LANES), BF16),
            pltpu.VMEM((fields, hidden), F32),
            pltpu.VMEM((9, hidden, hidden), F32),
            pltpu.VMEM((9, hidden, hidden), F32),
            pltpu.SemaphoreType.DMA((9,)),
        ],
        compiler_params=params,
        name="finish",
    )(mine, other, embed, first_weight, part, last_part)
    shape = (3, 3, hidden, hidden)
    return (features, grad_embed, grad_first.reshape(shape), grad_second.reshape(shape))


def solution(mesh):
    lat_count, lon_count = mesh.devices.shape
    inner = jax.sharding.Mesh(
        mesh.devices.reshape(lat_count, lon_count // 2, 2), ("lat", "ring", "core")
    )
    lon = ("ring", "core")
    in_specs = (
        P(None, "lat", lon),
        P("lat"),
        P("lat"),
        P(lon),
        P(lon),
        P(),
        P(),
        P(),
        P("lat", lon, None),
    )
    out_specs = (P("lat", lon, None), P(), P(), P())
    return jax.shard_map(
        on_device, mesh=inner, in_specs=in_specs, out_specs=out_specs, check_vma=False
    )
```
